32 devices in a mesh: ulysses: 2 (over x), blk: 16 (over z, y, core).
Axes of the slice: x: 2, y: 2, z: 4, core: 2. Of those that a mesh axis runs over, the one named last changes fastest.
Arguments:
- layer_input: bfloat16 [3, 3072, 768], P(None, ('ulysses', 'blk')), may hold values from -6 to 6
- query_key_value_weight: bfloat16 [768, 2304], P(('ulysses', 'blk')), may hold values from -0.21875 to 0.21875
- output_weight: bfloat16 [768, 768], P(('ulysses', 'blk')), may hold values from -1.75 to 1.75
- input_weight: bfloat16 [768, 3072], P(('ulysses', 'blk')), may hold values from -0.21875 to 0.21875
- down_weight: bfloat16 [3072, 768], P(('ulysses', 'blk')), may hold values from -0.109375 to 0.109375
- biases: bfloat16 [4, 768], P(None, ('ulysses', 'blk')), may hold values from -3 to 3
- hidden_unit_bias: bfloat16 [3072], P(('ulysses', 'blk')), may hold values from -3 to 3
- gains: bfloat16 [2, 768], P(None, ('ulysses', 'blk')), may hold values from 0.25 to 1.75
- shifts: bfloat16 [2, 768], P(None, ('ulysses', 'blk')), may hold values from -3 to 3
- cotangent: bfloat16 [3, 3072, 768], P(None, ('ulysses', 'blk')), may hold values from -6 to 6
- block_ids: int32 [3, 3072], replicated, may hold values from 0 to 23, never falling along the last dimension, each value on 1 to 256 neighbouring positions
- offsets: int32 [3], replicated, may hold values from 0 to 95
- pairing: int32 [12, 2], replicated, may hold values from 0 to 1, each once within a row
Outputs:
- hidden_out: bfloat16 [3, 3072, 768], P(None, ('ulysses', 'blk'))
- grad_input: bfloat16 [3, 3072, 768], P(None, ('ulysses', 'blk'))
- grad_w_qkv: float32 [768, 2304], P(('ulysses', 'blk'))
- grad_w_out: float32 [768, 768], P(('ulysses', 'blk'))
- grad_w_in: float32 [768, 3072], P(('ulysses', 'blk'))
- grad_w_down: float32 [3072, 768], P(('ulysses', 'blk'))
- grad_biases: float32 [4, 768], P(None, ('ulysses', 'blk'))
- grad_bias_in: float32 [3072], P(('ulysses', 'blk'))
- grad_gains: float32 [2, 768], P(None, ('ulysses', 'blk'))
- grad_shifts: float32 [2, 768], P(None, ('ulysses', 'blk'))
The draws below stay inside these ranges and needn't reach their ends.
Inputs may be any that keep to these rules, and one draw needn't show every extreme that they name: `block_ids`: along each sequence the block numbers never fall, and no block holds more than 256 tokens. `pairing`: each row names every large block once.
All inputs are finite; a program needn't handle non-finite values.
Results may differ from the reference program's by a relative error of at most 0.019.
Values may be sent and summed in bfloat16 or wider, within the bound.
No kernel may reach another device: no remote copies, remote signals or barrier semaphores. Data moves between devices by JAX's collectives and lax.ppermute only.
A program may use at most 320 MiB of HBM per device.

```python
import math
import jax
import jax.numpy as jnp
import numpy as np
from jax import lax

D = 768
H = 12
HD = 64
FF = 3072
TOK_SEQ_DEV = 96
SEQS = 3
DIFF_BLOCK = 256
SEQ_LEN = 3072
NBIG = 2
NBLOCKS = 24


def raised(entries, key, source, target, parts, factor):
    def block_of(position):
        return (jnp.arange(entries.shape[position]) // (entries.shape[position] // parts)).reshape((-1,) + (1,) * (entries.ndim - 1 - position))

    one_side = jax.random.permutation(key, parts)[block_of(target)]
    second = (block_of(target) + parts // 2) % parts
    return jnp.where((block_of(source) == one_side) | (block_of(source) == second), factor * entries, entries)


def steps_of(stream_key, dims, pieces, low, largest):
    loudness = 1.0
    for position, blocks in pieces:
        draws = jax.random.uniform(jax.random.fold_in(jax.random.fold_in(stream_key, 6), position), (blocks,), jnp.float32, low / len(pieces), largest / len(pieces))
        loudness = loudness * jnp.repeat(jnp.exp(draws), dims[position] // blocks).reshape((-1,) + (1,) * (len(dims) - 1 - position))
    return loudness


def profile(number_of, total, limit, skew):
    weights = [(1 << 20) // math.isqrt(standing ** skew) + 1 for standing in range(2, number_of + 1)]
    surplus, given = total - limit - (number_of - 1), [1] * (number_of - 1)
    while surplus > 0:
        candidates = [i for i in range(number_of - 1) if given[i] < limit]
        whole, left = sum([weights[i] for i in candidates]), surplus
        for i in candidates:
            extra = min(limit - given[i], max(1, left * weights[i] // whole), surplus)
            given[i] = given[i] + extra
            surplus = surplus - extra
    return np.array([limit] + given)


def ragged(own_key, amount, total, reach, slope):
    if amount == 2:
        one = jax.random.randint(own_key, (), max(1, total - reach), min(reach, total - 1) + 1)
        return jnp.stack([one, total - one])
    sizes = jnp.asarray(profile(amount, total, reach, slope), jnp.int32)
    couples = (amount - 1) // 2
    giver, sink = sizes[1:1 + 2 * couples:2], sizes[2:2 + 2 * couples:2]
    room = jnp.minimum(giver - 1, reach - sink)
    shifted = jax.random.randint(jax.random.fold_in(own_key, 1), (couples,), 0, 1 << 20) % (room + 1)
    sizes = sizes.at[1:1 + 2 * couples:2].set(giver - shifted).at[2:2 + 2 * couples:2].set(sink + shifted)
    return sizes[jax.random.permutation(jax.random.fold_in(own_key, 2), amount)]


def normal_values(key, dims, deviation, most, cuts=(), kind=jnp.bfloat16):
    level = steps_of(key, dims, cuts, -0.22, 0.18) if cuts else 1.0
    entries = jax.random.normal(key, dims, jnp.float32) * deviation * level
    return jnp.minimum(jnp.maximum(entries, -most), most).astype(kind)


def heavy_noise(key, extent, scale, limit, pieces, heavy, kind=jnp.bfloat16):
    drawn = scale * jax.random.normal(key, extent, jnp.float32)
    if pieces:
        drawn = drawn * steps_of(key, extent, pieces, -0.22, 0.18)
    return jnp.clip(raised(drawn, jax.random.fold_in(key, 3), *heavy), -limit, limit).astype(kind)


def setup_inputs(seed: int = 0) -> dict:
    streams_of = jax.random.split(jax.random.key(seed), 14)
    layer_input = heavy_noise(streams_of[0], (SEQS, SEQ_LEN, D), 1.0, 6.0, ((1, 32),), (1, 2, 32, 2.75))
    query_key_value_weight = normal_values(streams_of[1], (D, 3 * D), D ** -0.5, 0.21875, ((0, 32),))
    output_weight = normal_values(streams_of[2], (D, D), (D // 64) ** -0.5, 1.75, ((0, 32),))
    input_weight = normal_values(streams_of[3], (D, FF), D ** -0.5, 0.21875, ((0, 32),))
    down_weight = normal_values(streams_of[4], (FF, D), FF ** -0.5, 0.109375, ((0, 32),))
    biases = normal_values(streams_of[5], (4, D), 0.5, 3.0, ((1, 32),))
    hidden_unit_bias = normal_values(streams_of[6], (FF,), 0.5, 3.0, ((0, 32),))
    gains = jnp.clip(1.0 + 0.15 * jax.random.normal(streams_of[7], (2, D), jnp.float32), 0.25, 1.75).astype(jnp.bfloat16)
    shifts = normal_values(streams_of[8], (2, D), 0.5, 3.0, ((1, 32),))
    cotangent = heavy_noise(streams_of[9], (SEQS, SEQ_LEN, D), 1.0, 6.0, ((1, 32),), (1, 2, 32, 2.75))
    block_ids = jax.vmap(lambda own: jnp.searchsorted(jnp.cumsum(ragged(own, NBLOCKS, SEQ_LEN, DIFF_BLOCK, 0)), jnp.arange(SEQ_LEN), side="right"))(jax.random.split(streams_of[10], SEQS)).reshape((SEQS, SEQ_LEN)).astype(jnp.int32)
    offsets = jax.random.randint(streams_of[11], (SEQS,), 0, TOK_SEQ_DEV).astype(jnp.int32)
    pairing = jax.vmap(lambda own: jax.random.permutation(own, NBIG))(jax.random.split(streams_of[12], H)).reshape((H, NBIG)).astype(jnp.int32)
    return {"layer_input": layer_input, "query_key_value_weight": query_key_value_weight, "output_weight": output_weight, "input_weight": input_weight, "down_weight": down_weight, "biases": biases, "hidden_unit_bias": hidden_unit_bias, "gains": gains, "shifts": shifts, "cotangent": cotangent, "block_ids": block_ids, "offsets": offsets, "pairing": pairing}


NEG_FILL = -1e+30
NORM_EPS = 1e-12
TOP_PRECISION = lax.Precision.HIGHEST

@jax.custom_vjp
def low(v):
    return lax.optimization_barrier(v.astype(jnp.bfloat16)).astype(jnp.float32)

@jax.custom_vjp
def low_back(v):
    return v

def low_keep(v):
    return (low(v), None)

def low_pass(kept, grad):
    return (grad,)

def back_keep(v):
    return (v, None)

def back_low(kept, grad):
    return (low(grad),)
low.defvjp(low_keep, low_pass)
low_back.defvjp(back_keep, back_low)

def layer_norm(summed, gain_row, shift_row):
    average = lax.optimization_barrier(jnp.mean(summed, axis=-1, keepdims=True))
    centred = summed - average
    inv_std = lax.rsqrt(lax.optimization_barrier(jnp.mean(centred * centred, axis=-1, keepdims=True)) + NORM_EPS)
    return centred * inv_std * gain_row + shift_row

def attend(query, key, value, seq_ids, offset, pairing):
    length = query.shape[0]
    half_len = length // NBIG
    row_block = math.gcd(half_len, 512)
    key_halves = key.reshape(NBIG, half_len, H, HD)
    value_halves = value.reshape(NBIG, half_len, H, HD)
    id_halves = seq_ids.reshape(NBIG, half_len)
    head_ids = jnp.arange(H, dtype=jnp.int32)
    inside = jnp.arange(half_len, dtype=jnp.int32)
    score_scale = HD ** (-0.5)

    def one_block(block_idx):
        first_row = block_idx * row_block
        half_idx = first_row // half_len
        q_rows = lax.dynamic_slice_in_dim(query, first_row, row_block, 0)
        id_rows = lax.dynamic_slice_in_dim(seq_ids, first_row, row_block, 0)
        chosen = lax.dynamic_index_in_dim(pairing, half_idx, 1, keepdims=False)
        key_sel = key_halves[chosen, :, head_ids]
        value_sel = value_halves[chosen, :, head_ids]
        id_keys = id_halves[chosen]
        pos_keys = chosen[:, None] * half_len + inside[None, :]
        scores = low_back(jnp.einsum('qhd,hkd->hqk', q_rows, key_sel, precision=TOP_PRECISION) * score_scale)
        visible = (id_keys[:, None, :] <= id_rows[None, :, None]) & (pos_keys[:, None, :] >= offset)
        peak = lax.optimization_barrier(jnp.max(jnp.where(visible, scores, NEG_FILL), axis=-1, keepdims=True))
        exponent = jnp.exp(jnp.where(visible, scores - peak, -jnp.inf))
        totals = lax.optimization_barrier(jnp.sum(exponent, axis=-1, keepdims=True))
        probabilities = low(exponent / jnp.maximum(totals, 1.0))
        return jnp.einsum('hqk,hkd->qhd', probabilities, value_sel, precision=TOP_PRECISION)
    blocks = lax.map(jax.checkpoint(one_block), jnp.arange(length // row_block, dtype=jnp.int32))
    return blocks.reshape(length, H * HD)

def forward(layer_input, query_key_value_weight, output_weight, input_weight, down_weight, biases, hidden_unit_bias, gains, shifts, block_ids, offsets, pairing):
    model_width = layer_input.shape[-1]
    projected_rows = jnp.einsum('fqj,jo->fqo', layer_input, query_key_value_weight, precision=TOP_PRECISION)
    query = low_back(low(projected_rows[..., :model_width] + biases[0]))
    key = low_back(low(projected_rows[..., model_width:2 * model_width]))
    value = low_back(low(projected_rows[..., 2 * model_width:] + biases[1]))
    outputs = []
    for seq_idx in range(layer_input.shape[0]):
        seq_len = layer_input.shape[1]
        outputs.append(attend(query[seq_idx].reshape(seq_len, H, HD), key[seq_idx].reshape(seq_len, H, HD), value[seq_idx].reshape(seq_len, H, HD), block_ids[seq_idx], offsets[seq_idx], pairing))
    attention_result = low_back(low(jnp.stack(outputs)))
    attention_projection = low_back(jnp.einsum('fqj,jo->fqo', attention_result, output_weight, precision=TOP_PRECISION) + biases[2])
    middle_activations = layer_norm(layer_input + attention_projection, gains[0], shifts[0])
    inner_hidden = low_back(jnp.einsum('wgo,ot->wgt', low(middle_activations), input_weight, precision=TOP_PRECISION) + hidden_unit_bias)
    active_units = low(jax.nn.gelu(inner_hidden, approximate=False))
    feedforward_output = low_back(jnp.einsum('bvw,wq->bvq', active_units, down_weight, precision=TOP_PRECISION) + biases[3])
    return layer_norm(middle_activations + feedforward_output, gains[1], shifts[1])

def reference(layer_input, query_key_value_weight, output_weight, input_weight, down_weight, biases, hidden_unit_bias, gains, shifts, cotangent, block_ids, offsets, pairing):
    floats = tuple((array.astype(jnp.float32) for array in (layer_input, query_key_value_weight, output_weight, input_weight, down_weight, biases, hidden_unit_bias, gains, shifts)))

    def wrapped(*values):
        return forward(*values, block_ids, offsets, pairing)
    result, pullback = jax.vjp(wrapped, *floats)
    grads = pullback(cotangent.astype(jnp.float32))
    return (result.astype(jnp.bfloat16), grads[0].astype(jnp.bfloat16), grads[1], grads[2], grads[3], grads[4], grads[5], grads[6], grads[7], grads[8])
```

```python
import functools

import jax
import jax.numpy as jnp
from jax import lax
from jax.experimental import pallas as pl
from jax.experimental.pallas import tpu as pltpu
from jax.sharding import Mesh
from jax.sharding import PartitionSpec as P

H = 12
HD = 64
TP = 4
HG = H // TP
NORM_EPS = 1e-12
FILL = -1e30
FLOOR = -1e29
ALL = ("u", "r", "t")
BF = jnp.bfloat16
F32 = jnp.float32
VMEM_LIMIT = 56 * 1024 * 1024


def layer_norm(summed, gain_row, shift_row):
    average = jnp.mean(summed, axis=-1, keepdims=True)
    centred = summed - average
    inv_std = lax.rsqrt(jnp.mean(centred * centred, axis=-1, keepdims=True) + NORM_EPS)
    normed = centred * inv_std
    return (normed * gain_row + shift_row, normed, inv_std)


def norm_back(incoming, normed, inv_std, gain_row):
    scaled = incoming * gain_row
    return inv_std * (
        scaled
        - jnp.mean(scaled, axis=-1, keepdims=True)
        - normed * jnp.mean(scaled * normed, axis=-1, keepdims=True)
    )


def gelu_exact(inner_hidden):
    return jax.nn.gelu(inner_hidden, approximate=False)


def dot_nt(a, b):
    return lax.dot_general(a, b, (((1,), (1,)), ((), ())), preferred_element_type=F32)


def dot_nn(a, b):
    return lax.dot_general(a, b, (((1,), (0,)), ((), ())), preferred_element_type=F32)


def chunk_of(shards):
    return 8 if shards % 8 == 0 else shards


def forward_kernel(rows, shards, pair_ref, begin_ref, last_ref, q_ref, kv0, kv1, kv2, end_ref, att_ref, lse_ref, m_ref, l_ref, acc_ref):
    seq = pl.program_id(0)
    group = chunk_of(shards)
    nq = TP * rows
    width = group * rows
    for h, kv_ref in enumerate((kv0, kv1, kv2)):
        query = q_ref[:, 0, :, h * 128 : (h + 1) * 128].reshape(nq, 128)
        end = end_ref[0, h]
        begin = begin_ref[seq * HG + h]
        m_ref[...] = jnp.full_like(m_ref, FLOOR)
        l_ref[...] = jnp.zeros_like(l_ref)
        acc_ref[...] = jnp.zeros_like(acc_ref)

        def step(c, _):
            kv = kv_ref[0, pl.ds(c * group, group), 0].reshape(width, 128)
            spot = lax.broadcasted_iota(jnp.int32, (nq, width), 1) + c * width
            seen = (spot < end) & (spot >= begin)
            scores = jnp.where(seen, dot_nt(query, kv), FILL)
            old = m_ref[...]
            new = jnp.maximum(old, jnp.max(scores, axis=1, keepdims=True))
            weights = jnp.exp(scores - new)
            factor = jnp.exp(old - new)
            m_ref[...] = new
            l_ref[...] = l_ref[...] * factor + jnp.sum(weights, axis=1, keepdims=True)
            acc_ref[...] = acc_ref[...] * factor + dot_nn(weights.astype(BF), kv)
            return 0

        lax.fori_loop(0, pl.cdiv(last_ref[seq * HG + h], width), step, 0)
        total = jnp.maximum(l_ref[...], 1.0)
        lse_ref[0, h] = m_ref[...] + jnp.log(total)
        att = (acc_ref[...] / total).astype(BF)
        att_ref[:, 0, :, h * HD : (h + 1) * HD] = att[:, HD:].reshape(TP, rows, HD)


def query_kernel(rows, shards, pair_ref, begin_ref, last_ref, q_ref, kv0, kv1, kv2, end_ref, lse_ref, delta_ref, dout_ref, dq_ref, acc_ref):
    seq = pl.program_id(0)
    group = chunk_of(shards)
    nq = TP * rows
    width = group * rows
    for h, kv_ref in enumerate((kv0, kv1, kv2)):
        query = q_ref[:, 0, :, h * 128 : (h + 1) * 128].reshape(nq, 128)
        dout = dout_ref[:, 0, :, h * 128 : (h + 1) * 128].reshape(nq, 128)
        end = end_ref[0, h]
        lse = lse_ref[0, h]
        delta = delta_ref[0, h]
        begin = begin_ref[seq * HG + h]
        acc_ref[...] = jnp.zeros_like(acc_ref)

        def step(c, _):
            kv = kv_ref[0, pl.ds(c * group, group), 0].reshape(width, 128)
            spot = lax.broadcasted_iota(jnp.int32, (nq, width), 1) + c * width
            seen = (spot < end) & (spot >= begin)
            scores = jnp.where(seen, dot_nt(query, kv), FILL)
            prob = jnp.exp(scores - lse)
            dscore = (prob * (dot_nt(dout, kv) - delta)).astype(BF)
            acc_ref[...] += dot_nn(dscore, kv)
            return 0

        lax.fori_loop(0, pl.cdiv(last_ref[seq * HG + h], width), step, 0)
        dq = (acc_ref[...] * (HD**-0.5)).astype(BF)
        dq_ref[:, 0, :, h * HD : (h + 1) * HD] = dq[:, :HD].reshape(TP, rows, HD)


def key_kernel(rows, shards, pair_ref, begin_ref, first_ref, place_ref, q_ref, do_ref, kv0, kv1, kv2, stat_ref, dkv_ref, acc_ref):
    seq = pl.program_id(0)
    group = chunk_of(shards)
    nk = TP * rows
    width = group * rows
    start = place_ref[0]
    for h, kv_ref in enumerate((kv0, kv1, kv2)):
        kv = kv_ref[0, :, 0].reshape(nk, 128)
        begin = begin_ref[seq * HG + h]
        acc_ref[...] = jnp.zeros_like(acc_ref)

        def step(c, _):
            query = q_ref[pl.ds(c * group, group), 0, :, h * 128 : (h + 1) * 128].reshape(width, 128)
            dout = do_ref[pl.ds(c * group, group), 0, :, h * 128 : (h + 1) * 128].reshape(width, 128)
            stat = stat_ref[0, h, :, pl.ds(pl.multiple_of(c * width, 128), width)]
            lse, delta, end = stat[0:1], stat[1:2], stat[2:3].astype(jnp.int32)
            spot = lax.broadcasted_iota(jnp.int32, (nk, width), 0) + start
            seen = (spot < end) & (spot >= begin)
            scores = jnp.where(seen, dot_nt(kv, query), FILL)
            prob = jnp.exp(scores - lse)
            dscore = (prob * (dot_nt(kv, dout) - delta)).astype(BF)
            acc_ref[...] += dot_nn(dscore, query) + dot_nn(prob.astype(BF), dout)
            return 0

        lax.fori_loop(first_ref[seq * HG + h] // width, shards // group, step, 0)
        dkv_ref[:, 0, :, h * 128 : (h + 1) * 128] = acc_ref[...].astype(BF).reshape(TP, rows, 128)


def keys_spec(h, shards, rows):
    return pl.BlockSpec((1, shards, 1, rows, 128), lambda s, pair, *_: (pair[h], 0, s, 0, h))


def attend_forward(q_loc, kv, pair, begin, last, end_col):
    _, shards, seqs, rows, _ = kv.shape
    nq = TP * rows
    row_spec = pl.BlockSpec((TP, 1, rows, 384), lambda s, *_: (0, s, 0, 0))
    col_spec = pl.BlockSpec((1, HG, nq, 1), lambda s, *_: (s, 0, 0, 0))
    return pl.pallas_call(
        functools.partial(forward_kernel, rows, shards),
        grid_spec=pltpu.PrefetchScalarGridSpec(
            num_scalar_prefetch=3,
            grid=(seqs,),
            in_specs=[row_spec] + [keys_spec(h, shards, rows) for h in range(HG)] + [col_spec],
            out_specs=[pl.BlockSpec((TP, 1, rows, HG * HD), lambda s, *_: (0, s, 0, 0)), col_spec],
            scratch_shapes=[pltpu.VMEM((nq, 1), F32), pltpu.VMEM((nq, 1), F32), pltpu.VMEM((nq, 128), F32)],
        ),
        out_shape=[
            jax.ShapeDtypeStruct((TP, seqs, rows, HG * HD), BF),
            jax.ShapeDtypeStruct((seqs, HG, nq, 1), F32),
        ],
        compiler_params=pltpu.CompilerParams(vmem_limit_bytes=VMEM_LIMIT),
        name="attend_forward",
    )(pair, begin, last, q_loc, kv, kv, kv, end_col)


def attend_query(q_loc, kv, pair, begin, last, end_col, lse, delta, dout):
    _, shards, seqs, rows, _ = kv.shape
    nq = TP * rows
    row_spec = pl.BlockSpec((TP, 1, rows, 384), lambda s, *_: (0, s, 0, 0))
    col_spec = pl.BlockSpec((1, HG, nq, 1), lambda s, *_: (s, 0, 0, 0))
    return pl.pallas_call(
        functools.partial(query_kernel, rows, shards),
        grid_spec=pltpu.PrefetchScalarGridSpec(
            num_scalar_prefetch=3,
            grid=(seqs,),
            in_specs=[row_spec]
            + [keys_spec(h, shards, rows) for h in range(HG)]
            + [col_spec, col_spec, col_spec, row_spec],
            out_specs=pl.BlockSpec((TP, 1, rows, HG * HD), lambda s, *_: (0, s, 0, 0)),
            scratch_shapes=[pltpu.VMEM((nq, 128), F32)],
        ),
        out_shape=jax.ShapeDtypeStruct((TP, seqs, rows, HG * HD), BF),
        compiler_params=pltpu.CompilerParams(vmem_limit_bytes=VMEM_LIMIT),
        name="attend_query",
    )(pair, begin, last, q_loc, kv, kv, kv, end_col, lse, delta, dout)


def attend_key(q_all, do_all, kv, pair, begin, first, place, stats):
    _, shards, seqs, rows, _ = kv.shape
    nk = TP * rows
    all_spec = pl.BlockSpec((shards, 1, rows, 384), lambda s, *_: (0, s, 0, 0))

    def own_keys(h):
        return pl.BlockSpec((1, TP, 1, rows, 128), lambda s, pair, begin, first, place: (pair[h], place[1], s, 0, h))

    return pl.pallas_call(
        functools.partial(key_kernel, rows, shards),
        grid_spec=pltpu.PrefetchScalarGridSpec(
            num_scalar_prefetch=4,
            grid=(seqs,),
            in_specs=[all_spec, all_spec]
            + [own_keys(h) for h in range(HG)]
            + [pl.BlockSpec((1, HG, 8, shards * rows), lambda s, *_: (s, 0, 0, 0))],
            out_specs=pl.BlockSpec((TP, 1, rows, 384), lambda s, *_: (0, s, 0, 0)),
            scratch_shapes=[pltpu.VMEM((nk, 128), F32)],
        ),
        out_shape=jax.ShapeDtypeStruct((TP, seqs, rows, 384), BF),
        compiler_params=pltpu.CompilerParams(vmem_limit_bytes=VMEM_LIMIT),
        name="attend_key",
    )(pair, begin, first, place, q_all, do_all, kv, kv, kv, stats)


def ring_gather(piece, axis):
    size = lax.axis_size(axis)
    me = lax.axis_index(axis)
    out = jnp.zeros((size,) + piece.shape, piece.dtype)
    out = lax.dynamic_update_index_in_dim(out, piece, me, 0)
    for k in range(1, size):
        piece = lax.ppermute(piece, axis, [(i, (i + 1) % size) for i in range(size)])
        out = lax.dynamic_update_index_in_dim(out, piece, (me - k) % size, 0)
    return out


def per_device(layer_input, wqkv, wo, wi, wd, biases, hidden_bias, gains, shifts, cotangent, block_ids, offsets, pairing):
    seqs, rows, width = layer_input.shape
    devices = lax.axis_size(ALL)
    ring = lax.axis_size("r")
    shards = ring * TP
    half = shards * rows
    tokens = seqs * rows
    me_u, me_r, me_t = lax.axis_index("u"), lax.axis_index("r"), lax.axis_index("t")
    part = wqkv.shape[0]
    fpart = wd.shape[0]
    hidden = wi.shape[1]
    cols_in = hidden // width

    def rows_of(m):
        return [m[:, k * width : (k + 1) * width] for k in range(m.shape[1] // width)]

    small = jnp.concatenate([biases.reshape(-1), hidden_bias, gains.reshape(-1), shifts.reshape(-1)])
    small = jnp.zeros((16, width), BF).at[0, : small.shape[0]].set(small)
    counts = [tokens] + [part] * 3 + [part] + [part] * cols_in + [fpart, 16]
    packed = jnp.concatenate([layer_input.reshape(tokens, width)] + rows_of(wqkv) + [wo] + rows_of(wi) + [wd, small])
    everything = lax.all_gather(packed, ALL, axis=0, tiled=False)
    marks = [0]
    for n in counts:
        marks.append(marks[-1] + n)

    def piece(i):
        return everything[:, marks[i] : marks[i + 1]]

    x_all = piece(0).reshape(2, shards, seqs, rows, width)
    wq, wk, wv = (piece(1 + i).reshape(devices * part, width) for i in range(3))
    wo_all = piece(4).reshape(devices * part, width)
    wi_all = [piece(5 + i).reshape(devices * part, width) for i in range(cols_in)]
    wd_all = piece(5 + cols_in).reshape(devices * fpart, width)
    small_all = piece(6 + cols_in)[:, 0].astype(F32)
    bias_f = small_all[:, : 4 * part].reshape(devices, 4, part).transpose(1, 0, 2).reshape(4, width)
    bin_f = small_all[:, 4 * part : 4 * part + fpart].reshape(-1)
    at = 4 * part + fpart
    gain_f = small_all[:, at : at + 2 * part].reshape(devices, 2, part).transpose(1, 0, 2).reshape(2, width)
    shift_f = small_all[:, at + 2 * part : at + 4 * part].reshape(devices, 2, part).transpose(1, 0, 2).reshape(2, width)

    def heads_of(m):
        return lax.dynamic_slice_in_dim(m.reshape(m.shape[0], H, HD), me_t * HG, HG, 1)

    wq_h, wk_h, wv_h = heads_of(wq), heads_of(wk), heads_of(wv)
    bq_h, bv_h = heads_of(bias_f[0:1]), heads_of(bias_f[1:2])
    wq_pad = jnp.concatenate([wq_h, jnp.zeros_like(wq_h)], 2).reshape(width, HG * 128)
    wkv = jnp.concatenate([wk_h, wv_h], 2).reshape(width, HG * 128)
    bq_pad = jnp.concatenate([bq_h, jnp.zeros_like(bq_h)], 2).reshape(HG * 128)
    bkv = jnp.concatenate([jnp.zeros_like(bv_h), bv_h], 2).reshape(HG * 128)
    x_half = lax.dynamic_index_in_dim(x_all, me_u, 0, keepdims=False)
    kv = (jnp.einsum("urscd,de->ursce", x_all, wkv, preferred_element_type=F32) + bkv).astype(BF)
    q_all = ((jnp.einsum("rscd,de->rsce", x_half, wq_pad, preferred_element_type=F32) + bq_pad) * (HD**-0.5)).astype(BF)
    q_loc = lax.dynamic_slice_in_dim(q_all, me_r * TP, TP, 0)

    pair = lax.dynamic_slice_in_dim(lax.dynamic_index_in_dim(pairing, me_u, 1, keepdims=False), me_t * HG, HG, 0)
    ids = block_ids.reshape(seqs, 2, half)
    ids_own = lax.dynamic_index_in_dim(ids, me_u, 1, keepdims=False)
    ends = jnp.sum((ids[:, :, None, :] <= ids_own[:, None, :, None]).astype(jnp.int32), axis=-1)
    end_all = jnp.where((pair == 0)[None, :, None], ends[:, 0:1], ends[:, 1:2])
    end_loc = lax.dynamic_slice_in_dim(end_all, me_r * TP * rows, TP * rows, 2)
    begin = jnp.maximum(offsets[:, None] - pair[None, :] * half, 0).reshape(-1)
    last = end_loc[:, :, -1].reshape(-1)
    start = me_r * TP * rows
    first = jnp.sum((end_all <= start).astype(jnp.int32), axis=-1).reshape(-1)
    end_col = end_loc[..., None]

    att, lse = attend_forward(q_loc, kv, pair, begin, last, end_col)
    att_t = lax.all_to_all(att, "t", split_axis=0, concat_axis=0, tiled=True)
    att_tok = att_t.transpose(1, 2, 0, 3).reshape(tokens, width)

    x_own = layer_input.reshape(tokens, width)
    proj = dot_nn(att_tok, wo_all) + bias_f[2]
    mid, normed_one, inv_one = layer_norm(x_own.astype(F32) + proj, gain_f[0], shift_f[0])
    mid_low = mid.astype(BF)
    inner = jnp.concatenate([dot_nn(mid_low, w) for w in wi_all], axis=1) + bin_f
    active, gelu_pull = jax.vjp(gelu_exact, inner)
    active_low = active.astype(BF)
    feed = dot_nn(active_low, wd_all) + bias_f[3]
    second, normed_two, inv_two = layer_norm(mid + feed, gain_f[1], shift_f[1])
    hidden_out = second.astype(BF).reshape(seqs, rows, width)
    grad_out = cotangent.reshape(tokens, width).astype(F32)
    dgain_two = jnp.sum(grad_out * normed_two, axis=0)
    dshift_two = jnp.sum(grad_out, axis=0)
    dsecond = norm_back(grad_out, normed_two, inv_two, gain_f[1])
    dfeed = dsecond.astype(BF)
    dbias_out = jnp.sum(dfeed.astype(F32), axis=0)
    dactive = dot_nt(dfeed, wd_all)
    dinner = gelu_pull(dactive)[0].astype(BF)
    dbias_in = jnp.sum(dinner.astype(F32), axis=0)
    dmid = dsecond
    for k, w in enumerate(wi_all):
        dmid = dmid + dot_nt(dinner[:, k * width : (k + 1) * width], w)
    dgain_one = jnp.sum(dmid * normed_one, axis=0)
    dshift_one = jnp.sum(dmid, axis=0)
    dsum = norm_back(dmid, normed_one, inv_one, gain_f[0])
    dproj = dsum.astype(BF)
    dbias_o = jnp.sum(dproj.astype(F32), axis=0)
    datt = dot_nt(dproj, wo_all).astype(BF)

    def dot_tn(a, b):
        return lax.dot_general(a, b, (((0,), (0,)), ((), ())), preferred_element_type=F32).astype(BF)

    dwi = [dot_tn(mid_low, dinner[:, k * width : (k + 1) * width]).reshape(devices, part, width) for k in range(cols_in)]
    dwd = dot_tn(active_low, dfeed).reshape(devices, fpart, width)
    dwo = dot_tn(att_tok, dproj).reshape(devices, part, width)

    def shard_cols(v):
        return v.reshape(-1, devices, v.shape[-1] // devices).transpose(1, 0, 2).reshape(devices, -1)

    dsmall = jnp.concatenate(
        [
            shard_cols(jnp.stack([dbias_o, dbias_out])),
            shard_cols(dbias_in),
            shard_cols(jnp.stack([dgain_one, dgain_two])),
            shard_cols(jnp.stack([dshift_one, dshift_two])),
        ],
        axis=1,
    ).astype(BF)
    dsmall = jnp.zeros((devices, 16, width), BF).at[:, 0, : dsmall.shape[1]].set(dsmall)
    packed_grads = jnp.concatenate(dwi + [dwd, dwo, dsmall], axis=1)
    summed = lax.psum_scatter(packed_grads, ALL, scatter_dimension=0, tiled=False).astype(F32)
    at = cols_in * part
    grad_w_in = jnp.concatenate([summed[k * part : (k + 1) * part] for k in range(cols_in)], axis=1)
    grad_w_down = summed[at : at + fpart]
    grad_w_out = summed[at + fpart : at + fpart + part]
    flat = summed[at + fpart + part]
    grad_bo = flat[: 2 * part].reshape(2, part)
    grad_bin = flat[2 * part : 2 * part + fpart]
    at = 2 * part + fpart
    grad_gains = flat[at : at + 2 * part].reshape(2, part)
    grad_shifts = flat[at + 2 * part : at + 4 * part].reshape(2, part)

    datt_t = datt.reshape(seqs, rows, TP, HG * HD).transpose(2, 0, 1, 3)
    dout = lax.all_to_all(datt_t, "t", split_axis=0, concat_axis=0, tiled=True)
    spread = (TP, seqs, rows, HG, HD)
    delta = jnp.sum((dout.astype(F32) * att.astype(F32)).reshape(spread), axis=-1)
    delta = delta.transpose(1, 3, 0, 2).reshape(seqs, HG, TP * rows)
    dout_pad = jnp.pad(dout.reshape(spread), ((0, 0),) * 4 + ((HD, 0),)).reshape(TP, seqs, rows, HG * 128)
    dout_r = ring_gather(dout, "r")
    stat_r = ring_gather(jnp.stack([lse[..., 0], delta], axis=2), "r")
    dq = attend_query(q_loc, kv, pair, begin, last, end_col, lse, delta[..., None], dout_pad)
    do_all = jnp.pad(dout_r.reshape((shards,) + spread[1:]), ((0, 0),) * 4 + ((HD, 0),)).reshape(shards, seqs, rows, HG * 128)
    stats = stat_r.transpose(1, 2, 3, 0, 4).reshape(seqs, HG, 2, half)
    stats = jnp.concatenate([stats, end_all[:, :, None].astype(F32), jnp.zeros((seqs, HG, 5, half), F32)], axis=2)
    place = jnp.stack([start, me_r]).astype(jnp.int32)
    dkv = attend_key(q_all, do_all, kv, pair, begin, first, place, stats)

    is_own = jnp.repeat(pair == me_u, 128)[None]
    dq2 = dq.reshape(TP * tokens, HG * HD)
    dkv2 = dkv.reshape(TP * tokens, HG * 128)
    dkv_own = jnp.where(is_own, dkv2, 0).astype(BF)
    dkv_oth = jnp.where(is_own, 0, dkv2).astype(BF)
    wq_own = wq_h.reshape(width, HG * HD)
    from_own = (dot_nt(dq2, wq_own) + dot_nt(dkv_own, wkv)).astype(BF).reshape(TP, tokens, width)
    from_oth = dot_nt(dkv_oth, wkv).astype(BF).reshape(TP, tokens, width)
    swap = [(0, 1), (1, 0)]
    got_oth = lax.all_to_all(from_oth, "t", split_axis=0, concat_axis=0, tiled=True)
    got_own = lax.all_to_all(from_own, "t", split_axis=0, concat_axis=0, tiled=True)
    oth = lax.ppermute(jnp.sum(got_oth.astype(F32), axis=0).astype(BF), "u", swap)
    grad_input = dsum + jnp.sum(got_own.astype(F32), axis=0) + oth.astype(F32)
    grad_input = grad_input.astype(BF).reshape(seqs, rows, width)

    x_rows = lax.dynamic_slice_in_dim(x_all, me_r * TP, TP, 1).reshape(2, TP * tokens, width)
    x_mine = lax.dynamic_index_in_dim(x_rows, me_u, 0, keepdims=False)
    x_yours = lax.dynamic_index_in_dim(x_rows, 1 - me_u, 0, keepdims=False)

    def dot_tn32(a, b):
        return lax.dot_general(a, b, (((0,), (0,)), ((), ())), preferred_element_type=F32)

    dwq = dot_tn32(x_mine, dq2)
    dwkv = dot_tn32(x_mine, dkv_own) + dot_tn32(x_yours, dkv_oth)
    dbq = jnp.sum(dq2.astype(F32), axis=0)
    dbkv = jnp.sum(dkv2.astype(F32), axis=0)
    send = jnp.concatenate([dwq, dwkv], axis=1).astype(BF).reshape(devices, part, 576)
    extra = jnp.concatenate([dbq, dbkv]).astype(BF)
    send = jnp.concatenate([send, jnp.broadcast_to(extra, (devices, 8, 576))], axis=1)
    got = lax.all_to_all(send, ALL, split_axis=0, concat_axis=0, tiled=True)
    got = jnp.sum(got.astype(F32).reshape(2 * ring, TP, part + 8, 576), axis=0)
    got_q = got[:, :, :192].transpose(1, 0, 2).reshape(part + 8, width)
    got_kv = got[:, :, 192:].reshape(TP, part + 8, HG, 2, HD).transpose(3, 1, 0, 2, 4).reshape(2, part + 8, width)
    grad_w_qkv = jnp.concatenate([got_q[:part], got_kv[0, :part], got_kv[1, :part]], axis=1)
    mine = lax.axis_index(ALL) * part
    grad_bq = lax.dynamic_slice_in_dim(got_q[part], mine, part, 0)
    grad_bv = lax.dynamic_slice_in_dim(got_kv[1, part], mine, part, 0)
    grad_biases = jnp.concatenate([jnp.stack([grad_bq, grad_bv]), grad_bo])
    return (hidden_out, grad_input, grad_w_qkv, grad_w_out, grad_w_in, grad_w_down, grad_biases, grad_bin, grad_gains, grad_shifts)


def solution(mesh):
    wide = mesh.shape["blk"]
    grid = Mesh(mesh.devices.reshape(2, wide // TP, TP), ALL)
    rows2, cols1 = P(ALL, None), P(None, ALL)
    toks = P(None, ALL, None)
    return jax.shard_map(
        per_device,
        mesh=grid,
        in_specs=(toks, rows2, rows2, rows2, rows2, cols1, P(ALL), cols1, cols1, toks, P(), P(), P()),
        out_specs=(toks, toks, rows2, rows2, rows2, rows2, cols1, P(ALL), cols1, cols1),
        check_vma=False,
    )
```

```python
import functools

import jax
import jax.numpy as jnp
from jax import lax
from jax.experimental import pallas as pl
from jax.experimental.pallas import tpu as pltpu
from jax.sharding import Mesh
from jax.sharding import PartitionSpec as P

H = 12
HD = 64
TP = 4
HG = H // TP
NORM_EPS = 1e-12
FILL = -1e30
FLOOR = -1e29
ALL = ("u", "r", "y", "c")
BF = jnp.bfloat16
F32 = jnp.float32
VMEM_LIMIT = 56 * 1024 * 1024


def split_three(v):
    high = v.astype(BF)
    v = v - high.astype(F32)
    middle = v.astype(BF)
    return high, middle, (v - middle.astype(F32)).astype(BF)


def dot_nt(a, b):
    return lax.dot_general(a, b, (((1,), (1,)), ((), ())), preferred_element_type=F32)


def dot_nn(a, b):
    return lax.dot_general(a, b, (((1,), (0,)), ((), ())), preferred_element_type=F32)


def dot_tn(a, b):
    return lax.dot_general(a, b, (((0,), (0,)), ((), ())), preferred_element_type=F32)


def lanes_like(shape):
    return lax.broadcasted_iota(jnp.int32, shape, len(shape) - 1)


def chooser(h, kind, depth):
    at = HD + kind * 3 * HG + 3 * h
    lane = lanes_like((depth, 128))
    return jnp.where((lane >= at) & (lane < at + 3), -1.0, 0.0).astype(BF)


def chunk_of(shards):
    return 16 if shards % 16 == 0 else shards


def key_spots(first, count, begin, end_row):
    spot = lax.broadcasted_iota(jnp.int32, (count, 1), 0) + first
    return jnp.where(spot >= begin, spot, 1 << 30) < end_row


def forward_kernel(rows, shards, pair_ref, begin_ref, last_ref, q_ref, kv0, kv1, kv2, end_ref, att_ref, m_ref, l_ref, acc_ref):
    seq = pl.program_id(0)
    group = chunk_of(shards)
    nq = TP * rows
    width = group * rows
    for h in range(HG):
        m_ref[h] = jnp.full((1, nq), FLOOR, F32)
        l_ref[h] = jnp.zeros((1, nq), F32)
        acc_ref[h] = jnp.zeros((128, nq), F32)

    def step(c, _):
        for h, kv_ref in enumerate((kv0, kv1, kv2)):
            query = q_ref[:, 0, :, h * 128 : (h + 1) * 128].reshape(nq, 128)
            kv = kv_ref[0, pl.ds(c * group, group), 0].reshape(width, 128)
            seen = key_spots(c * width, width, begin_ref[seq * HG + h], end_ref[0, h])
            scores = jnp.where(seen, dot_nt(kv, query), FILL)
            old = m_ref[h]
            new = jnp.maximum(old, jnp.max(scores, axis=0, keepdims=True))
            weights = jnp.exp(scores - new)
            factor = jnp.exp(old - new)
            m_ref[h] = new
            l_ref[h] = l_ref[h] * factor + jnp.sum(weights, axis=0, keepdims=True)
            acc_ref[h] = acc_ref[h] * factor + dot_tn(kv, weights.astype(BF))
        return 0

    trips = [pl.cdiv(last_ref[seq * HG + h], width) for h in range(HG)]
    lax.fori_loop(0, functools.reduce(jnp.maximum, trips), step, 0)
    turn = lax.broadcasted_iota(jnp.int32, (HD, nq), 0)
    notes = jnp.zeros((HD, nq), F32)
    for h in range(HG):
        total = jnp.maximum(l_ref[h], 1.0)
        for p, value in enumerate(split_three(m_ref[h] + jnp.log(total))):
            notes = jnp.where(turn == 3 * HG + 3 * h + p, value.astype(F32), notes)
        att = (acc_ref[h] / total)[HD:].T.astype(BF)
        att_ref[:, 0, :, h * HD : (h + 1) * HD] = att.reshape(TP, rows, HD)
    att_ref[:, 0, :, HG * HD :] = notes.T.astype(BF).reshape(TP, rows, HD)


def output_gradient(load_ref, h, count):
    dout = load_ref[:, 0, :, h * HD : (h + 1) * HD].reshape(count, HD)
    return jnp.concatenate([jnp.zeros_like(dout), dout], axis=1)


def query_kernel(rows, shards, pair_ref, begin_ref, last_ref, q_ref, kv0, kv1, kv2, end_ref, load_ref, dq_ref, acc_ref):
    seq = pl.program_id(0)
    group = chunk_of(shards)
    nq = TP * rows
    width = group * rows
    notes = load_ref[:, 0, :, 128:].reshape(nq, 128)
    acc_ref[...] = jnp.zeros_like(acc_ref)

    def step(c, _):
        for h, kv_ref in enumerate((kv0, kv1, kv2)):
            query = q_ref[:, 0, :, h * 128 : (h + 1) * 128].reshape(nq, 128)
            kv = kv_ref[0, pl.ds(c * group, group), 0].reshape(width, 128)
            seen = key_spots(c * width, width, begin_ref[seq * HG + h], end_ref[0, h])
            query = jnp.concatenate([query, notes], axis=1)
            dout = jnp.concatenate([output_gradient(load_ref, h, nq), notes], axis=1)
            scores = dot_nt(jnp.concatenate([kv, chooser(h, 1, width)], axis=1), query)
            prob = jnp.exp(jnp.where(seen, scores, FILL))
            dprob = dot_nt(jnp.concatenate([kv, chooser(h, 0, width)], axis=1), dout)
            acc_ref[h] += dot_tn(kv, (prob * dprob).astype(BF))
        return 0

    trips = [pl.cdiv(last_ref[seq * HG + h], width) for h in range(HG)]
    lax.fori_loop(0, functools.reduce(jnp.maximum, trips), step, 0)
    for h in range(HG):
        dq = (acc_ref[h][:HD] * (HD**-0.5)).T.astype(BF)
        dq_ref[:, 0, :, h * HD : (h + 1) * HD] = dq.reshape(TP, rows, HD)


def key_kernel(rows, pair_ref, begin_ref, reach_ref, place_ref, q_ref, load_ref, kv0, kv1, kv2, end_ref, old_ref, dkv_ref):
    seq = pl.program_id(0)
    span = TP * rows
    start = place_ref[0]
    reach = [reach_ref[seq * HG + h] for h in range(HG)]
    needed = functools.reduce(jnp.maximum, reach) > start

    @pl.when(needed)
    def _():
        notes = load_ref[:, 0, :, 128:].reshape(span, 128)
        for h, kv_ref in enumerate((kv0, kv1, kv2)):
            lanes = slice(h * 128, (h + 1) * 128)
            kv = kv_ref[0, :, 0].reshape(span, 128)
            query = q_ref[:, 0, :, lanes].reshape(span, 128)
            dout = output_gradient(load_ref, h, span)
            seen = key_spots(start, span, begin_ref[seq * HG + h], end_ref[0, h])
            scores = dot_nt(jnp.concatenate([kv, chooser(h, 1, span)], axis=1), jnp.concatenate([query, notes], axis=1))
            prob = jnp.exp(jnp.where(seen, scores, FILL))
            dprob = dot_nt(jnp.concatenate([kv, chooser(h, 0, span)], axis=1), jnp.concatenate([dout, notes], axis=1))
            sides = jnp.concatenate([(prob * dprob).astype(BF), prob.astype(BF)], axis=1)
            new = dot_nn(sides, jnp.concatenate([query, dout], axis=0))
            dkv_ref[:, 0, :, lanes] = old_ref[:, 0, :, lanes] + new.reshape(TP, rows, 128)

    @pl.when(jnp.logical_not(needed))
    def _():
        dkv_ref[...] = old_ref[...]


def project_kernel(seqs, rows, fresh, spot_ref, *refs):
    pieces, w_ref, bias_ref = refs[:8], refs[8], refs[9]
    kv_out, q_out, kv_tmp, q_tmp, kv_sem, q_sem = refs[10 if fresh else 12 :]
    keys = HG * 128
    tokens = seqs * rows
    me_u, me_y, me_c, source = (spot_ref[i] for i in range(4))
    for which in range(2):
        core = me_c if which == 0 else 1 - me_c
        x = jnp.concatenate([pieces[which * 4 + i][...] for i in range(4)], axis=0)
        if which == 0:
            q_tmp[...] = jnp.zeros_like(q_tmp)
        kv = (dot_nn(x, w_ref[:, :keys]) + bias_ref[0:1, :keys]).astype(BF)
        for i in range(4):
            p, q = i // 2, i % 2
            x_rel = jnp.where(core == 0, q, p)
            y_rel = jnp.where(core == 0, p, q)
            shard = jnp.bitwise_xor(me_y, y_rel) * 2 + core
            slot = which * 4 + i
            kv_tmp[slot] = kv[i * tokens : (i + 1) * tokens].reshape(seqs, rows, keys)
            spot = kv_out.at[jnp.bitwise_xor(me_u, x_rel), source, shard]
            pltpu.make_async_copy(kv_tmp.at[slot], spot, kv_sem.at[slot]).start()
        second = jnp.where(core == 0, x[2 * tokens : 3 * tokens], x[tokens : 2 * tokens])
        for y_rel, part in enumerate((x[:tokens], second)):
            query = (dot_nn(part, w_ref[:, keys:]) + bias_ref[0:1, keys:]) * (HD**-0.5)
            slot = which * 2 + y_rel
            query = query.astype(BF)
            for h in range(HG):
                q_tmp[slot, :, :, h * 128 : h * 128 + HD] = query[:, h * HD : (h + 1) * HD].reshape(seqs, rows, HD)
            shard = jnp.bitwise_xor(me_y, y_rel) * 2 + core
            pltpu.make_async_copy(q_tmp.at[slot], q_out.at[source, shard], q_sem.at[slot]).start()
    for slot in range(8):
        pltpu.make_async_copy(kv_tmp.at[slot], kv_out.at[0, 0, 0], kv_sem.at[slot]).wait()
    for slot in range(4):
        pltpu.make_async_copy(q_tmp.at[slot], q_out.at[0, 0], q_sem.at[slot]).wait()


def project(pieces, weight, bias, spot, buffers, ring, seqs, rows):
    keys = HG * 128
    width = weight.shape[0]
    tokens = seqs * rows
    extra = [] if buffers is None else list(buffers)
    anywhere = pl.BlockSpec(memory_space=pl.ANY)
    local = pl.BlockSpec(memory_space=pltpu.VMEM)
    return pl.pallas_call(
        functools.partial(project_kernel, seqs, rows, not extra),
        in_specs=[pl.BlockSpec(memory_space=pltpu.SMEM)] + [local] * 10 + [anywhere] * len(extra),
        out_specs=[anywhere, anywhere],
        scratch_shapes=[
            pltpu.VMEM((8, seqs, rows, keys), BF),
            pltpu.VMEM((4, seqs, rows, keys), BF),
            pltpu.SemaphoreType.DMA((8,)),
            pltpu.SemaphoreType.DMA((4,)),
        ],
        out_shape=[
            jax.ShapeDtypeStruct((2, ring, TP, seqs, rows, keys), BF),
            jax.ShapeDtypeStruct((ring, TP, seqs, rows, keys), BF),
        ],
        input_output_aliases={11: 0, 12: 1} if extra else {},
        compiler_params=pltpu.CompilerParams(vmem_limit_bytes=VMEM_LIMIT),
        cost_estimate=pl.CostEstimate(flops=12 * tokens * width * keys * 2, bytes_accessed=12 << 20, transcendentals=0),
        name="project",
    )(spot, *pieces, weight, bias, *extra)


def keys_spec(h, shards, rows):
    return pl.BlockSpec((1, shards, 1, rows, 128), lambda s, pair, *_: (pair[h], 0, s, 0, h))


def attend_forward(q_loc, kv, pair, begin, last, end_row_own):
    _, shards, seqs, rows, _ = kv.shape
    nq = TP * rows
    row_spec = pl.BlockSpec((TP, 1, rows, 384), lambda s, *_: (0, s, 0, 0))
    end_spec = pl.BlockSpec((1, HG, 1, nq), lambda s, *_: (s, 0, 0, 0))
    return pl.pallas_call(
        functools.partial(forward_kernel, rows, shards),
        grid_spec=pltpu.PrefetchScalarGridSpec(
            num_scalar_prefetch=3,
            grid=(seqs,),
            in_specs=[row_spec] + [keys_spec(h, shards, rows) for h in range(HG)] + [end_spec],
            out_specs=pl.BlockSpec((TP, 1, rows, 256), lambda s, *_: (0, s, 0, 0)),
            scratch_shapes=[pltpu.VMEM((HG, 1, nq), F32), pltpu.VMEM((HG, 1, nq), F32), pltpu.VMEM((HG, 128, nq), F32)],
        ),
        out_shape=jax.ShapeDtypeStruct((TP, seqs, rows, 256), BF),
        compiler_params=pltpu.CompilerParams(vmem_limit_bytes=VMEM_LIMIT),
        cost_estimate=pl.CostEstimate(flops=4 * 9 * nq * shards * rows * 128, bytes_accessed=12 << 20, transcendentals=0),
        name="attend_forward",
    )(pair, begin, last, q_loc, kv, kv, kv, end_row_own)


def attend_query(q_loc, kv, pair, begin, last, end_row_own, load):
    _, shards, seqs, rows, _ = kv.shape
    nq = TP * rows
    row_spec = pl.BlockSpec((TP, 1, rows, 384), lambda s, *_: (0, s, 0, 0))
    end_spec = pl.BlockSpec((1, HG, 1, nq), lambda s, *_: (s, 0, 0, 0))
    return pl.pallas_call(
        functools.partial(query_kernel, rows, shards),
        grid_spec=pltpu.PrefetchScalarGridSpec(
            num_scalar_prefetch=3,
            grid=(seqs,),
            in_specs=[row_spec]
            + [keys_spec(h, shards, rows) for h in range(HG)]
            + [end_spec, pl.BlockSpec((TP, 1, rows, 256), lambda s, *_: (0, s, 0, 0))],
            out_specs=pl.BlockSpec((TP, 1, rows, HG * HD), lambda s, *_: (0, s, 0, 0)),
            scratch_shapes=[pltpu.VMEM((HG, 128, nq), F32)],
        ),
        out_shape=jax.ShapeDtypeStruct((TP, seqs, rows, HG * HD), BF),
        compiler_params=pltpu.CompilerParams(vmem_limit_bytes=VMEM_LIMIT),
        cost_estimate=pl.CostEstimate(flops=6 * 9 * nq * shards * rows * 128, bytes_accessed=12 << 20, transcendentals=0),
        name="attend_query",
    )(pair, begin, last, q_loc, kv, kv, kv, end_row_own, load)


def attend_key(q_all, load, kv, pair, begin, reach, place, end_row, old):
    _, shards, seqs, rows, _ = kv.shape

    def own_keys(h):
        return pl.BlockSpec((1, TP, 1, rows, 128), lambda s, pair, begin, reach, place: (pair[h], place[1], s, 0, h))

    total = pl.BlockSpec((TP, 1, rows, 384), lambda s, *_: (0, s, 0, 0))
    return pl.pallas_call(
        functools.partial(key_kernel, rows),
        grid_spec=pltpu.PrefetchScalarGridSpec(
            num_scalar_prefetch=4,
            grid=(seqs,),
            in_specs=[
                pl.BlockSpec((TP, 1, rows, 384), lambda s, pair, begin, reach, place: (place[2], s, 0, 0)),
                pl.BlockSpec((TP, 1, rows, 256), lambda s, *_: (0, s, 0, 0)),
            ]
            + [own_keys(h) for h in range(HG)]
            + [pl.BlockSpec((1, HG, 1, TP * rows), lambda s, *_: (s, 0, 0, 0)), total],
            out_specs=total,
        ),
        out_shape=jax.ShapeDtypeStruct((TP, seqs, rows, 384), F32),
        input_output_aliases={10: 0},
        compiler_params=pltpu.CompilerParams(vmem_limit_bytes=VMEM_LIMIT),
        cost_estimate=pl.CostEstimate(flops=8 * 9 * (TP * rows) ** 2 * 128, bytes_accessed=8 << 20, transcendentals=0),
        name="attend_key",
    )(pair, begin, reach, place, q_all, load, kv, kv, kv, end_row, old)


def norm_parts(summed):
    centred = summed - jnp.mean(summed, axis=1, keepdims=True)
    inv_std = lax.rsqrt(jnp.mean(centred * centred, axis=1, keepdims=True) + NORM_EPS)
    return centred * inv_std, inv_std


def dense_kernel(fold, att_ref, x_ref, cot_ref, order_ref, dense_ref, out_ref, load_ref, dsum_ref, keep_ref, send_ref, w, note, grad, grad_note, act, slope, turn, in_sem, out_sem):
    tokens, width = x_ref.shape
    blocks = 2 * fold + 1

    def fetch(b):
        wide = pl.ds(b * width, width) if b < blocks else pl.ds(blocks * width, 128)
        return pltpu.make_async_copy(dense_ref.at[:, wide], w.at[b] if b < blocks else note, in_sem.at[b])

    def ship(b, side):
        wide = pl.ds(b * width, width) if b < blocks else pl.ds(blocks * width, 128)
        rows = pl.ds(side * (width // 2), width // 2)
        source = grad.at[b, rows] if b < blocks else grad_note.at[rows]
        return pltpu.make_async_copy(source, (send_ref if side else keep_ref).at[:, wide], out_sem.at[2 * b + side])

    def start_ship(b):
        ship(b, 0).start()
        ship(b, 1).start()

    for b in [0, blocks] + list(range(1, blocks)):
        fetch(b).start()
    att = jnp.concatenate([att_ref[t, :, : HG * HD] for t in range(TP)], axis=1)
    row = lax.broadcasted_iota(jnp.int32, (width, width), 0)
    turn[...] = (row == order_ref[0:1]).astype(F32).astype(BF)

    def turned(v):
        return dot_nn(v, turn[...]).astype(BF)

    fetch(0).wait()
    fetch(blocks).wait()
    vec = note[...].astype(F32).T
    gain_one, gain_two, shift_one, shift_two = (vec[i : i + 1] for i in range(2, 6))
    normed_one, inv_one = norm_parts(x_ref[...].astype(F32) + dot_nn(att, w[0]) + vec[0:1])
    mid = normed_one * gain_one + shift_one
    mid_low = mid.astype(BF)
    feed = mid + vec[1:2]
    for k in range(fold):
        fetch(1 + k).wait()
        inner = dot_nn(mid_low, w[1 + k]) + vec[6 + k : 7 + k]
        spread = 0.5 + 0.5 * lax.erf(inner * (0.5**0.5))
        act[k] = (inner * spread).astype(BF)
        slope[k] = spread + inner * (jnp.exp(-0.5 * inner * inner) * 0.3989422804014327)
    for k in range(fold):
        fetch(1 + fold + k).wait()
        feed = feed + dot_nn(act[k], w[1 + fold + k])
    normed_two, inv_two = norm_parts(feed)
    out_ref[...] = (normed_two * gain_two + shift_two).astype(BF)
    grad_out = cot_ref[...].astype(F32)

    def back(incoming, normed, inv_std, gain):
        scaled = incoming * gain
        along = jnp.mean(scaled * normed, axis=1, keepdims=True)
        return inv_std * (scaled - jnp.mean(scaled, axis=1, keepdims=True) - normed * along)

    def total(v):
        return jnp.sum(v, axis=0, keepdims=True)

    dsecond = back(grad_out, normed_two, inv_two, gain_two)
    dfeed = dsecond.astype(BF)
    sums = [None, total(dfeed.astype(F32)), None, total(grad_out * normed_two), None, total(grad_out)]
    dmid = dsecond
    mid_turned = turned(mid_low)
    for k in range(fold):
        dinner = (dot_nt(dfeed, w[1 + fold + k]) * slope[k]).astype(BF)
        sums.append(total(dinner.astype(F32)))
        grad[k] = dot_tn(mid_turned, dinner).astype(BF)
        start_ship(k)
        grad[fold + k] = dot_tn(turned(act[k]), dfeed).astype(BF)
        start_ship(fold + k)
        dmid = dmid + dot_nt(dinner, w[1 + k])
    dsum = back(dmid, normed_one, inv_one, gain_one)
    dsum_ref[...] = dsum
    dproj = dsum.astype(BF)
    sums[0], sums[2], sums[4] = total(dproj.astype(F32)), total(dmid * normed_one), total(dmid)
    datt = dot_nt(dproj, w[0]).astype(BF)
    product = datt.astype(F32) * att.astype(F32)
    high = product.astype(BF)
    rest = (product - high.astype(F32)).astype(BF)
    feature = lax.broadcasted_iota(jnp.int32, (width, 128), 0)
    lane = lanes_like((width, 128))
    third = lanes_like((tokens, HD)) % 3
    for t in range(TP):
        of_head = ((feature // HD == t * HG + lane // 3) & (lane < 3 * HG)).astype(F32).astype(BF)
        delta = (dot_nn(high, of_head) + dot_nn(rest, of_head))[:, :HD]
        one, two, three = (v.astype(F32) for v in split_three(delta))
        notes = jnp.where(third == 0, one, jnp.where(third == 1, two, three))
        load_ref[t, :, : HG * HD] = datt[:, t * HG * HD : (t + 1) * HG * HD]
        load_ref[t, :, HG * HD :] = (notes + att_ref[t, :, HG * HD :].astype(F32)).astype(BF)
    grad[2 * fold] = dot_tn(turned(att), dproj).astype(BF)
    start_ship(2 * fold)
    table = jnp.concatenate(sums + [jnp.zeros((128 - len(sums), width), F32)], axis=0)
    grad_note[...] = dot_nn(table.astype(BF), turn[...]).T.astype(BF)
    start_ship(blocks)
    for b in range(blocks + 1):
        ship(b, 0).wait()
        ship(b, 1).wait()


def dense_layers(att, x, cotangent, order, dense, fold):
    tokens, width = x.shape
    blocks = 2 * fold + 1
    local = pl.BlockSpec(memory_space=pltpu.VMEM)
    anywhere = pl.BlockSpec(memory_space=pl.ANY)
    return pl.pallas_call(
        functools.partial(dense_kernel, fold),
        in_specs=[local, local, local, local, anywhere],
        out_specs=[local, local, local, anywhere, anywhere],
        out_shape=[
            jax.ShapeDtypeStruct((tokens, width), BF),
            jax.ShapeDtypeStruct((TP, tokens, 256), BF),
            jax.ShapeDtypeStruct((tokens, width), F32),
            jax.ShapeDtypeStruct((width // 2, blocks * width + 128), BF),
            jax.ShapeDtypeStruct((width // 2, blocks * width + 128), BF),
        ],
        scratch_shapes=[
            pltpu.VMEM((blocks, width, width), BF),
            pltpu.VMEM((width, 128), BF),
            pltpu.VMEM((blocks, width, width), BF),
            pltpu.VMEM((width, 128), BF),
            pltpu.VMEM((fold, tokens, width), BF),
            pltpu.VMEM((fold, tokens, width), F32),
            pltpu.VMEM((width, width), BF),
            pltpu.SemaphoreType.DMA((blocks + 1,)),
            pltpu.SemaphoreType.DMA((2 * blocks + 2,)),
        ],
        compiler_params=pltpu.CompilerParams(vmem_limit_bytes=VMEM_LIMIT),
        cost_estimate=pl.CostEstimate(flops=54 * tokens * width * width, bytes_accessed=24 << 20, transcendentals=0),
        name="dense_layers",
    )(att, x, cotangent, order, dense)


def tail_kernel(rows, part, spot_ref, dq_ref, dkv_ref, w_ref, *refs):
    pieces, (keep_ref, send_ref, dw_ref) = refs[:8], refs[8:]
    me_y, me_c = spot_ref[1], spot_ref[2]
    lane = lanes_like((1, HG * 128))
    is_own = jnp.zeros((1, HG * 128), jnp.int32)
    for h in range(HG):
        is_own = jnp.where(lane // 128 == h, spot_ref[3 + h], is_own)
    tokens, width = pieces[0].shape
    own_side, oth_side, near_x, far_x = [], [], [], []
    sum_q = sum_kv = 0.0
    for which, out_ref in enumerate((keep_ref, send_ref)):
        core = me_c if which == 0 else 1 - me_c
        middle = [pieces[4 * which + i][...] for i in (1, 2)]
        for y_rel in range(2):
            shard = jnp.bitwise_xor(me_y, y_rel) * 2 + core
            dq = dq_ref[shard].reshape(tokens, HG * HD)
            dkv = dkv_ref[shard].reshape(tokens, HG * 128)
            own = jnp.concatenate([jnp.where(is_own == 1, dkv, 0.0).astype(BF), dq], axis=1)
            oth = jnp.where(is_own == 1, 0.0, dkv).astype(BF)
            sum_q = sum_q + jnp.sum(dq.astype(F32), axis=0, keepdims=True)
            sum_kv = sum_kv + jnp.sum(dkv.astype(BF).astype(F32), axis=0, keepdims=True)
            to_own = dot_nt(own, w_ref[:, : HG * (128 + HD)]).astype(BF)
            to_oth = dot_nt(oth, w_ref[:, : HG * 128]).astype(BF)
            for x_rel, value in enumerate((to_own, to_oth)):
                out_ref[jnp.where(core == 0, x_rel, y_rel), jnp.where(core == 0, y_rel, x_rel)] = value
            own_side.append(own)
            oth_side.append(oth)
            first, last = pieces[4 * which][...], pieces[4 * which + 3][...]
            one = jnp.where(core == 0, middle[0], middle[1])
            two = jnp.where(core == 0, middle[1], middle[0])
            near_x.append(first if y_rel == 0 else two)
            far_x.append(one if y_rel == 0 else last)
    near = dot_tn(jnp.concatenate(near_x, axis=0), jnp.concatenate(own_side, axis=0))
    far = dot_tn(jnp.concatenate(far_x, axis=0), jnp.concatenate(oth_side, axis=0))
    dw_ref[:, : HG * 128] = (near[:, : HG * 128] + far).astype(BF)
    dw_ref[:, HG * 128 : HG * (128 + HD)] = near[:, HG * 128 :].astype(BF)
    values = [sum_q[:, h * HD : (h + 1) * HD] for h in range(HG)]
    values += [sum_kv[:, h * 128 + HD : (h + 1) * 128] for h in range(HG)]
    values = jnp.concatenate(values + [jnp.zeros((128 - 2 * HG, HD), F32)], axis=0).astype(BF)
    inside = lax.broadcasted_iota(jnp.int32, (width, 128), 0) % part
    place = (inside == lanes_like((width, 128))).astype(F32).astype(BF)
    dw_ref[:, HG * (128 + HD) :] = dot_nn(place, values).astype(BF)


def tail(spot, dq, dkv, weight, pieces, part):
    _, seqs, rows, _ = dq.shape
    tokens, width = pieces[0].shape
    local = pl.BlockSpec(memory_space=pltpu.VMEM)
    return pl.pallas_call(
        functools.partial(tail_kernel, rows, part),
        in_specs=[pl.BlockSpec(memory_space=pltpu.SMEM)] + [local] * 11,
        out_specs=[local, local, local],
        out_shape=[
            jax.ShapeDtypeStruct((2, 2, tokens, width), BF),
            jax.ShapeDtypeStruct((2, 2, tokens, width), BF),
            jax.ShapeDtypeStruct((width, 640), BF),
        ],
        compiler_params=pltpu.CompilerParams(vmem_limit_bytes=VMEM_LIMIT),
        cost_estimate=pl.CostEstimate(flops=16 * tokens * width * 480, bytes_accessed=16 << 20, transcendentals=0),
        name="tail",
    )(spot, dq, dkv, weight, *pieces)


def assemble_kernel(got_ref, grad_ref, note_ref):
    width = grad_ref.shape[1] // 3
    for t in range(TP):
        total = got_ref[0, t].astype(F32)
        for i in range(1, got_ref.shape[0]):
            total = total + got_ref[i, t].astype(F32)
        at = t * HG * HD
        grad_ref[:, at : at + HG * HD] = total[:, HG * 128 : HG * (128 + HD)]
        for h in range(HG):
            for j in range(2):
                to = (1 + j) * width + at + h * HD
                grad_ref[:, to : to + HD] = total[:, h * 128 + j * HD : h * 128 + (j + 1) * HD]
        note_ref[t] = total[:, HG * (128 + HD) :]


def assemble(got):
    _, _, part, _ = got.shape
    local = pl.BlockSpec(memory_space=pltpu.VMEM)
    return pl.pallas_call(
        assemble_kernel,
        in_specs=[local],
        out_specs=[local, local],
        out_shape=[
            jax.ShapeDtypeStruct((part, 3 * H * HD), F32),
            jax.ShapeDtypeStruct((TP, part, HD), F32),
        ],
        compiler_params=pltpu.CompilerParams(vmem_limit_bytes=VMEM_LIMIT),
        name="assemble",
    )(got)


def swap_on(axis):
    return lambda v: lax.ppermute(v, axis, [(0, 1), (1, 0)])


def crossing(first):
    pairs = []
    for u in range(2):
        for y in range(2):
            for c in range(2):
                along_u = (c == 0) == first
                to = (1 - u, y, c) if along_u else (u, 1 - y, c)
                pairs.append(((u * 2 + y) * 2 + c, (to[0] * 2 + to[1]) * 2 + to[2]))
    return lambda v: lax.ppermute(v, ("u", "y", "c"), pairs)


def after(v, *earlier):
    return lax.optimization_barrier((v,) + earlier)[0]


def add(a, b):
    return (a.astype(F32) + b.astype(F32)).astype(BF)


def pick(v, index, axis):
    return lax.dynamic_index_in_dim(v, index, axis, keepdims=False)


def put(buffer, v, index):
    return lax.dynamic_update_index_in_dim(buffer, v, index, 0)


def per_device(layer_input, wqkv, wo, wi, wd, biases, hidden_bias, gains, shifts, cotangent, block_ids, offsets, pairing):
    seqs, rows, width = layer_input.shape
    devices = lax.axis_size(ALL)
    ring = lax.axis_size("r")
    shards = ring * TP
    half = shards * rows
    tokens = seqs * rows
    me_u, me_r, me_y, me_c = (lax.axis_index(a) for a in ALL)
    me_t = me_y * 2 + me_c
    part = wqkv.shape[0]
    hidden = wi.shape[1]
    fold = hidden // width
    swap_u, swap_c = swap_on("u"), swap_on("c")
    cross_one, cross_two = crossing(True), crossing(False)
    forward = [(i, (i + 1) % ring) for i in range(ring)]

    notes = [biases[2:].T, gains.T, shifts.T, hidden_bias.reshape(fold, part).T]
    notes = jnp.concatenate(notes + [jnp.zeros((part, 128 - 6 - fold), BF)], axis=1)
    wi_turned = wi.reshape(part, devices, fold, part).transpose(0, 2, 1, 3).reshape(part, hidden)
    wd_cols = [wd[k * part : (k + 1) * part] for k in range(fold)]
    dense = lax.all_gather(jnp.concatenate([wo, wi_turned] + wd_cols + [notes], axis=1), ALL, axis=0, tiled=True)

    by_head = wqkv.reshape(part, 3, TP, HG, HD)
    blocks_kv = by_head[:, 1:].transpose(2, 0, 3, 1, 4).reshape(TP, part, HG * 128)
    blocks_q = by_head[:, 0].transpose(1, 0, 2, 3).reshape(TP, part, HG * HD)
    ends = jnp.pad(biases[:2].T, ((0, 0), (0, HD - 2)))
    blocks = jnp.concatenate([blocks_kv, blocks_q, jnp.broadcast_to(ends, (TP, part, HD))], axis=2)
    blocks = lax.all_to_all(blocks, ("y", "c"), split_axis=0, concat_axis=0, tiled=True)
    column = put(jnp.zeros((ring,) + blocks.shape, BF), blocks, me_r)
    for k in range(1, ring):
        got = lax.ppermute(blocks, "r", [(i, (i + k) % ring) for i in range(ring)])
        column = put(column, got, (me_r - k) % ring)
    both = jnp.zeros((2,) + column.shape, BF)
    w_here = put(put(both, column, me_u), swap_u(column), 1 - me_u).reshape(width, 640)
    b_heads = w_here[:, 576:578].astype(F32)
    b_heads = lax.dynamic_slice_in_dim(b_heads, me_t * HG * HD, HG * HD, 0).T
    b_kv = jnp.concatenate([jnp.zeros((HG, HD), F32), b_heads[1].reshape(HG, HD)], axis=1).reshape(-1)
    b_here = jnp.concatenate([b_kv, b_heads[0], jnp.zeros((HD,), F32)])
    b_here = jnp.broadcast_to(b_here, (8, 640))

    x_own = layer_input.reshape(tokens, width)
    piece = x_own
    stages = []
    for k in range(ring):
        if k == 1:
            piece, column = lax.optimization_barrier((piece, column))
        if k:
            piece = lax.ppermute(piece, "r", forward)
        if k >= 2:
            piece, stages[k - 2] = lax.optimization_barrier((piece, stages[k - 2]))
        one = cross_one(piece)
        two = cross_two(piece)
        if k == 1:
            one, w_here = lax.optimization_barrier((one, w_here))
        three = cross_two(one)
        if k >= 2:
            three, stages[k - 1] = lax.optimization_barrier((three, stages[k - 1]))
        mine = [piece, one, two, three]
        theirs = [swap_c(m) for m in mine]
        if k == 0:
            x_near = (mine, theirs)
        spot = jnp.stack([me_u, me_y, me_c, (me_r - k) % ring]).astype(jnp.int32)
        stages.append(project(mine + theirs, w_here, b_here, spot, stages[-1] if stages else None, ring, seqs, rows))
    buffers = stages[-1]
    kv = buffers[0].reshape(2, shards, seqs, rows, HG * 128)
    q_all = buffers[1].reshape(shards, seqs, rows, HG * 128)
    q_loc = lax.dynamic_slice_in_dim(q_all, me_r * TP, TP, 0)

    pair = lax.dynamic_slice_in_dim(pick(pairing, me_u, 1), me_t * HG, HG, 0)
    ids = block_ids.reshape(seqs, 2, half)
    ids_own = pick(ids, me_u, 1)
    ends = jnp.sum((ids[:, :, None, :] <= ids_own[:, None, :, None]).astype(jnp.int32), axis=-1)
    end_all = jnp.where((pair == 0)[None, :, None], ends[:, 0:1], ends[:, 1:2])
    end_loc = lax.dynamic_slice_in_dim(end_all, me_r * TP * rows, TP * rows, 2)
    begin = jnp.maximum(offsets[:, None] - pair[None, :] * half, 0).reshape(-1)
    last = end_loc[:, :, -1].reshape(-1)
    start = me_r * TP * rows
    end_ring = end_all.reshape(seqs, HG, ring, TP * rows)
    end_row_own = end_loc[:, :, None]

    att = attend_forward(q_loc, kv, pair, begin, last, end_row_own)
    att = lax.all_to_all(att, ("y", "c"), split_axis=0, concat_axis=0, tiled=True).reshape(TP, tokens, 256)

    index = jnp.arange(width, dtype=jnp.int32)
    inner_at, index = index % part, index // part
    r_rel, index = index % ring, index // ring
    s_rel, f_rel, c_rel = index % 2, index // 2 % 2, index // 4
    core = me_c ^ c_rel
    to_u = me_u ^ jnp.where(core == 0, f_rel, s_rel)
    to_y = me_y ^ jnp.where(core == 0, s_rel, f_rel)
    order = (((to_u * ring + (me_r + r_rel) % ring) * 2 + to_y) * 2 + core) * part + inner_at
    order = jnp.broadcast_to(order.astype(jnp.int32), (8, width))
    hidden_out, load, dsum, stay, leave = dense_layers(att, x_own, cotangent.reshape(tokens, width), order, dense, fold)
    hidden_out = hidden_out.reshape(seqs, rows, width)
    came = swap_c(leave)
    cut = width // 4
    high, low = add(stay[cut:], came[cut:]), add(stay[:cut], came[:cut])
    high_first = high
    cut = width // 8
    load = load.reshape(TP, seqs, rows, 256)
    load = lax.all_to_all(load, ("y", "c"), split_axis=0, concat_axis=0, tiled=True)
    came = cross_one(after(high_first, load))
    place = jnp.stack([start, me_r])
    dkv = jnp.zeros((TP, seqs, rows, HG * 128), F32)
    moving = load
    done = []
    for k in range(ring):
        if k >= 2:
            moving, done[k - 2] = lax.optimization_barrier((moving, done[k - 2]))
        if k == 2:
            moving, dq = lax.optimization_barrier((moving, dq))
        if k:
            moving = lax.ppermute(moving, "r", forward)
        source = (me_r - k) % ring
        ends_k = pick(end_ring, source, 2)
        where = jnp.concatenate([place, source[None]]).astype(jnp.int32)
        before = done[-1] if done else dkv
        if k == ring - 2:
            high2, low2 = add(low[cut:], came[cut:]), add(low[:cut], came[:cut])
            stay = add(low2, cross_two(high2))
            before = after(before, high2)
        done.append(attend_key(q_all, moving, kv, pair, begin, ends_k[:, :, -1].reshape(-1), where, ends_k[:, :, None], before))
        if k == 0:
            dq = attend_query(q_loc, kv, pair, begin, last, end_row_own, after(load, high))

    summed = stay[:part].astype(F32)
    for j in range(1, ring):
        along = [(i, (i + j) % ring) for i in range(ring)]
        summed = summed + lax.ppermute(stay[j * part : (j + 1) * part], "r", along).astype(F32)
    grad_w_in = summed[:, :hidden].reshape(part, fold, devices, part).transpose(0, 2, 1, 3).reshape(part, hidden)
    grad_w_down = jnp.concatenate([summed[:, hidden + k * width : hidden + (k + 1) * width] for k in range(fold)], axis=0)
    grad_w_out = summed[:, 2 * hidden : 2 * hidden + width]
    flat = summed[:, 2 * hidden + width : 2 * hidden + width + 6 + fold].T
    grad_bo, grad_gains, grad_shifts, grad_bin = flat[0:2], flat[2:4], flat[4:6], flat[6:].reshape(-1)


    spot = jnp.concatenate([jnp.stack([me_u, me_y, me_c]), (pair == me_u).astype(jnp.int32)])
    keep, send, dw = tail(spot.astype(jnp.int32), dq, done[-1], w_here, x_near[0] + x_near[1], part)
    keep = add(keep, swap_c(send))
    dw = after(dw, keep)
    got = lax.all_to_all(dw.reshape(devices, part, 640), ALL, split_axis=0, concat_axis=0, tiled=True)
    came = cross_one(keep[1])
    final = cross_two(add(keep[0, 1], came[1]))
    grad_input = dsum + keep[0, 0].astype(F32) + came[0].astype(F32) + final.astype(F32)
    grad_input = grad_input.astype(BF).reshape(seqs, rows, width)
    grad_w_qkv, note = assemble(after(got, final).reshape(2 * ring, TP, part, 640))
    at = lax.axis_index(ALL) * part
    grad_bq = lax.dynamic_slice_in_dim(note[:, :HG].reshape(width), at, part, 0)
    grad_bv = lax.dynamic_slice_in_dim(note[:, HG : 2 * HG].reshape(width), at, part, 0)
    grad_biases = jnp.concatenate([jnp.stack([grad_bq, grad_bv]), grad_bo])
    return (hidden_out, grad_input, grad_w_qkv, grad_w_out, grad_w_in, grad_w_down, grad_biases, grad_bin, grad_gains, grad_shifts)


def solution(mesh):
    wide = mesh.shape["blk"]
    grid = Mesh(mesh.devices.reshape(2, wide // TP, 2, TP // 2), ALL)
    rows2, cols1 = P(ALL, None), P(None, ALL)
    toks = P(None, ALL, None)
    return jax.shard_map(
        per_device,
        mesh=grid,
        in_specs=(toks, rows2, rows2, rows2, rows2, cols1, P(ALL), cols1, cols1, toks, P(), P(), P()),
        out_specs=(toks, toks, rows2, rows2, rows2, rows2, cols1, P(ALL), cols1, cols1),
        check_vma=False,
    )
```

```python
import functools

import jax
import jax.numpy as jnp
from jax import lax
from jax.experimental import pallas as pl
from jax.experimental.pallas import tpu as pltpu
from jax.sharding import Mesh
from jax.sharding import PartitionSpec as P

H = 12
HD = 64
TP = 4
HG = H // TP
NORM_EPS = 1e-12
FILL = -1e30
FLOOR = -1e29
ALL = ("u", "r", "y", "c")
BF = jnp.bfloat16
F32 = jnp.float32
VMEM_LIMIT = 56 * 1024 * 1024


def split_three(v):
    high = v.astype(BF)
    v = v - high.astype(F32)
    middle = v.astype(BF)
    return high, middle, (v - middle.astype(F32)).astype(BF)


def dot_nt(a, b):
    return lax.dot_general(a, b, (((1,), (1,)), ((), ())), preferred_element_type=F32)


def dot_nn(a, b):
    return lax.dot_general(a, b, (((1,), (0,)), ((), ())), preferred_element_type=F32)


def dot_tn(a, b):
    return lax.dot_general(a, b, (((0,), (0,)), ((), ())), preferred_element_type=F32)


def lanes_like(shape):
    return lax.broadcasted_iota(jnp.int32, shape, len(shape) - 1)


def chooser(h, kind, depth):
    at = HD + kind * 3 * HG + 3 * h
    lane = lanes_like((depth, 128))
    return jnp.where((lane >= at) & (lane < at + 3), -1.0, 0.0).astype(BF)


def chunk_of(shards):
    return 16 if shards % 16 == 0 else shards


def key_spots(first, count, begin, end_row):
    spot = lax.broadcasted_iota(jnp.int32, (count, 1), 0) + first
    return jnp.where(spot >= begin, spot, 1 << 30) < end_row


def forward_kernel(rows, shards, pair_ref, begin_ref, last_ref, q_ref, kv0, kv1, kv2, end_ref, att_ref, m_ref, l_ref, acc_ref):
    seq = pl.program_id(0)
    group = chunk_of(shards)
    nq = TP * rows
    width = group * rows
    for h in range(HG):
        m_ref[h] = jnp.full((1, nq), FLOOR, F32)
        l_ref[h] = jnp.zeros((1, nq), F32)
        acc_ref[h] = jnp.zeros((128, nq), F32)

    def step(c, _):
        for h, kv_ref in enumerate((kv0, kv1, kv2)):
            query = q_ref[:, 0, :, h * 128 : (h + 1) * 128].reshape(nq, 128)
            kv = kv_ref[0, pl.ds(c * group, group), 0].reshape(width, 128)
            seen = key_spots(c * width, width, begin_ref[seq * HG + h], end_ref[0, h])
            scores = jnp.where(seen, dot_nt(kv, query), FILL)
            old = m_ref[h]
            new = jnp.maximum(old, jnp.max(scores, axis=0, keepdims=True))
            weights = jnp.exp(scores - new)
            factor = jnp.exp(old - new)
            m_ref[h] = new
            l_ref[h] = l_ref[h] * factor + jnp.sum(weights, axis=0, keepdims=True)
            acc_ref[h] = acc_ref[h] * factor + dot_tn(kv, weights.astype(BF))
        return 0

    trips = [pl.cdiv(last_ref[seq * HG + h], width) for h in range(HG)]
    lax.fori_loop(0, functools.reduce(jnp.maximum, trips), step, 0)
    turn = lax.broadcasted_iota(jnp.int32, (HD, nq), 0)
    notes = jnp.zeros((HD, nq), F32)
    for h in range(HG):
        total = jnp.maximum(l_ref[h], 1.0)
        for p, value in enumerate(split_three(m_ref[h] + jnp.log(total))):
            notes = jnp.where(turn == 3 * HG + 3 * h + p, value.astype(F32), notes)
        att = (acc_ref[h] / total)[HD:].T.astype(BF)
        att_ref[:, 0, :, h * HD : (h + 1) * HD] = att.reshape(TP, rows, HD)
    att_ref[:, 0, :, HG * HD :] = notes.T.astype(BF).reshape(TP, rows, HD)


def output_gradient(load_ref, h, count):
    dout = load_ref[:, 0, :, h * HD : (h + 1) * HD].reshape(count, HD)
    return jnp.concatenate([jnp.zeros_like(dout), dout], axis=1)


def query_kernel(rows, shards, pair_ref, begin_ref, last_ref, q_ref, kv0, kv1, kv2, end_ref, load_ref, dq_ref, acc_ref):
    seq = pl.program_id(0)
    group = chunk_of(shards)
    nq = TP * rows
    width = group * rows
    notes = load_ref[:, 0, :, 128:].reshape(nq, 128)
    acc_ref[...] = jnp.zeros_like(acc_ref)

    def step(c, _):
        for h, kv_ref in enumerate((kv0, kv1, kv2)):
            query = q_ref[:, 0, :, h * 128 : (h + 1) * 128].reshape(nq, 128)
            kv = kv_ref[0, pl.ds(c * group, group), 0].reshape(width, 128)
            seen = key_spots(c * width, width, begin_ref[seq * HG + h], end_ref[0, h])
            query = jnp.concatenate([query, notes], axis=1)
            dout = jnp.concatenate([output_gradient(load_ref, h, nq), notes], axis=1)
            scores = dot_nt(jnp.concatenate([kv, chooser(h, 1, width)], axis=1), query)
            prob = jnp.exp(jnp.where(seen, scores, FILL))
            dprob = dot_nt(jnp.concatenate([kv, chooser(h, 0, width)], axis=1), dout)
            acc_ref[h] += dot_tn(kv, (prob * dprob).astype(BF))
        return 0

    trips = [pl.cdiv(last_ref[seq * HG + h], width) for h in range(HG)]
    lax.fori_loop(0, functools.reduce(jnp.maximum, trips), step, 0)
    for h in range(HG):
        dq = (acc_ref[h][:HD] * (HD**-0.5)).T.astype(BF)
        dq_ref[:, 0, :, h * HD : (h + 1) * HD] = dq.reshape(TP, rows, HD)


def key_kernel(rows, pair_ref, begin_ref, reach_ref, place_ref, q_ref, load_ref, kv0, kv1, kv2, end_ref, old_ref, dkv_ref):
    seq = pl.program_id(0)
    span = TP * rows
    start = place_ref[0]
    reach = [reach_ref[seq * HG + h] for h in range(HG)]
    needed = functools.reduce(jnp.maximum, reach) > start

    @pl.when(needed)
    def _():
        notes = load_ref[:, 0, :, 128:].reshape(span, 128)
        for h, kv_ref in enumerate((kv0, kv1, kv2)):
            lanes = slice(h * 128, (h + 1) * 128)
            kv = kv_ref[0, :, 0].reshape(span, 128)
            query = q_ref[:, 0, :, lanes].reshape(span, 128)
            dout = output_gradient(load_ref, h, span)
            seen = key_spots(start, span, begin_ref[seq * HG + h], end_ref[0, h])
            scores = dot_nt(jnp.concatenate([kv, chooser(h, 1, span)], axis=1), jnp.concatenate([query, notes], axis=1))
            prob = jnp.exp(jnp.where(seen, scores, FILL))
            dprob = dot_nt(jnp.concatenate([kv, chooser(h, 0, span)], axis=1), jnp.concatenate([dout, notes], axis=1))
            sides = jnp.concatenate([(prob * dprob).astype(BF), prob.astype(BF)], axis=1)
            new = dot_nn(sides, jnp.concatenate([query, dout], axis=0))
            dkv_ref[:, 0, :, lanes] = old_ref[:, 0, :, lanes] + new.reshape(TP, rows, 128)

    @pl.when(jnp.logical_not(needed))
    def _():
        dkv_ref[...] = old_ref[...]


def project_kernel(seqs, rows, fresh, spot_ref, *refs):
    pieces, w_ref, bias_ref = refs[:8], refs[8], refs[9]
    kv_out, q_out, kv_tmp, q_tmp, kv_sem, q_sem = refs[10 if fresh else 12 :]
    keys = HG * 128
    tokens = seqs * rows
    me_u, me_y, me_c, source = (spot_ref[i] for i in range(4))
    for which in range(2):
        core = me_c if which == 0 else 1 - me_c
        x = jnp.concatenate([pieces[which * 4 + i][...] for i in range(4)], axis=0)
        if which == 0:
            q_tmp[...] = jnp.zeros_like(q_tmp)
        kv = (dot_nn(x, w_ref[:, :keys]) + bias_ref[0:1, :keys]).astype(BF)
        for i in range(4):
            p, q = i // 2, i % 2
            x_rel = jnp.where(core == 0, q, p)
            y_rel = jnp.where(core == 0, p, q)
            shard = jnp.bitwise_xor(me_y, y_rel) * 2 + core
            slot = which * 4 + i
            kv_tmp[slot] = kv[i * tokens : (i + 1) * tokens].reshape(seqs, rows, keys)
            spot = kv_out.at[jnp.bitwise_xor(me_u, x_rel), source, shard]
            pltpu.make_async_copy(kv_tmp.at[slot], spot, kv_sem.at[slot]).start()
        second = jnp.where(core == 0, x[2 * tokens : 3 * tokens], x[tokens : 2 * tokens])
        for y_rel, part in enumerate((x[:tokens], second)):
            query = (dot_nn(part, w_ref[:, keys:]) + bias_ref[0:1, keys:]) * (HD**-0.5)
            slot = which * 2 + y_rel
            query = query.astype(BF)
            for h in range(HG):
                q_tmp[slot, :, :, h * 128 : h * 128 + HD] = query[:, h * HD : (h + 1) * HD].reshape(seqs, rows, HD)
            shard = jnp.bitwise_xor(me_y, y_rel) * 2 + core
            pltpu.make_async_copy(q_tmp.at[slot], q_out.at[source, shard], q_sem.at[slot]).start()
    for slot in range(8):
        pltpu.make_async_copy(kv_tmp.at[slot], kv_out.at[0, 0, 0], kv_sem.at[slot]).wait()
    for slot in range(4):
        pltpu.make_async_copy(q_tmp.at[slot], q_out.at[0, 0], q_sem.at[slot]).wait()


def project(pieces, weight, bias, spot, buffers, ring, seqs, rows):
    keys = HG * 128
    width = weight.shape[0]
    tokens = seqs * rows
    extra = [] if buffers is None else list(buffers)
    anywhere = pl.BlockSpec(memory_space=pl.ANY)
    local = pl.BlockSpec(memory_space=pltpu.VMEM)
    return pl.pallas_call(
        functools.partial(project_kernel, seqs, rows, not extra),
        in_specs=[pl.BlockSpec(memory_space=pltpu.SMEM)] + [local] * 10 + [anywhere] * len(extra),
        out_specs=[anywhere, anywhere],
        scratch_shapes=[
            pltpu.VMEM((8, seqs, rows, keys), BF),
            pltpu.VMEM((4, seqs, rows, keys), BF),
            pltpu.SemaphoreType.DMA((8,)),
            pltpu.SemaphoreType.DMA((4,)),
        ],
        out_shape=[
            jax.ShapeDtypeStruct((2, ring, TP, seqs, rows, keys), BF),
            jax.ShapeDtypeStruct((ring, TP, seqs, rows, keys), BF),
        ],
        input_output_aliases={11: 0, 12: 1} if extra else {},
        compiler_params=pltpu.CompilerParams(vmem_limit_bytes=VMEM_LIMIT),
        cost_estimate=pl.CostEstimate(flops=12 * tokens * width * keys * 2, bytes_accessed=12 << 20, transcendentals=0),
        name="project",
    )(spot, *pieces, weight, bias, *extra)


def keys_spec(h, shards, rows):
    return pl.BlockSpec((1, shards, 1, rows, 128), lambda s, pair, *_: (pair[h], 0, s, 0, h))


def attend_forward(q_loc, kv, pair, begin, last, end_row_own):
    _, shards, seqs, rows, _ = kv.shape
    nq = TP * rows
    row_spec = pl.BlockSpec((TP, 1, rows, 384), lambda s, *_: (0, s, 0, 0))
    end_spec = pl.BlockSpec((1, HG, 1, nq), lambda s, *_: (s, 0, 0, 0))
    return pl.pallas_call(
        functools.partial(forward_kernel, rows, shards),
        grid_spec=pltpu.PrefetchScalarGridSpec(
            num_scalar_prefetch=3,
            grid=(seqs,),
            in_specs=[row_spec] + [keys_spec(h, shards, rows) for h in range(HG)] + [end_spec],
            out_specs=pl.BlockSpec((TP, 1, rows, 256), lambda s, *_: (0, s, 0, 0)),
            scratch_shapes=[pltpu.VMEM((HG, 1, nq), F32), pltpu.VMEM((HG, 1, nq), F32), pltpu.VMEM((HG, 128, nq), F32)],
        ),
        out_shape=jax.ShapeDtypeStruct((TP, seqs, rows, 256), BF),
        compiler_params=pltpu.CompilerParams(vmem_limit_bytes=VMEM_LIMIT),
        cost_estimate=pl.CostEstimate(flops=4 * 9 * nq * shards * rows * 128, bytes_accessed=12 << 20, transcendentals=0),
        name="attend_forward",
    )(pair, begin, last, q_loc, kv, kv, kv, end_row_own)


def attend_query(q_loc, kv, pair, begin, last, end_row_own, load):
    _, shards, seqs, rows, _ = kv.shape
    nq = TP * rows
    row_spec = pl.BlockSpec((TP, 1, rows, 384), lambda s, *_: (0, s, 0, 0))
    end_spec = pl.BlockSpec((1, HG, 1, nq), lambda s, *_: (s, 0, 0, 0))
    return pl.pallas_call(
        functools.partial(query_kernel, rows, shards),
        grid_spec=pltpu.PrefetchScalarGridSpec(
            num_scalar_prefetch=3,
            grid=(seqs,),
            in_specs=[row_spec]
            + [keys_spec(h, shards, rows) for h in range(HG)]
            + [end_spec, pl.BlockSpec((TP, 1, rows, 256), lambda s, *_: (0, s, 0, 0))],
            out_specs=pl.BlockSpec((TP, 1, rows, HG * HD), lambda s, *_: (0, s, 0, 0)),
            scratch_shapes=[pltpu.VMEM((HG, 128, nq), F32)],
        ),
        out_shape=jax.ShapeDtypeStruct((TP, seqs, rows, HG * HD), BF),
        compiler_params=pltpu.CompilerParams(vmem_limit_bytes=VMEM_LIMIT),
        cost_estimate=pl.CostEstimate(flops=6 * 9 * nq * shards * rows * 128, bytes_accessed=12 << 20, transcendentals=0),
        name="attend_query",
    )(pair, begin, last, q_loc, kv, kv, kv, end_row_own, load)


def attend_key(q_all, load, kv, pair, begin, reach, place, end_row, old):
    _, shards, seqs, rows, _ = kv.shape

    def own_keys(h):
        return pl.BlockSpec((1, TP, 1, rows, 128), lambda s, pair, begin, reach, place: (pair[h], place[1], s, 0, h))

    total = pl.BlockSpec((TP, 1, rows, 384), lambda s, *_: (0, s, 0, 0))
    return pl.pallas_call(
        functools.partial(key_kernel, rows),
        grid_spec=pltpu.PrefetchScalarGridSpec(
            num_scalar_prefetch=4,
            grid=(seqs,),
            in_specs=[
                pl.BlockSpec((TP, 1, rows, 384), lambda s, pair, begin, reach, place: (place[2], s, 0, 0)),
                pl.BlockSpec((TP, 1, rows, 256), lambda s, *_: (0, s, 0, 0)),
            ]
            + [own_keys(h) for h in range(HG)]
            + [pl.BlockSpec((1, HG, 1, TP * rows), lambda s, *_: (s, 0, 0, 0)), total],
            out_specs=total,
        ),
        out_shape=jax.ShapeDtypeStruct((TP, seqs, rows, 384), F32),
        input_output_aliases={10: 0},
        compiler_params=pltpu.CompilerParams(vmem_limit_bytes=VMEM_LIMIT),
        cost_estimate=pl.CostEstimate(flops=8 * 9 * (TP * rows) ** 2 * 128, bytes_accessed=8 << 20, transcendentals=0),
        name="attend_key",
    )(pair, begin, reach, place, q_all, load, kv, kv, kv, end_row, old)


def norm_parts(summed):
    centred = summed - jnp.mean(summed, axis=1, keepdims=True)
    inv_std = lax.rsqrt(jnp.mean(centred * centred, axis=1, keepdims=True) + NORM_EPS)
    return centred * inv_std, inv_std


def dense_kernel(fold, att_ref, x_ref, cot_ref, order_ref, dense_ref, out_ref, load_ref, dsum_ref, keep_ref, send_ref, w, note, grad, grad_note, act, slope, turn, in_sem, out_sem):
    tokens, width = x_ref.shape
    blocks = 2 * fold + 1

    def fetch(b):
        wide = pl.ds(b * width, width) if b < blocks else pl.ds(blocks * width, 128)
        return pltpu.make_async_copy(dense_ref.at[:, wide], w.at[b] if b < blocks else note, in_sem.at[b])

    def ship(b, side):
        wide = pl.ds(b * width, width) if b < blocks else pl.ds(blocks * width, 128)
        rows = pl.ds(side * (width // 2), width // 2)
        source = grad.at[b, rows] if b < blocks else grad_note.at[rows]
        return pltpu.make_async_copy(source, (send_ref if side else keep_ref).at[:, wide], out_sem.at[2 * b + side])

    def start_ship(b):
        ship(b, 0).start()
        ship(b, 1).start()

    for b in [0, blocks] + list(range(1, blocks)):
        fetch(b).start()
    att = jnp.concatenate([att_ref[t, :, : HG * HD] for t in range(TP)], axis=1)
    row = lax.broadcasted_iota(jnp.int32, (width, width), 0)
    turn[...] = (row == order_ref[0:1]).astype(F32).astype(BF)

    def turned(v):
        return dot_nn(v, turn[...]).astype(BF)

    fetch(0).wait()
    fetch(blocks).wait()
    vec = note[...].astype(F32).T
    gain_one, gain_two, shift_one, shift_two = (vec[i : i + 1] for i in range(2, 6))
    normed_one, inv_one = norm_parts(x_ref[...].astype(F32) + dot_nn(att, w[0]) + vec[0:1])
    mid = normed_one * gain_one + shift_one
    mid_low = mid.astype(BF)
    feed = mid + vec[1:2]
    for k in range(fold):
        fetch(1 + k).wait()
        inner = dot_nn(mid_low, w[1 + k]) + vec[6 + k : 7 + k]
        spread = 0.5 + 0.5 * lax.erf(inner * (0.5**0.5))
        act[k] = (inner * spread).astype(BF)
        slope[k] = spread + inner * (jnp.exp(-0.5 * inner * inner) * 0.3989422804014327)
    for k in range(fold):
        fetch(1 + fold + k).wait()
        feed = feed + dot_nn(act[k], w[1 + fold + k])
    normed_two, inv_two = norm_parts(feed)
    out_ref[...] = (normed_two * gain_two + shift_two).astype(BF)
    grad_out = cot_ref[...].astype(F32)

    def back(incoming, normed, inv_std, gain):
        scaled = incoming * gain
        along = jnp.mean(scaled * normed, axis=1, keepdims=True)
        return inv_std * (scaled - jnp.mean(scaled, axis=1, keepdims=True) - normed * along)

    def total(v):
        return jnp.sum(v, axis=0, keepdims=True)

    dsecond = back(grad_out, normed_two, inv_two, gain_two)
    dfeed = dsecond.astype(BF)
    sums = [None, total(dfeed.astype(F32)), None, total(grad_out * normed_two), None, total(grad_out)]
    dmid = dsecond
    mid_turned = turned(mid_low)
    for k in range(fold):
        dinner = (dot_nt(dfeed, w[1 + fold + k]) * slope[k]).astype(BF)
        sums.append(total(dinner.astype(F32)))
        grad[k] = dot_tn(mid_turned, dinner).astype(BF)
        start_ship(k)
        grad[fold + k] = dot_tn(turned(act[k]), dfeed).astype(BF)
        start_ship(fold + k)
        dmid = dmid + dot_nt(dinner, w[1 + k])
    dsum = back(dmid, normed_one, inv_one, gain_one)
    dsum_ref[...] = dsum
    dproj = dsum.astype(BF)
    sums[0], sums[2], sums[4] = total(dproj.astype(F32)), total(dmid * normed_one), total(dmid)
    datt = dot_nt(dproj, w[0]).astype(BF)
    product = datt.astype(F32) * att.astype(F32)
    high = product.astype(BF)
    rest = (product - high.astype(F32)).astype(BF)
    feature = lax.broadcasted_iota(jnp.int32, (width, 128), 0)
    lane = lanes_like((width, 128))
    third = lanes_like((tokens, HD)) % 3
    for t in range(TP):
        of_head = ((feature // HD == t * HG + lane // 3) & (lane < 3 * HG)).astype(F32).astype(BF)
        delta = (dot_nn(high, of_head) + dot_nn(rest, of_head))[:, :HD]
        one, two, three = (v.astype(F32) for v in split_three(delta))
        notes = jnp.where(third == 0, one, jnp.where(third == 1, two, three))
        load_ref[t, :, : HG * HD] = datt[:, t * HG * HD : (t + 1) * HG * HD]
        load_ref[t, :, HG * HD :] = (notes + att_ref[t, :, HG * HD :].astype(F32)).astype(BF)
    grad[2 * fold] = dot_tn(turned(att), dproj).astype(BF)
    start_ship(2 * fold)
    table = jnp.concatenate(sums + [jnp.zeros((128 - len(sums), width), F32)], axis=0)
    grad_note[...] = dot_nn(table.astype(BF), turn[...]).T.astype(BF)
    start_ship(blocks)
    for b in range(blocks + 1):
        ship(b, 0).wait()
        ship(b, 1).wait()


def dense_layers(att, x, cotangent, order, dense, fold):
    tokens, width = x.shape
    blocks = 2 * fold + 1
    local = pl.BlockSpec(memory_space=pltpu.VMEM)
    anywhere = pl.BlockSpec(memory_space=pl.ANY)
    return pl.pallas_call(
        functools.partial(dense_kernel, fold),
        in_specs=[local, local, local, local, anywhere],
        out_specs=[local, local, local, anywhere, anywhere],
        out_shape=[
            jax.ShapeDtypeStruct((tokens, width), BF),
            jax.ShapeDtypeStruct((TP, tokens, 256), BF),
            jax.ShapeDtypeStruct((tokens, width), F32),
            jax.ShapeDtypeStruct((width // 2, blocks * width + 128), BF),
            jax.ShapeDtypeStruct((width // 2, blocks * width + 128), BF),
        ],
        scratch_shapes=[
            pltpu.VMEM((blocks, width, width), BF),
            pltpu.VMEM((width, 128), BF),
            pltpu.VMEM((blocks, width, width), BF),
            pltpu.VMEM((width, 128), BF),
            pltpu.VMEM((fold, tokens, width), BF),
            pltpu.VMEM((fold, tokens, width), F32),
            pltpu.VMEM((width, width), BF),
            pltpu.SemaphoreType.DMA((blocks + 1,)),
            pltpu.SemaphoreType.DMA((2 * blocks + 2,)),
        ],
        compiler_params=pltpu.CompilerParams(vmem_limit_bytes=VMEM_LIMIT),
        cost_estimate=pl.CostEstimate(flops=54 * tokens * width * width, bytes_accessed=24 << 20, transcendentals=0),
        name="dense_layers",
    )(att, x, cotangent, order, dense)


def tail_kernel(rows, part, spot_ref, dq_ref, dkv_ref, w_ref, *refs):
    pieces, (keep_ref, send_ref, dw_ref) = refs[:8], refs[8:]
    me_y, me_c = spot_ref[1], spot_ref[2]
    lane = lanes_like((1, HG * 128))
    is_own = jnp.zeros((1, HG * 128), jnp.int32)
    for h in range(HG):
        is_own = jnp.where(lane // 128 == h, spot_ref[3 + h], is_own)
    tokens, width = pieces[0].shape
    own_side, oth_side, near_x, far_x = [], [], [], []
    sum_q = sum_kv = 0.0
    for which, out_ref in enumerate((keep_ref, send_ref)):
        core = me_c if which == 0 else 1 - me_c
        middle = [pieces[4 * which + i][...] for i in (1, 2)]
        for y_rel in range(2):
            shard = jnp.bitwise_xor(me_y, y_rel) * 2 + core
            dq = dq_ref[shard].reshape(tokens, HG * HD)
            dkv = dkv_ref[shard].reshape(tokens, HG * 128)
            own = jnp.concatenate([jnp.where(is_own == 1, dkv, 0.0).astype(BF), dq], axis=1)
            oth = jnp.where(is_own == 1, 0.0, dkv).astype(BF)
            sum_q = sum_q + jnp.sum(dq.astype(F32), axis=0, keepdims=True)
            sum_kv = sum_kv + jnp.sum(dkv.astype(BF).astype(F32), axis=0, keepdims=True)
            to_own = dot_nt(own, w_ref[:, : HG * (128 + HD)]).astype(BF)
            to_oth = dot_nt(oth, w_ref[:, : HG * 128]).astype(BF)
            for x_rel, value in enumerate((to_own, to_oth)):
                out_ref[jnp.where(core == 0, x_rel, y_rel), jnp.where(core == 0, y_rel, x_rel)] = value
            own_side.append(own)
            oth_side.append(oth)
            first, last = pieces[4 * which][...], pieces[4 * which + 3][...]
            one = jnp.where(core == 0, middle[0], middle[1])
            two = jnp.where(core == 0, middle[1], middle[0])
            near_x.append(first if y_rel == 0 else two)
            far_x.append(one if y_rel == 0 else last)
    near = dot_tn(jnp.concatenate(near_x, axis=0), jnp.concatenate(own_side, axis=0))
    far = dot_tn(jnp.concatenate(far_x, axis=0), jnp.concatenate(oth_side, axis=0))
    dw_ref[:, : HG * 128] = (near[:, : HG * 128] + far).astype(BF)
    dw_ref[:, HG * 128 : HG * (128 + HD)] = near[:, HG * 128 :].astype(BF)
    values = [sum_q[:, h * HD : (h + 1) * HD] for h in range(HG)]
    values += [sum_kv[:, h * 128 + HD : (h + 1) * 128] for h in range(HG)]
    values = jnp.concatenate(values + [jnp.zeros((128 - 2 * HG, HD), F32)], axis=0).astype(BF)
    inside = lax.broadcasted_iota(jnp.int32, (width, 128), 0) % part
    place = (inside == lanes_like((width, 128))).astype(F32).astype(BF)
    dw_ref[:, HG * (128 + HD) :] = dot_nn(place, values).astype(BF)


def tail(spot, dq, dkv, weight, pieces, part):
    _, seqs, rows, _ = dq.shape
    tokens, width = pieces[0].shape
    local = pl.BlockSpec(memory_space=pltpu.VMEM)
    return pl.pallas_call(
        functools.partial(tail_kernel, rows, part),
        in_specs=[pl.BlockSpec(memory_space=pltpu.SMEM)] + [local] * 11,
        out_specs=[local, local, local],
        out_shape=[
            jax.ShapeDtypeStruct((2, 2, tokens, width), BF),
            jax.ShapeDtypeStruct((2, 2, tokens, width), BF),
            jax.ShapeDtypeStruct((width, 640), BF),
        ],
        compiler_params=pltpu.CompilerParams(vmem_limit_bytes=VMEM_LIMIT),
        cost_estimate=pl.CostEstimate(flops=16 * tokens * width * 480, bytes_accessed=16 << 20, transcendentals=0),
        name="tail",
    )(spot, dq, dkv, weight, *pieces)


def finish_kernel(fold, *refs):
    blocks, (in_ref, down_ref, out_ref, note_ref) = refs[:-4], refs[-4:]
    part, width = out_ref.shape
    hidden = fold * width
    piece = width // fold

    def total(at, size):
        value = blocks[0][:, at : at + size].astype(F32)
        for block in blocks[1:]:
            value = value + block[:, at : at + size].astype(F32)
        return value

    row = lax.broadcasted_iota(jnp.int32, (piece, width), 0)
    for k in range(fold):
        target = row // part * (fold * part) + k * part + row % part
        move = (lanes_like((piece, width)) == target).astype(F32).astype(BF)
        value = total(k * width, width)
        high = value.astype(BF)
        rest = (value - high.astype(F32)).astype(BF)
        for o in range(fold):
            cols = slice(o * piece, (o + 1) * piece)
            placed = dot_nn(high[:, cols], move) + dot_nn(rest[:, cols], move)
            to = slice(o * width, (o + 1) * width)
            in_ref[:, to] = placed if k == 0 else in_ref[:, to] + placed
        down_ref[k] = total(hidden + k * width, width)
    out_ref[...] = total(2 * hidden, width)
    note_ref[...] = total(2 * hidden + width, 128)


def finish(blocks, fold, width):
    part = blocks[0].shape[0]
    local = pl.BlockSpec(memory_space=pltpu.VMEM)
    return pl.pallas_call(
        functools.partial(finish_kernel, fold),
        in_specs=[local] * len(blocks),
        out_specs=[local] * 4,
        out_shape=[
            jax.ShapeDtypeStruct((part, fold * width), F32),
            jax.ShapeDtypeStruct((fold, part, width), F32),
            jax.ShapeDtypeStruct((part, width), F32),
            jax.ShapeDtypeStruct((part, 128), F32),
        ],
        compiler_params=pltpu.CompilerParams(vmem_limit_bytes=VMEM_LIMIT),
        cost_estimate=pl.CostEstimate(flops=1 << 27, bytes_accessed=2 << 20, transcendentals=0),
        name="finish",
    )(*blocks)


def assemble_kernel(got_ref, grad_ref, note_ref):
    width = grad_ref.shape[1] // 3
    for t in range(TP):
        total = got_ref[0, t].astype(F32)
        for i in range(1, got_ref.shape[0]):
            total = total + got_ref[i, t].astype(F32)
        at = t * HG * HD
        grad_ref[:, at : at + HG * HD] = total[:, HG * 128 : HG * (128 + HD)]
        for h in range(HG):
            for j in range(2):
                to = (1 + j) * width + at + h * HD
                grad_ref[:, to : to + HD] = total[:, h * 128 + j * HD : h * 128 + (j + 1) * HD]
        note_ref[t] = total[:, HG * (128 + HD) :]


def assemble(got):
    _, _, part, _ = got.shape
    local = pl.BlockSpec(memory_space=pltpu.VMEM)
    return pl.pallas_call(
        assemble_kernel,
        in_specs=[local],
        out_specs=[local, local],
        out_shape=[
            jax.ShapeDtypeStruct((part, 3 * H * HD), F32),
            jax.ShapeDtypeStruct((TP, part, HD), F32),
        ],
        compiler_params=pltpu.CompilerParams(vmem_limit_bytes=VMEM_LIMIT),
        name="assemble",
    )(got)


def swap_on(axis):
    return lambda v: lax.ppermute(v, axis, [(0, 1), (1, 0)])


def crossing(first):
    pairs = []
    for u in range(2):
        for y in range(2):
            for c in range(2):
                along_u = (c == 0) == first
                to = (1 - u, y, c) if along_u else (u, 1 - y, c)
                pairs.append(((u * 2 + y) * 2 + c, (to[0] * 2 + to[1]) * 2 + to[2]))
    return lambda v: lax.ppermute(v, ("u", "y", "c"), pairs)


def after(v, *earlier):
    return lax.optimization_barrier((v,) + earlier)[0]


def add(a, b):
    return (a.astype(F32) + b.astype(F32)).astype(BF)


def pick(v, index, axis):
    return lax.dynamic_index_in_dim(v, index, axis, keepdims=False)


def put(buffer, v, index):
    return lax.dynamic_update_index_in_dim(buffer, v, index, 0)


def per_device(layer_input, wqkv, wo, wi, wd, biases, hidden_bias, gains, shifts, cotangent, block_ids, offsets, pairing):
    seqs, rows, width = layer_input.shape
    devices = lax.axis_size(ALL)
    ring = lax.axis_size("r")
    shards = ring * TP
    half = shards * rows
    tokens = seqs * rows
    me_u, me_r, me_y, me_c = (lax.axis_index(a) for a in ALL)
    me_t = me_y * 2 + me_c
    part = wqkv.shape[0]
    hidden = wi.shape[1]
    fold = hidden // width
    swap_u, swap_c = swap_on("u"), swap_on("c")
    cross_one, cross_two = crossing(True), crossing(False)
    forward = [(i, (i + 1) % ring) for i in range(ring)]

    notes = [biases[2:].T, gains.T, shifts.T, hidden_bias.reshape(fold, part).T]
    notes = jnp.concatenate(notes + [jnp.zeros((part, 128 - 6 - fold), BF)], axis=1)
    wi_turned = wi.reshape(part, devices, fold, part).transpose(0, 2, 1, 3).reshape(part, hidden)
    wd_cols = [wd[k * part : (k + 1) * part] for k in range(fold)]
    dense_own = jnp.concatenate([wo, wi_turned] + wd_cols + [notes], axis=1)

    by_head = wqkv.reshape(part, 3, TP, HG, HD)
    blocks_kv = by_head[:, 1:].transpose(2, 0, 3, 1, 4).reshape(TP, part, HG * 128)
    blocks_q = by_head[:, 0].transpose(1, 0, 2, 3).reshape(TP, part, HG * HD)
    ends = jnp.pad(biases[:2].T, ((0, 0), (0, HD - 2)))
    blocks = jnp.concatenate([blocks_kv, blocks_q, jnp.broadcast_to(ends, (TP, part, HD))], axis=2)
    blocks = lax.all_to_all(blocks, ("y", "c"), split_axis=0, concat_axis=0, tiled=True)
    column = put(jnp.zeros((ring,) + blocks.shape, BF), blocks, me_r)
    for k in range(1, ring):
        got = lax.ppermute(blocks, "r", [(i, (i + k) % ring) for i in range(ring)])
        column = put(column, got, (me_r - k) % ring)
    early = (cross_one(layer_input.reshape(tokens, width)), cross_two(layer_input.reshape(tokens, width)))
    column = after(column, *early)
    dense = lax.all_gather(after(dense_own, column), ALL, axis=0, tiled=True)
    both = jnp.zeros((2,) + column.shape, BF)
    w_here = put(put(both, column, me_u), swap_u(column), 1 - me_u).reshape(width, 640)
    b_heads = w_here[:, 576:578].astype(F32)
    b_heads = lax.dynamic_slice_in_dim(b_heads, me_t * HG * HD, HG * HD, 0).T
    b_kv = jnp.concatenate([jnp.zeros((HG, HD), F32), b_heads[1].reshape(HG, HD)], axis=1).reshape(-1)
    b_here = jnp.concatenate([b_kv, b_heads[0], jnp.zeros((HD,), F32)])
    b_here = jnp.broadcast_to(b_here, (8, 640))

    x_own = layer_input.reshape(tokens, width)
    piece = x_own
    stages = []
    for k in range(ring):
        if k == 1:
            piece, column = lax.optimization_barrier((piece, column))
        if k:
            piece = lax.ppermute(piece, "r", forward)
        if k >= 2:
            piece, stages[k - 2] = lax.optimization_barrier((piece, stages[k - 2]))
        one, two = early if k == 0 else (cross_one(piece), cross_two(piece))
        if k == 1:
            one, w_here = lax.optimization_barrier((one, w_here))
        three = cross_two(one)
        if k >= 2:
            three, stages[k - 1] = lax.optimization_barrier((three, stages[k - 1]))
        mine = [piece, one, two, three]
        theirs = [swap_c(m) for m in mine]
        if k == 0:
            x_near = (mine, theirs)
        spot = jnp.stack([me_u, me_y, me_c, (me_r - k) % ring]).astype(jnp.int32)
        stages.append(project(mine + theirs, w_here, b_here, spot, stages[-1] if stages else None, ring, seqs, rows))
    buffers = stages[-1]
    kv = buffers[0].reshape(2, shards, seqs, rows, HG * 128)
    q_all = buffers[1].reshape(shards, seqs, rows, HG * 128)
    q_loc = lax.dynamic_slice_in_dim(q_all, me_r * TP, TP, 0)

    pair = lax.dynamic_slice_in_dim(pick(pairing, me_u, 1), me_t * HG, HG, 0)
    ids = block_ids.reshape(seqs, 2, half)
    ids_own = pick(ids, me_u, 1)
    ends = jnp.sum((ids[:, :, None, :] <= ids_own[:, None, :, None]).astype(jnp.int32), axis=-1)
    end_all = jnp.where((pair == 0)[None, :, None], ends[:, 0:1], ends[:, 1:2])
    end_loc = lax.dynamic_slice_in_dim(end_all, me_r * TP * rows, TP * rows, 2)
    begin = jnp.maximum(offsets[:, None] - pair[None, :] * half, 0).reshape(-1)
    last = end_loc[:, :, -1].reshape(-1)
    start = me_r * TP * rows
    end_ring = end_all.reshape(seqs, HG, ring, TP * rows)
    end_row_own = end_loc[:, :, None]

    att = attend_forward(q_loc, kv, pair, begin, last, end_row_own)
    att = lax.all_to_all(att, ("y", "c"), split_axis=0, concat_axis=0, tiled=True).reshape(TP, tokens, 256)

    index = jnp.arange(width, dtype=jnp.int32)
    inner_at, index = index % part, index // part
    r_rel, index = index % ring, index // ring
    s_rel, f_rel, c_rel = index % 2, index // 2 % 2, index // 4
    core = me_c ^ c_rel
    to_u = me_u ^ jnp.where(core == 0, f_rel, s_rel)
    to_y = me_y ^ jnp.where(core == 0, s_rel, f_rel)
    order = (((to_u * ring + (me_r + r_rel) % ring) * 2 + to_y) * 2 + core) * part + inner_at
    order = jnp.broadcast_to(order.astype(jnp.int32), (8, width))
    hidden_out, load, dsum, stay, leave = dense_layers(att, x_own, cotangent.reshape(tokens, width), order, dense, fold)
    hidden_out = hidden_out.reshape(seqs, rows, width)
    came = swap_c(leave)
    cut = width // 4
    high, low = add(stay[cut:], came[cut:]), add(stay[:cut], came[:cut])
    high_first = high
    cut = width // 8
    load = load.reshape(TP, seqs, rows, 256)
    load = lax.all_to_all(load, ("y", "c"), split_axis=0, concat_axis=0, tiled=True)
    came = cross_one(after(high_first, load))
    place = jnp.stack([start, me_r])
    dkv = jnp.zeros((TP, seqs, rows, HG * 128), F32)
    moving = load
    done = []
    for k in range(ring):
        if k >= 2:
            moving, done[k - 2] = lax.optimization_barrier((moving, done[k - 2]))
        if k == 2:
            moving, dq = lax.optimization_barrier((moving, dq))
        if k:
            moving = lax.ppermute(moving, "r", forward)
        source = (me_r - k) % ring
        ends_k = pick(end_ring, source, 2)
        where = jnp.concatenate([place, source[None]]).astype(jnp.int32)
        before = done[-1] if done else dkv
        if k == ring - 2:
            high2, low2 = add(low[cut:], came[cut:]), add(low[:cut], came[:cut])
            stay = add(low2, cross_two(high2))
            before = after(before, high2)
        done.append(attend_key(q_all, moving, kv, pair, begin, ends_k[:, :, -1].reshape(-1), where, ends_k[:, :, None], before))
        if k == 0:
            dq = attend_query(q_loc, kv, pair, begin, last, end_row_own, after(load, high))

    summed = stay[:part].astype(F32)
    for j in range(1, ring):
        along = [(i, (i + j) % ring) for i in range(ring)]
        summed = summed + lax.ppermute(stay[j * part : (j + 1) * part], "r", along).astype(F32)
    spot = jnp.concatenate([jnp.stack([me_u, me_y, me_c]), (pair == me_u).astype(jnp.int32)])
    keep, send, dw = tail(spot.astype(jnp.int32), dq, done[-1], w_here, x_near[0] + x_near[1], part)
    keep = add(keep, swap_c(send))
    dw = after(dw, keep)
    got = lax.all_to_all(dw.reshape(devices, part, 640), ALL, split_axis=0, concat_axis=0, tiled=True)
    came = cross_one(keep[1])
    onward = add(keep[0, 1], came[1])
    final = cross_two(onward)
    grad_w_in, grad_w_down, grad_w_out, flat = finish([after(summed, onward)], fold, width)
    grad_w_down = grad_w_down.reshape(fold * part, width)
    flat = flat[:, : 6 + fold].T
    grad_bo, grad_gains, grad_shifts, grad_bin = flat[0:2], flat[2:4], flat[4:6], flat[6:].reshape(-1)

    grad_input = dsum + keep[0, 0].astype(F32) + came[0].astype(F32) + final.astype(F32)
    grad_input = grad_input.astype(BF).reshape(seqs, rows, width)
    grad_w_qkv, note = assemble(after(got, final).reshape(2 * ring, TP, part, 640))
    at = lax.axis_index(ALL) * part
    grad_bq = lax.dynamic_slice_in_dim(note[:, :HG].reshape(width), at, part, 0)
    grad_bv = lax.dynamic_slice_in_dim(note[:, HG : 2 * HG].reshape(width), at, part, 0)
    grad_biases = jnp.concatenate([jnp.stack([grad_bq, grad_bv]), grad_bo])
    return (hidden_out, grad_input, grad_w_qkv, grad_w_out, grad_w_in, grad_w_down, grad_biases, grad_bin, grad_gains, grad_shifts)


def solution(mesh):
    wide = mesh.shape["blk"]
    grid = Mesh(mesh.devices.reshape(2, wide // TP, 2, TP // 2), ALL)
    rows2, cols1 = P(ALL, None), P(None, ALL)
    toks = P(None, ALL, None)
    return jax.shard_map(
        per_device,
        mesh=grid,
        in_specs=(toks, rows2, rows2, rows2, rows2, cols1, P(ALL), cols1, cols1, toks, P(), P(), P()),
        out_specs=(toks, toks, rows2, rows2, rows2, rows2, cols1, P(ALL), cols1, cols1),
        check_vma=False,
    )
```

```python
import functools

import jax
import jax.numpy as jnp
from jax import lax
from jax.experimental import pallas as pl
from jax.experimental.pallas import tpu as pltpu
from jax.sharding import Mesh
from jax.sharding import PartitionSpec as P

H = 12
HD = 64
TP = 4
HG = H // TP
NORM_EPS = 1e-12
FILL = -1e30
FLOOR = -1e29
ALL = ("u", "r", "y", "c")
BF = jnp.bfloat16
F32 = jnp.float32
VMEM_LIMIT = 56 * 1024 * 1024


def split_three(v):
    high = v.astype(BF)
    v = v - high.astype(F32)
    middle = v.astype(BF)
    return high, middle, (v - middle.astype(F32)).astype(BF)


def dot_nt(a, b):
    return lax.dot_general(a, b, (((1,), (1,)), ((), ())), preferred_element_type=F32)


def dot_nn(a, b):
    return lax.dot_general(a, b, (((1,), (0,)), ((), ())), preferred_element_type=F32)


def dot_tn(a, b):
    return lax.dot_general(a, b, (((0,), (0,)), ((), ())), preferred_element_type=F32)


def lanes_like(shape):
    return lax.broadcasted_iota(jnp.int32, shape, len(shape) - 1)


def chooser(h, kind, depth):
    at = HD + kind * 3 * HG + 3 * h
    lane = lanes_like((depth, 128))
    return jnp.where((lane >= at) & (lane < at + 3), -1.0, 0.0).astype(BF)


def chunk_of(shards):
    return 16 if shards % 16 == 0 else shards


def key_spots(first, count, begin, end_row):
    spot = lax.broadcasted_iota(jnp.int32, (count, 1), 0) + first
    return jnp.where(spot >= begin, spot, 1 << 30) < end_row


def forward_kernel(rows, shards, pair_ref, begin_ref, last_ref, q_ref, kv0, kv1, kv2, end_ref, att_ref, m_ref, l_ref, acc_ref):
    seq = pl.program_id(0)
    group = chunk_of(shards)
    nq = TP * rows
    width = group * rows
    for h in range(HG):
        m_ref[h] = jnp.full((1, nq), FLOOR, F32)
        l_ref[h] = jnp.zeros((1, nq), F32)
        acc_ref[h] = jnp.zeros((128, nq), F32)

    def step(c, _):
        for h, kv_ref in enumerate((kv0, kv1, kv2)):
            query = q_ref[:, 0, :, h * 128 : (h + 1) * 128].reshape(nq, 128)
            kv = kv_ref[0, pl.ds(c * group, group), 0].reshape(width, 128)
            seen = key_spots(c * width, width, begin_ref[seq * HG + h], end_ref[0, h])
            scores = jnp.where(seen, dot_nt(kv, query), FILL)
            old = m_ref[h]
            new = jnp.maximum(old, jnp.max(scores, axis=0, keepdims=True))
            weights = jnp.exp(scores - new)
            factor = jnp.exp(old - new)
            m_ref[h] = new
            l_ref[h] = l_ref[h] * factor + jnp.sum(weights, axis=0, keepdims=True)
            acc_ref[h] = acc_ref[h] * factor + dot_tn(kv, weights.astype(BF))
        return 0

    trips = [pl.cdiv(last_ref[seq * HG + h], width) for h in range(HG)]
    lax.fori_loop(0, functools.reduce(jnp.maximum, trips), step, 0)
    turn = lax.broadcasted_iota(jnp.int32, (HD, nq), 0)
    notes = jnp.zeros((HD, nq), F32)
    for h in range(HG):
        total = jnp.maximum(l_ref[h], 1.0)
        for p, value in enumerate(split_three(m_ref[h] + jnp.log(total))):
            notes = jnp.where(turn == 3 * HG + 3 * h + p, value.astype(F32), notes)
        att = (acc_ref[h] / total)[HD:].T.astype(BF)
        att_ref[:, 0, :, h * HD : (h + 1) * HD] = att.reshape(TP, rows, HD)
    att_ref[:, 0, :, HG * HD :] = notes.T.astype(BF).reshape(TP, rows, HD)


def output_gradient(load_ref, h, count):
    dout = load_ref[:, 0, :, h * HD : (h + 1) * HD].reshape(count, HD)
    return jnp.concatenate([jnp.zeros_like(dout), dout], axis=1)


def query_kernel(rows, shards, pair_ref, begin_ref, last_ref, q_ref, kv0, kv1, kv2, end_ref, load_ref, dq_ref, acc_ref):
    seq = pl.program_id(0)
    group = chunk_of(shards)
    nq = TP * rows
    width = group * rows
    notes = load_ref[:, 0, :, 128:].reshape(nq, 128)
    acc_ref[...] = jnp.zeros_like(acc_ref)

    def step(c, _):
        for h, kv_ref in enumerate((kv0, kv1, kv2)):
            query = q_ref[:, 0, :, h * 128 : (h + 1) * 128].reshape(nq, 128)
            kv = kv_ref[0, pl.ds(c * group, group), 0].reshape(width, 128)
            seen = key_spots(c * width, width, begin_ref[seq * HG + h], end_ref[0, h])
            query = jnp.concatenate([query, notes], axis=1)
            dout = jnp.concatenate([output_gradient(load_ref, h, nq), notes], axis=1)
            scores = dot_nt(jnp.concatenate([kv, chooser(h, 1, width)], axis=1), query)
            prob = jnp.exp(jnp.where(seen, scores, FILL))
            dprob = dot_nt(jnp.concatenate([kv, chooser(h, 0, width)], axis=1), dout)
            acc_ref[h] += dot_tn(kv, (prob * dprob).astype(BF))
        return 0

    trips = [pl.cdiv(last_ref[seq * HG + h], width) for h in range(HG)]
    lax.fori_loop(0, functools.reduce(jnp.maximum, trips), step, 0)
    for h in range(HG):
        dq = (acc_ref[h][:HD] * (HD**-0.5)).T.astype(BF)
        dq_ref[:, 0, :, h * HD : (h + 1) * HD] = dq.reshape(TP, rows, HD)


def key_kernel(rows, pair_ref, begin_ref, reach_ref, place_ref, q_ref, load_ref, kv0, kv1, kv2, end_ref, old_ref, dkv_ref):
    seq = pl.program_id(0)
    span = TP * rows
    start = place_ref[0]
    reach = [reach_ref[seq * HG + h] for h in range(HG)]
    needed = functools.reduce(jnp.maximum, reach) > start

    @pl.when(needed)
    def _():
        notes = load_ref[:, 0, :, 128:].reshape(span, 128)
        for h, kv_ref in enumerate((kv0, kv1, kv2)):
            lanes = slice(h * 128, (h + 1) * 128)
            kv = kv_ref[0, :, 0].reshape(span, 128)
            query = q_ref[:, 0, :, lanes].reshape(span, 128)
            dout = output_gradient(load_ref, h, span)
            seen = key_spots(start, span, begin_ref[seq * HG + h], end_ref[0, h])
            scores = dot_nt(jnp.concatenate([kv, chooser(h, 1, span)], axis=1), jnp.concatenate([query, notes], axis=1))
            prob = jnp.exp(jnp.where(seen, scores, FILL))
            dprob = dot_nt(jnp.concatenate([kv, chooser(h, 0, span)], axis=1), jnp.concatenate([dout, notes], axis=1))
            sides = jnp.concatenate([(prob * dprob).astype(BF), prob.astype(BF)], axis=1)
            new = dot_nn(sides, jnp.concatenate([query, dout], axis=0))
            dkv_ref[:, 0, :, lanes] = old_ref[:, 0, :, lanes] + new.reshape(TP, rows, 128)

    @pl.when(jnp.logical_not(needed))
    def _():
        dkv_ref[...] = old_ref[...]


def project_kernel(seqs, rows, fresh, spot_ref, *refs):
    pieces, w_ref, bias_ref = refs[:8], refs[8], refs[9]
    kv_out, q_out, kv_tmp, q_tmp, kv_sem, q_sem = refs[10 if fresh else 12 :]
    keys = HG * 128
    tokens = seqs * rows
    me_u, me_y, me_c, source = (spot_ref[i] for i in range(4))
    for which in range(2):
        core = me_c if which == 0 else 1 - me_c
        x = jnp.concatenate([pieces[which * 4 + i][...] for i in range(4)], axis=0)
        if which == 0:
            q_tmp[...] = jnp.zeros_like(q_tmp)
        kv = (dot_nn(x, w_ref[:, :keys]) + bias_ref[0:1, :keys]).astype(BF)
        for i in range(4):
            p, q = i // 2, i % 2
            x_rel = jnp.where(core == 0, q, p)
            y_rel = jnp.where(core == 0, p, q)
            shard = jnp.bitwise_xor(me_y, y_rel) * 2 + core
            slot = which * 4 + i
            kv_tmp[slot] = kv[i * tokens : (i + 1) * tokens].reshape(seqs, rows, keys)
            spot = kv_out.at[jnp.bitwise_xor(me_u, x_rel), source, shard]
            pltpu.make_async_copy(kv_tmp.at[slot], spot, kv_sem.at[slot]).start()
        second = jnp.where(core == 0, x[2 * tokens : 3 * tokens], x[tokens : 2 * tokens])
        for y_rel, part in enumerate((x[:tokens], second)):
            query = (dot_nn(part, w_ref[:, keys:]) + bias_ref[0:1, keys:]) * (HD**-0.5)
            slot = which * 2 + y_rel
            query = query.astype(BF)
            for h in range(HG):
                q_tmp[slot, :, :, h * 128 : h * 128 + HD] = query[:, h * HD : (h + 1) * HD].reshape(seqs, rows, HD)
            shard = jnp.bitwise_xor(me_y, y_rel) * 2 + core
            pltpu.make_async_copy(q_tmp.at[slot], q_out.at[source, shard], q_sem.at[slot]).start()
    for slot in range(8):
        pltpu.make_async_copy(kv_tmp.at[slot], kv_out.at[0, 0, 0], kv_sem.at[slot]).wait()
    for slot in range(4):
        pltpu.make_async_copy(q_tmp.at[slot], q_out.at[0, 0], q_sem.at[slot]).wait()


def project(pieces, weight, bias, spot, buffers, ring, seqs, rows):
    keys = HG * 128
    width = weight.shape[0]
    tokens = seqs * rows
    extra = [] if buffers is None else list(buffers)
    anywhere = pl.BlockSpec(memory_space=pl.ANY)
    local = pl.BlockSpec(memory_space=pltpu.VMEM)
    return pl.pallas_call(
        functools.partial(project_kernel, seqs, rows, not extra),
        in_specs=[pl.BlockSpec(memory_space=pltpu.SMEM)] + [local] * 10 + [anywhere] * len(extra),
        out_specs=[anywhere, anywhere],
        scratch_shapes=[
            pltpu.VMEM((8, seqs, rows, keys), BF),
            pltpu.VMEM((4, seqs, rows, keys), BF),
            pltpu.SemaphoreType.DMA((8,)),
            pltpu.SemaphoreType.DMA((4,)),
        ],
        out_shape=[
            jax.ShapeDtypeStruct((2, ring, TP, seqs, rows, keys), BF),
            jax.ShapeDtypeStruct((ring, TP, seqs, rows, keys), BF),
        ],
        input_output_aliases={11: 0, 12: 1} if extra else {},
        compiler_params=pltpu.CompilerParams(vmem_limit_bytes=VMEM_LIMIT),
        cost_estimate=pl.CostEstimate(flops=12 * tokens * width * keys * 2, bytes_accessed=12 << 20, transcendentals=0),
        name="project",
    )(spot, *pieces, weight, bias, *extra)


def keys_spec(h, shards, rows):
    return pl.BlockSpec((1, shards, 1, rows, 128), lambda s, pair, *_: (pair[h], 0, s, 0, h))


def attend_forward(q_all, kv, pair, begin, last, end_row_own):
    _, shards, seqs, rows, _ = kv.shape
    nq = TP * rows
    row_spec = pl.BlockSpec((TP, 1, rows, 384), lambda s, pair, begin, last: (last[seqs * HG], s, 0, 0))
    end_spec = pl.BlockSpec((1, HG, 1, nq), lambda s, *_: (s, 0, 0, 0))
    return pl.pallas_call(
        functools.partial(forward_kernel, rows, shards),
        grid_spec=pltpu.PrefetchScalarGridSpec(
            num_scalar_prefetch=3,
            grid=(seqs,),
            in_specs=[row_spec] + [keys_spec(h, shards, rows) for h in range(HG)] + [end_spec],
            out_specs=pl.BlockSpec((TP, 1, rows, 256), lambda s, *_: (0, s, 0, 0)),
            scratch_shapes=[pltpu.VMEM((HG, 1, nq), F32), pltpu.VMEM((HG, 1, nq), F32), pltpu.VMEM((HG, 128, nq), F32)],
        ),
        out_shape=jax.ShapeDtypeStruct((TP, seqs, rows, 256), BF),
        compiler_params=pltpu.CompilerParams(vmem_limit_bytes=VMEM_LIMIT),
        cost_estimate=pl.CostEstimate(flops=4 * 9 * nq * shards * rows * 128, bytes_accessed=12 << 20, transcendentals=0),
        name="attend_forward",
    )(pair, begin, last, q_all, kv, kv, kv, end_row_own)


def attend_query(q_all, kv, pair, begin, last, end_row_own, load):
    _, shards, seqs, rows, _ = kv.shape
    nq = TP * rows
    row_spec = pl.BlockSpec((TP, 1, rows, 384), lambda s, pair, begin, last: (last[seqs * HG], s, 0, 0))
    end_spec = pl.BlockSpec((1, HG, 1, nq), lambda s, *_: (s, 0, 0, 0))
    return pl.pallas_call(
        functools.partial(query_kernel, rows, shards),
        grid_spec=pltpu.PrefetchScalarGridSpec(
            num_scalar_prefetch=3,
            grid=(seqs,),
            in_specs=[row_spec]
            + [keys_spec(h, shards, rows) for h in range(HG)]
            + [end_spec, pl.BlockSpec((TP, 1, rows, 256), lambda s, *_: (0, s, 0, 0))],
            out_specs=pl.BlockSpec((TP, 1, rows, HG * HD), lambda s, *_: (0, s, 0, 0)),
            scratch_shapes=[pltpu.VMEM((HG, 128, nq), F32)],
        ),
        out_shape=jax.ShapeDtypeStruct((TP, seqs, rows, HG * HD), BF),
        compiler_params=pltpu.CompilerParams(vmem_limit_bytes=VMEM_LIMIT),
        cost_estimate=pl.CostEstimate(flops=6 * 9 * nq * shards * rows * 128, bytes_accessed=12 << 20, transcendentals=0),
        name="attend_query",
    )(pair, begin, last, q_all, kv, kv, kv, end_row_own, load)


def attend_key(q_all, load, kv, pair, begin, reach, place, end_row, old):
    _, shards, seqs, rows, _ = kv.shape

    def own_keys(h):
        return pl.BlockSpec((1, TP, 1, rows, 128), lambda s, pair, begin, reach, place: (pair[h], place[1], s, 0, h))

    total = pl.BlockSpec((TP, 1, rows, 384), lambda s, *_: (0, s, 0, 0))
    return pl.pallas_call(
        functools.partial(key_kernel, rows),
        grid_spec=pltpu.PrefetchScalarGridSpec(
            num_scalar_prefetch=4,
            grid=(seqs,),
            in_specs=[
                pl.BlockSpec((TP, 1, rows, 384), lambda s, pair, begin, reach, place: (place[2], s, 0, 0)),
                pl.BlockSpec((TP, 1, rows, 256), lambda s, *_: (0, s, 0, 0)),
            ]
            + [own_keys(h) for h in range(HG)]
            + [pl.BlockSpec((1, HG, 1, TP * rows), lambda s, *_: (s, 0, 0, 0)), total],
            out_specs=total,
        ),
        out_shape=jax.ShapeDtypeStruct((TP, seqs, rows, 384), F32),
        input_output_aliases={10: 0},
        compiler_params=pltpu.CompilerParams(vmem_limit_bytes=VMEM_LIMIT),
        cost_estimate=pl.CostEstimate(flops=8 * 9 * (TP * rows) ** 2 * 128, bytes_accessed=8 << 20, transcendentals=0),
        name="attend_key",
    )(pair, begin, reach, place, q_all, load, kv, kv, kv, end_row, old)


def norm_parts(summed):
    centred = summed - jnp.mean(summed, axis=1, keepdims=True)
    inv_std = lax.rsqrt(jnp.mean(centred * centred, axis=1, keepdims=True) + NORM_EPS)
    return centred * inv_std, inv_std


def dense_kernel(fold, att_ref, x_ref, cot_ref, order_ref, dense_ref, out_ref, load_ref, dsum_ref, keep_ref, send_ref, w, note, grad, grad_note, act, slope, turn, in_sem, out_sem):
    tokens, width = x_ref.shape
    blocks = 2 * fold + 1

    def fetch(b):
        wide = pl.ds(b * width, width) if b < blocks else pl.ds(blocks * width, 128)
        return pltpu.make_async_copy(dense_ref.at[:, wide], w.at[b] if b < blocks else note, in_sem.at[b])

    def ship(b, side):
        wide = pl.ds(b * width, width) if b < blocks else pl.ds(blocks * width, 128)
        rows = pl.ds(side * (width // 2), width // 2)
        source = grad.at[b, rows] if b < blocks else grad_note.at[rows]
        return pltpu.make_async_copy(source, (send_ref if side else keep_ref).at[:, wide], out_sem.at[2 * b + side])

    def start_ship(b):
        ship(b, 0).start()
        ship(b, 1).start()

    for b in [0, blocks] + list(range(1, blocks)):
        fetch(b).start()
    att = jnp.concatenate([att_ref[t, :, : HG * HD] for t in range(TP)], axis=1)
    row = lax.broadcasted_iota(jnp.int32, (width, width), 0)
    turn[...] = (row == order_ref[0:1]).astype(F32).astype(BF)

    def turned(v):
        return dot_nn(v, turn[...]).astype(BF)

    fetch(0).wait()
    fetch(blocks).wait()
    vec = note[...].astype(F32).T
    gain_one, gain_two, shift_one, shift_two = (vec[i : i + 1] for i in range(2, 6))
    normed_one, inv_one = norm_parts(x_ref[...].astype(F32) + dot_nn(att, w[0]) + vec[0:1])
    mid = normed_one * gain_one + shift_one
    mid_low = mid.astype(BF)
    feed = mid + vec[1:2]
    for k in range(fold):
        fetch(1 + k).wait()
        inner = dot_nn(mid_low, w[1 + k]) + vec[6 + k : 7 + k]
        spread = 0.5 + 0.5 * lax.erf(inner * (0.5**0.5))
        act[k] = (inner * spread).astype(BF)
        slope[k] = spread + inner * (jnp.exp(-0.5 * inner * inner) * 0.3989422804014327)
    for k in range(fold):
        fetch(1 + fold + k).wait()
        feed = feed + dot_nn(act[k], w[1 + fold + k])
    normed_two, inv_two = norm_parts(feed)
    out_ref[...] = (normed_two * gain_two + shift_two).astype(BF)
    grad_out = cot_ref[...].astype(F32)

    def back(incoming, normed, inv_std, gain):
        scaled = incoming * gain
        along = jnp.mean(scaled * normed, axis=1, keepdims=True)
        return inv_std * (scaled - jnp.mean(scaled, axis=1, keepdims=True) - normed * along)

    def total(v):
        return jnp.sum(v, axis=0, keepdims=True)

    dsecond = back(grad_out, normed_two, inv_two, gain_two)
    dfeed = dsecond.astype(BF)
    sums = [None, total(dfeed.astype(F32)), None, total(grad_out * normed_two), None, total(grad_out)]
    dmid = dsecond
    mid_turned = turned(mid_low)
    for k in range(fold):
        dinner = (dot_nt(dfeed, w[1 + fold + k]) * slope[k]).astype(BF)
        sums.append(total(dinner.astype(F32)))
        grad[k] = dot_tn(mid_turned, dinner).astype(BF)
        start_ship(k)
        grad[fold + k] = dot_tn(turned(act[k]), dfeed).astype(BF)
        start_ship(fold + k)
        dmid = dmid + dot_nt(dinner, w[1 + k])
    dsum = back(dmid, normed_one, inv_one, gain_one)
    dsum_ref[...] = dsum
    dproj = dsum.astype(BF)
    sums[0], sums[2], sums[4] = total(dproj.astype(F32)), total(dmid * normed_one), total(dmid)
    datt = dot_nt(dproj, w[0]).astype(BF)
    product = datt.astype(F32) * att.astype(F32)
    high = product.astype(BF)
    rest = (product - high.astype(F32)).astype(BF)
    feature = lax.broadcasted_iota(jnp.int32, (width, 128), 0)
    lane = lanes_like((width, 128))
    third = lanes_like((tokens, HD)) % 3
    for t in range(TP):
        of_head = ((feature // HD == t * HG + lane // 3) & (lane < 3 * HG)).astype(F32).astype(BF)
        delta = (dot_nn(high, of_head) + dot_nn(rest, of_head))[:, :HD]
        one, two, three = (v.astype(F32) for v in split_three(delta))
        notes = jnp.where(third == 0, one, jnp.where(third == 1, two, three))
        load_ref[t, :, : HG * HD] = datt[:, t * HG * HD : (t + 1) * HG * HD]
        load_ref[t, :, HG * HD :] = (notes + att_ref[t, :, HG * HD :].astype(F32)).astype(BF)
    grad[2 * fold] = dot_tn(turned(att), dproj).astype(BF)
    start_ship(2 * fold)
    table = jnp.concatenate(sums + [jnp.zeros((128 - len(sums), width), F32)], axis=0)
    grad_note[...] = dot_nn(table.astype(BF), turn[...]).T.astype(BF)
    start_ship(blocks)
    for b in range(blocks + 1):
        ship(b, 0).wait()
        ship(b, 1).wait()


def dense_layers(att, x, cotangent, order, dense, fold):
    tokens, width = x.shape
    blocks = 2 * fold + 1
    local = pl.BlockSpec(memory_space=pltpu.VMEM)
    anywhere = pl.BlockSpec(memory_space=pl.ANY)
    return pl.pallas_call(
        functools.partial(dense_kernel, fold),
        in_specs=[local, local, local, local, anywhere],
        out_specs=[local, local, local, anywhere, anywhere],
        out_shape=[
            jax.ShapeDtypeStruct((tokens, width), BF),
            jax.ShapeDtypeStruct((TP, tokens, 256), BF),
            jax.ShapeDtypeStruct((tokens, width), F32),
            jax.ShapeDtypeStruct((width // 2, blocks * width + 128), BF),
            jax.ShapeDtypeStruct((width // 2, blocks * width + 128), BF),
        ],
        scratch_shapes=[
            pltpu.VMEM((blocks, width, width), BF),
            pltpu.VMEM((width, 128), BF),
            pltpu.VMEM((blocks, width, width), BF),
            pltpu.VMEM((width, 128), BF),
            pltpu.VMEM((fold, tokens, width), BF),
            pltpu.VMEM((fold, tokens, width), F32),
            pltpu.VMEM((width, width), BF),
            pltpu.SemaphoreType.DMA((blocks + 1,)),
            pltpu.SemaphoreType.DMA((2 * blocks + 2,)),
        ],
        compiler_params=pltpu.CompilerParams(vmem_limit_bytes=VMEM_LIMIT),
        cost_estimate=pl.CostEstimate(flops=54 * tokens * width * width, bytes_accessed=24 << 20, transcendentals=0),
        name="dense_layers",
    )(att, x, cotangent, order, dense)


def tail_kernel(rows, part, spot_ref, dq_ref, dkv_ref, w_ref, *refs):
    pieces, (keep_ref, send_ref, dw_ref) = refs[:8], refs[8:]
    me_y, me_c = spot_ref[1], spot_ref[2]
    lane = lanes_like((1, HG * 128))
    is_own = jnp.zeros((1, HG * 128), jnp.int32)
    for h in range(HG):
        is_own = jnp.where(lane // 128 == h, spot_ref[3 + h], is_own)
    tokens, width = pieces[0].shape
    own_side, oth_side, near_x, far_x = [], [], [], []
    sum_q = sum_kv = 0.0
    for which, out_ref in enumerate((keep_ref, send_ref)):
        core = me_c if which == 0 else 1 - me_c
        middle = [pieces[4 * which + i][...] for i in (1, 2)]
        for y_rel in range(2):
            shard = jnp.bitwise_xor(me_y, y_rel) * 2 + core
            dq = dq_ref[shard].reshape(tokens, HG * HD)
            dkv = dkv_ref[shard].reshape(tokens, HG * 128)
            own = jnp.concatenate([jnp.where(is_own == 1, dkv, 0.0).astype(BF), dq], axis=1)
            oth = jnp.where(is_own == 1, 0.0, dkv).astype(BF)
            sum_q = sum_q + jnp.sum(dq.astype(F32), axis=0, keepdims=True)
            sum_kv = sum_kv + jnp.sum(dkv.astype(BF).astype(F32), axis=0, keepdims=True)
            to_own = dot_nt(own, w_ref[:, : HG * (128 + HD)]).astype(BF)
            to_oth = dot_nt(oth, w_ref[:, : HG * 128]).astype(BF)
            for x_rel, value in enumerate((to_own, to_oth)):
                out_ref[jnp.where(core == 0, x_rel, y_rel), jnp.where(core == 0, y_rel, x_rel)] = value
            own_side.append(own)
            oth_side.append(oth)
            first, last = pieces[4 * which][...], pieces[4 * which + 3][...]
            one = jnp.where(core == 0, middle[0], middle[1])
            two = jnp.where(core == 0, middle[1], middle[0])
            near_x.append(first if y_rel == 0 else two)
            far_x.append(one if y_rel == 0 else last)
    near = dot_tn(jnp.concatenate(near_x, axis=0), jnp.concatenate(own_side, axis=0))
    far = dot_tn(jnp.concatenate(far_x, axis=0), jnp.concatenate(oth_side, axis=0))
    dw_ref[:, : HG * 128] = (near[:, : HG * 128] + far).astype(BF)
    dw_ref[:, HG * 128 : HG * (128 + HD)] = near[:, HG * 128 :].astype(BF)
    values = [sum_q[:, h * HD : (h + 1) * HD] for h in range(HG)]
    values += [sum_kv[:, h * 128 + HD : (h + 1) * 128] for h in range(HG)]
    values = jnp.concatenate(values + [jnp.zeros((128 - 2 * HG, HD), F32)], axis=0).astype(BF)
    inside = lax.broadcasted_iota(jnp.int32, (width, 128), 0) % part
    place = (inside == lanes_like((width, 128))).astype(F32).astype(BF)
    dw_ref[:, HG * (128 + HD) :] = dot_nn(place, values).astype(BF)


def tail(spot, dq, dkv, weight, pieces, part):
    _, seqs, rows, _ = dq.shape
    tokens, width = pieces[0].shape
    local = pl.BlockSpec(memory_space=pltpu.VMEM)
    return pl.pallas_call(
        functools.partial(tail_kernel, rows, part),
        in_specs=[pl.BlockSpec(memory_space=pltpu.SMEM)] + [local] * 11,
        out_specs=[local, local, local],
        out_shape=[
            jax.ShapeDtypeStruct((2, 2, tokens, width), BF),
            jax.ShapeDtypeStruct((2, 2, tokens, width), BF),
            jax.ShapeDtypeStruct((width, 640), BF),
        ],
        compiler_params=pltpu.CompilerParams(vmem_limit_bytes=VMEM_LIMIT),
        cost_estimate=pl.CostEstimate(flops=16 * tokens * width * 480, bytes_accessed=16 << 20, transcendentals=0),
        name="tail",
    )(spot, dq, dkv, weight, *pieces)


def finish_kernel(fold, *refs):
    blocks, (in_ref, down_ref, out_ref, note_ref) = refs[:-4], refs[-4:]
    part, width = out_ref.shape
    hidden = fold * width
    piece = width // fold

    def total(at, size):
        value = blocks[0][:, at : at + size].astype(F32)
        for block in blocks[1:]:
            value = value + block[:, at : at + size].astype(F32)
        return value

    row = lax.broadcasted_iota(jnp.int32, (piece, width), 0)
    for k in range(fold):
        target = row // part * (fold * part) + k * part + row % part
        move = (lanes_like((piece, width)) == target).astype(F32).astype(BF)
        value = total(k * width, width)
        high = value.astype(BF)
        rest = (value - high.astype(F32)).astype(BF)
        for o in range(fold):
            cols = slice(o * piece, (o + 1) * piece)
            placed = dot_nn(high[:, cols], move) + dot_nn(rest[:, cols], move)
            to = slice(o * width, (o + 1) * width)
            in_ref[:, to] = placed if k == 0 else in_ref[:, to] + placed
        down_ref[k] = total(hidden + k * width, width)
    out_ref[...] = total(2 * hidden, width)
    note_ref[...] = total(2 * hidden + width, 128)


def finish(blocks, fold, width):
    part = blocks[0].shape[0]
    local = pl.BlockSpec(memory_space=pltpu.VMEM)
    return pl.pallas_call(
        functools.partial(finish_kernel, fold),
        in_specs=[local] * len(blocks),
        out_specs=[local] * 4,
        out_shape=[
            jax.ShapeDtypeStruct((part, fold * width), F32),
            jax.ShapeDtypeStruct((fold, part, width), F32),
            jax.ShapeDtypeStruct((part, width), F32),
            jax.ShapeDtypeStruct((part, 128), F32),
        ],
        compiler_params=pltpu.CompilerParams(vmem_limit_bytes=VMEM_LIMIT),
        cost_estimate=pl.CostEstimate(flops=1 << 27, bytes_accessed=2 << 20, transcendentals=0),
        name="finish",
    )(*blocks)


def assemble_kernel(got_ref, grad_ref, note_ref):
    width = grad_ref.shape[1] // 3
    for t in range(TP):
        total = got_ref[0, t].astype(F32)
        for i in range(1, got_ref.shape[0]):
            total = total + got_ref[i, t].astype(F32)
        at = t * HG * HD
        grad_ref[:, at : at + HG * HD] = total[:, HG * 128 : HG * (128 + HD)]
        for h in range(HG):
            for j in range(2):
                to = (1 + j) * width + at + h * HD
                grad_ref[:, to : to + HD] = total[:, h * 128 + j * HD : h * 128 + (j + 1) * HD]
        note_ref[t] = total[:, HG * (128 + HD) :]


def assemble(got):
    _, _, part, _ = got.shape
    local = pl.BlockSpec(memory_space=pltpu.VMEM)
    return pl.pallas_call(
        assemble_kernel,
        in_specs=[local],
        out_specs=[local, local],
        out_shape=[
            jax.ShapeDtypeStruct((part, 3 * H * HD), F32),
            jax.ShapeDtypeStruct((TP, part, HD), F32),
        ],
        compiler_params=pltpu.CompilerParams(vmem_limit_bytes=VMEM_LIMIT),
        name="assemble",
    )(got)


def swap_on(axis):
    return lambda v: lax.ppermute(v, axis, [(0, 1), (1, 0)])


def crossing(first):
    pairs = []
    for u in range(2):
        for y in range(2):
            for c in range(2):
                along_u = (c == 0) == first
                to = (1 - u, y, c) if along_u else (u, 1 - y, c)
                pairs.append(((u * 2 + y) * 2 + c, (to[0] * 2 + to[1]) * 2 + to[2]))
    return lambda v: lax.ppermute(v, ("u", "y", "c"), pairs)


def after(v, *earlier):
    return lax.optimization_barrier((v,) + earlier)[0]


def add(a, b):
    return (a.astype(F32) + b.astype(F32)).astype(BF)


def pick(v, index, axis):
    return lax.dynamic_index_in_dim(v, index, axis, keepdims=False)


def put(buffer, v, index):
    return lax.dynamic_update_index_in_dim(buffer, v, index, 0)


def per_device(layer_input, wqkv, wo, wi, wd, biases, hidden_bias, gains, shifts, cotangent, block_ids, offsets, pairing):
    seqs, rows, width = layer_input.shape
    devices = lax.axis_size(ALL)
    ring = lax.axis_size("r")
    shards = ring * TP
    half = shards * rows
    tokens = seqs * rows
    me_u, me_r, me_y, me_c = (lax.axis_index(a) for a in ALL)
    me_t = me_y * 2 + me_c
    part = wqkv.shape[0]
    hidden = wi.shape[1]
    fold = hidden // width
    swap_u, swap_c = swap_on("u"), swap_on("c")
    cross_one, cross_two = crossing(True), crossing(False)
    forward = [(i, (i + 1) % ring) for i in range(ring)]

    notes = [biases[2:].T, gains.T, shifts.T, hidden_bias.reshape(fold, part).T]
    notes = jnp.concatenate(notes + [jnp.zeros((part, 128 - 6 - fold), BF)], axis=1)
    wi_turned = wi.reshape(part, devices, fold, part).transpose(0, 2, 1, 3).reshape(part, hidden)
    wd_cols = [wd[k * part : (k + 1) * part] for k in range(fold)]
    dense_own = jnp.concatenate([wo, wi_turned] + wd_cols + [notes], axis=1)

    by_head = wqkv.reshape(part, 3, TP, HG, HD)
    blocks_kv = by_head[:, 1:].transpose(2, 0, 3, 1, 4).reshape(TP, part, HG * 128)
    blocks_q = by_head[:, 0].transpose(1, 0, 2, 3).reshape(TP, part, HG * HD)
    ends = jnp.pad(biases[:2].T, ((0, 0), (0, HD - 2)))
    blocks = jnp.concatenate([blocks_kv, blocks_q, jnp.broadcast_to(ends, (TP, part, HD))], axis=2)
    blocks = lax.all_to_all(blocks, ("y", "c"), split_axis=0, concat_axis=0, tiled=True)
    column = put(jnp.zeros((ring,) + blocks.shape, BF), blocks, me_r)
    for k in range(1, ring):
        got = lax.ppermute(blocks, "r", [(i, (i + k) % ring) for i in range(ring)])
        column = put(column, got, (me_r - k) % ring)
    early = (cross_one(layer_input.reshape(tokens, width)), cross_two(layer_input.reshape(tokens, width)))
    column = after(column, *early)
    dense = lax.all_gather(after(dense_own, column), ALL, axis=0, tiled=True)
    both = jnp.zeros((2,) + column.shape, BF)
    w_here = put(put(both, column, me_u), swap_u(column), 1 - me_u).reshape(width, 640)
    b_heads = w_here[:, 576:578].astype(F32)
    b_heads = lax.dynamic_slice_in_dim(b_heads, me_t * HG * HD, HG * HD, 0).T
    b_kv = jnp.concatenate([jnp.zeros((HG, HD), F32), b_heads[1].reshape(HG, HD)], axis=1).reshape(-1)
    b_here = jnp.concatenate([b_kv, b_heads[0], jnp.zeros((HD,), F32)])
    b_here = jnp.broadcast_to(b_here, (8, 640))

    x_own = layer_input.reshape(tokens, width)
    piece = x_own
    stages = []
    for k in range(ring):
        if k == 1:
            piece, column = lax.optimization_barrier((piece, column))
        if k:
            piece = lax.ppermute(piece, "r", forward)
        if k >= 2:
            piece, stages[k - 2] = lax.optimization_barrier((piece, stages[k - 2]))
        one, two = early if k == 0 else (cross_one(piece), cross_two(piece))
        if k == 1:
            one, w_here = lax.optimization_barrier((one, w_here))
        three = cross_two(one)
        if k >= 2:
            three, stages[k - 1] = lax.optimization_barrier((three, stages[k - 1]))
        mine = [piece, one, two, three]
        theirs = [swap_c(m) for m in mine]
        if k == 0:
            x_near = (mine, theirs)
        spot = jnp.stack([me_u, me_y, me_c, (me_r - k) % ring]).astype(jnp.int32)
        stages.append(project(mine + theirs, w_here, b_here, spot, stages[-1] if stages else None, ring, seqs, rows))
    buffers = stages[-1]
    kv = buffers[0].reshape(2, shards, seqs, rows, HG * 128)
    q_all = buffers[1].reshape(shards, seqs, rows, HG * 128)

    pair = lax.dynamic_slice_in_dim(pick(pairing, me_u, 1), me_t * HG, HG, 0)
    ids = block_ids.reshape(seqs, 2, half)
    ids_own = pick(ids, me_u, 1)
    ends = jnp.sum((ids[:, :, None, :] <= ids_own[:, None, :, None]).astype(jnp.int32), axis=-1)
    end_all = jnp.where((pair == 0)[None, :, None], ends[:, 0:1], ends[:, 1:2])
    end_loc = lax.dynamic_slice_in_dim(end_all, me_r * TP * rows, TP * rows, 2)
    begin = jnp.maximum(offsets[:, None] - pair[None, :] * half, 0).reshape(-1)
    last = jnp.concatenate([end_loc[:, :, -1].reshape(-1), me_r[None].astype(jnp.int32)])
    start = me_r * TP * rows
    end_ring = end_all.reshape(seqs, HG, ring, TP * rows)
    end_row_own = end_loc[:, :, None]

    att = attend_forward(q_all, kv, pair, begin, last, end_row_own)
    att = lax.all_to_all(att, ("y", "c"), split_axis=0, concat_axis=0, tiled=True).reshape(TP, tokens, 256)

    index = jnp.arange(width, dtype=jnp.int32)
    inner_at, index = index % part, index // part
    r_rel, index = index % ring, index // ring
    s_rel, f_rel, c_rel = index % 2, index // 2 % 2, index // 4
    core = me_c ^ c_rel
    to_u = me_u ^ jnp.where(core == 0, f_rel, s_rel)
    to_y = me_y ^ jnp.where(core == 0, s_rel, f_rel)
    order = (((to_u * ring + (me_r + r_rel) % ring) * 2 + to_y) * 2 + core) * part + inner_at
    order = jnp.broadcast_to(order.astype(jnp.int32), (8, width))
    hidden_out, load, dsum, stay, leave = dense_layers(att, x_own, cotangent.reshape(tokens, width), order, dense, fold)
    hidden_out = hidden_out.reshape(seqs, rows, width)
    came = swap_c(leave)
    cut = width // 4
    high, low = add(stay[cut:], came[cut:]), add(stay[:cut], came[:cut])
    high_first = high
    cut = width // 8
    load = load.reshape(TP, seqs, rows, 256)
    load = lax.all_to_all(load, ("y", "c"), split_axis=0, concat_axis=0, tiled=True)
    came = cross_one(after(high_first, load))
    place = jnp.stack([start, me_r])
    dkv = jnp.zeros((TP, seqs, rows, HG * 128), F32)
    moving = load
    done = []
    for k in range(ring):
        if k >= 2:
            moving, done[k - 2] = lax.optimization_barrier((moving, done[k - 2]))
        if k:
            moving = lax.ppermute(moving, "r", forward)
        source = (me_r - k) % ring
        ends_k = pick(end_ring, source, 2)
        where = jnp.concatenate([place, source[None]]).astype(jnp.int32)
        before = done[-1] if done else dkv
        if k == 2:
            dq = attend_query(q_all, kv, pair, begin, last, end_row_own, after(load, high_first, moving))
        if k == ring - 1:
            before = after(before, dq)
        if k == ring - 2:
            came = after(came, done[1], moving)
            high2, low2 = add(low[cut:], came[cut:]), add(low[:cut], came[:cut])
            stay = add(low2, cross_two(high2))
            before = after(before, high2)
        done.append(attend_key(q_all, moving, kv, pair, begin, ends_k[:, :, -1].reshape(-1), where, ends_k[:, :, None], before))

    summed = stay[:part].astype(F32)
    for j in range(1, ring):
        along = [(i, (i + j) % ring) for i in range(ring)]
        summed = summed + lax.ppermute(stay[j * part : (j + 1) * part], "r", along).astype(F32)
    spot = jnp.concatenate([jnp.stack([me_u, me_y, me_c]), (pair == me_u).astype(jnp.int32)])
    keep, send, dw = tail(spot.astype(jnp.int32), dq, done[-1], w_here, x_near[0] + x_near[1], part)
    keep = add(keep, swap_c(send))
    dw = after(dw, keep)
    got = lax.all_to_all(dw.reshape(devices, part, 640), ALL, split_axis=0, concat_axis=0, tiled=True)
    came = cross_one(keep[1])
    onward = add(keep[0, 1], came[1])
    final = cross_two(onward)
    grad_w_in, grad_w_down, grad_w_out, flat = finish([after(summed, onward)], fold, width)
    grad_w_down = grad_w_down.reshape(fold * part, width)
    flat = flat[:, : 6 + fold].T
    grad_bo, grad_gains, grad_shifts, grad_bin = flat[0:2], flat[2:4], flat[4:6], flat[6:].reshape(-1)

    grad_input = dsum + keep[0, 0].astype(F32) + came[0].astype(F32) + final.astype(F32)
    grad_input = grad_input.astype(BF).reshape(seqs, rows, width)
    grad_w_qkv, note = assemble(after(got, final).reshape(2 * ring, TP, part, 640))
    at = lax.axis_index(ALL) * part
    grad_bq = lax.dynamic_slice_in_dim(note[:, :HG].reshape(width), at, part, 0)
    grad_bv = lax.dynamic_slice_in_dim(note[:, HG : 2 * HG].reshape(width), at, part, 0)
    grad_biases = jnp.concatenate([jnp.stack([grad_bq, grad_bv]), grad_bo])
    return (hidden_out, grad_input, grad_w_qkv, grad_w_out, grad_w_in, grad_w_down, grad_biases, grad_bin, grad_gains, grad_shifts)


def solution(mesh):
    wide = mesh.shape["blk"]
    grid = Mesh(mesh.devices.reshape(2, wide // TP, 2, TP // 2), ALL)
    rows2, cols1 = P(ALL, None), P(None, ALL)
    toks = P(None, ALL, None)
    return jax.shard_map(
        per_device,
        mesh=grid,
        in_specs=(toks, rows2, rows2, rows2, rows2, cols1, P(ALL), cols1, cols1, toks, P(), P(), P()),
        out_specs=(toks, toks, rows2, rows2, rows2, rows2, cols1, P(ALL), cols1, cols1),
        check_vma=False,
    )
```

```python
import functools

import jax
import jax.numpy as jnp
from jax import lax
from jax.experimental import pallas as pl
from jax.experimental.pallas import tpu as pltpu
from jax.sharding import Mesh
from jax.sharding import PartitionSpec as P

H = 12
HD = 64
TP = 4
HG = H // TP
NORM_EPS = 1e-12
FILL = -1e30
FLOOR = -1e29
ALL = ("u", "r", "y", "c")
BF = jnp.bfloat16
F32 = jnp.float32
VMEM_LIMIT = 56 * 1024 * 1024


def split_three(v):
    high = v.astype(BF)
    v = v - high.astype(F32)
    middle = v.astype(BF)
    return high, middle, (v - middle.astype(F32)).astype(BF)


def dot_nt(a, b):
    return lax.dot_general(a, b, (((1,), (1,)), ((), ())), preferred_element_type=F32)


def dot_nn(a, b):
    return lax.dot_general(a, b, (((1,), (0,)), ((), ())), preferred_element_type=F32)


def dot_tn(a, b):
    return lax.dot_general(a, b, (((0,), (0,)), ((), ())), preferred_element_type=F32)


def lanes_like(shape):
    return lax.broadcasted_iota(jnp.int32, shape, len(shape) - 1)


def chooser(h, kind, depth):
    at = HD + kind * 3 * HG + 3 * h
    lane = lanes_like((depth, 128))
    return jnp.where((lane >= at) & (lane < at + 3), -1.0, 0.0).astype(BF)


def chunk_of(shards):
    return 16 if shards % 16 == 0 else shards


def key_spots(first, count, begin, end_row):
    spot = lax.broadcasted_iota(jnp.int32, (count, 1), 0) + first
    return jnp.where(spot >= begin, spot, 1 << 30) < end_row


def forward_kernel(rows, shards, pair_ref, begin_ref, last_ref, q_ref, kv0, kv1, kv2, end_ref, att_ref, m_ref, l_ref, acc_ref):
    seq = pl.program_id(0)
    group = chunk_of(shards)
    nq = TP * rows
    width = group * rows
    for h in range(HG):
        m_ref[h] = jnp.full((1, nq), FLOOR, F32)
        l_ref[h] = jnp.zeros((1, nq), F32)
        acc_ref[h] = jnp.zeros((128, nq), F32)

    def step(c, _):
        for h, kv_ref in enumerate((kv0, kv1, kv2)):
            query = q_ref[:, 0, :, h * 128 : (h + 1) * 128].reshape(nq, 128)
            kv = kv_ref[0, pl.ds(c * group, group), 0].reshape(width, 128)
            seen = key_spots(c * width, width, begin_ref[seq * HG + h], end_ref[0, h])
            scores = jnp.where(seen, dot_nt(kv, query), FILL)
            old = m_ref[h]
            new = jnp.maximum(old, jnp.max(scores, axis=0, keepdims=True))
            weights = jnp.exp(scores - new)
            factor = jnp.exp(old - new)
            m_ref[h] = new
            l_ref[h] = l_ref[h] * factor + jnp.sum(weights, axis=0, keepdims=True)
            acc_ref[h] = acc_ref[h] * factor + dot_tn(kv, weights.astype(BF))
        return 0

    trips = [pl.cdiv(last_ref[seq * HG + h], width) for h in range(HG)]
    lax.fori_loop(0, functools.reduce(jnp.maximum, trips), step, 0)
    turn = lax.broadcasted_iota(jnp.int32, (HD, nq), 0)
    notes = jnp.zeros((HD, nq), F32)
    for h in range(HG):
        total = jnp.maximum(l_ref[h], 1.0)
        for p, value in enumerate(split_three(m_ref[h] + jnp.log(total))):
            notes = jnp.where(turn == 3 * HG + 3 * h + p, value.astype(F32), notes)
        att = (acc_ref[h] / total)[HD:].T.astype(BF)
        att_ref[:, 0, :, h * HD : (h + 1) * HD] = att.reshape(TP, rows, HD)
    att_ref[:, 0, :, HG * HD :] = notes.T.astype(BF).reshape(TP, rows, HD)


def output_gradient(load_ref, h, count):
    dout = load_ref[:, 0, :, h * HD : (h + 1) * HD].reshape(count, HD)
    return jnp.concatenate([jnp.zeros_like(dout), dout], axis=1)


def query_kernel(rows, shards, pair_ref, begin_ref, last_ref, q_ref, kv0, kv1, kv2, end_ref, load_ref, dq_ref, acc_ref):
    seq = pl.program_id(0)
    group = chunk_of(shards)
    nq = TP * rows
    width = group * rows
    notes = load_ref[:, 0, :, 128:].reshape(nq, 128)
    acc_ref[...] = jnp.zeros_like(acc_ref)

    def step(c, _):
        for h, kv_ref in enumerate((kv0, kv1, kv2)):
            query = q_ref[:, 0, :, h * 128 : (h + 1) * 128].reshape(nq, 128)
            kv = kv_ref[0, pl.ds(c * group, group), 0].reshape(width, 128)
            seen = key_spots(c * width, width, begin_ref[seq * HG + h], end_ref[0, h])
            query = jnp.concatenate([query, notes], axis=1)
            dout = jnp.concatenate([output_gradient(load_ref, h, nq), notes], axis=1)
            scores = dot_nt(jnp.concatenate([kv, chooser(h, 1, width)], axis=1), query)
            prob = jnp.exp(jnp.where(seen, scores, FILL))
            dprob = dot_nt(jnp.concatenate([kv, chooser(h, 0, width)], axis=1), dout)
            acc_ref[h] += dot_tn(kv, (prob * dprob).astype(BF))
        return 0

    trips = [pl.cdiv(last_ref[seq * HG + h], width) for h in range(HG)]
    lax.fori_loop(0, functools.reduce(jnp.maximum, trips), step, 0)
    for h in range(HG):
        dq = (acc_ref[h][:HD] * (HD**-0.5)).T.astype(BF)
        dq_ref[:, 0, :, h * HD : (h + 1) * HD] = dq.reshape(TP, rows, HD)


def key_kernel(rows, pair_ref, begin_ref, reach_ref, place_ref, q_ref, load_ref, kv0, kv1, kv2, end_ref, old_ref, dkv_ref):
    seq = pl.program_id(0)
    span = TP * rows
    start = place_ref[0]
    reach = [reach_ref[seq * HG + h] for h in range(HG)]
    needed = functools.reduce(jnp.maximum, reach) > start

    @pl.when(needed)
    def _():
        notes = load_ref[:, 0, :, 128:].reshape(span, 128)
        for h, kv_ref in enumerate((kv0, kv1, kv2)):
            lanes = slice(h * 128, (h + 1) * 128)
            kv = kv_ref[0, :, 0].reshape(span, 128)
            query = q_ref[:, 0, :, lanes].reshape(span, 128)
            dout = output_gradient(load_ref, h, span)
            seen = key_spots(start, span, begin_ref[seq * HG + h], end_ref[0, h])
            scores = dot_nt(jnp.concatenate([kv, chooser(h, 1, span)], axis=1), jnp.concatenate([query, notes], axis=1))
            prob = jnp.exp(jnp.where(seen, scores, FILL))
            dprob = dot_nt(jnp.concatenate([kv, chooser(h, 0, span)], axis=1), jnp.concatenate([dout, notes], axis=1))
            sides = jnp.concatenate([(prob * dprob).astype(BF), prob.astype(BF)], axis=1)
            new = dot_nn(sides, jnp.concatenate([query, dout], axis=0))
            dkv_ref[:, 0, :, lanes] = old_ref[:, 0, :, lanes] + new.reshape(TP, rows, 128)

    @pl.when(jnp.logical_not(needed))
    def _():
        dkv_ref[...] = old_ref[...]


def project_kernel(seqs, rows, fresh, spot_ref, *refs):
    pieces, w_ref, bias_ref = refs[:8], refs[8], refs[9]
    kv_out, q_out, kv_tmp, q_tmp, kv_sem, q_sem = refs[10 if fresh else 12 :]
    keys = HG * 128
    tokens = seqs * rows
    me_u, me_y, me_c, source = (spot_ref[i] for i in range(4))
    for which in range(2):
        core = me_c if which == 0 else 1 - me_c
        x = jnp.concatenate([pieces[which * 4 + i][...] for i in range(4)], axis=0)
        if which == 0:
            q_tmp[...] = jnp.zeros_like(q_tmp)
        kv = (dot_nn(x, w_ref[:, :keys]) + bias_ref[0:1, :keys]).astype(BF)
        for i in range(4):
            p, q = i // 2, i % 2
            x_rel = jnp.where(core == 0, q, p)
            y_rel = jnp.where(core == 0, p, q)
            shard = jnp.bitwise_xor(me_y, y_rel) * 2 + core
            slot = which * 4 + i
            kv_tmp[slot] = kv[i * tokens : (i + 1) * tokens].reshape(seqs, rows, keys)
            spot = kv_out.at[jnp.bitwise_xor(me_u, x_rel), source, shard]
            pltpu.make_async_copy(kv_tmp.at[slot], spot, kv_sem.at[slot]).start()
        second = jnp.where(core == 0, x[2 * tokens : 3 * tokens], x[tokens : 2 * tokens])
        for y_rel, part in enumerate((x[:tokens], second)):
            query = (dot_nn(part, w_ref[:, keys:]) + bias_ref[0:1, keys:]) * (HD**-0.5)
            slot = which * 2 + y_rel
            query = query.astype(BF)
            for h in range(HG):
                q_tmp[slot, :, :, h * 128 : h * 128 + HD] = query[:, h * HD : (h + 1) * HD].reshape(seqs, rows, HD)
            shard = jnp.bitwise_xor(me_y, y_rel) * 2 + core
            pltpu.make_async_copy(q_tmp.at[slot], q_out.at[source, shard], q_sem.at[slot]).start()
    for slot in range(8):
        pltpu.make_async_copy(kv_tmp.at[slot], kv_out.at[0, 0, 0], kv_sem.at[slot]).wait()
    for slot in range(4):
        pltpu.make_async_copy(q_tmp.at[slot], q_out.at[0, 0], q_sem.at[slot]).wait()


def project(pieces, weight, bias, spot, buffers, ring, seqs, rows):
    keys = HG * 128
    width = weight.shape[0]
    tokens = seqs * rows
    extra = [] if buffers is None else list(buffers)
    anywhere = pl.BlockSpec(memory_space=pl.ANY)
    local = pl.BlockSpec(memory_space=pltpu.VMEM)
    return pl.pallas_call(
        functools.partial(project_kernel, seqs, rows, not extra),
        in_specs=[pl.BlockSpec(memory_space=pltpu.SMEM)] + [local] * 10 + [anywhere] * len(extra),
        out_specs=[anywhere, anywhere],
        scratch_shapes=[
            pltpu.VMEM((8, seqs, rows, keys), BF),
            pltpu.VMEM((4, seqs, rows, keys), BF),
            pltpu.SemaphoreType.DMA((8,)),
            pltpu.SemaphoreType.DMA((4,)),
        ],
        out_shape=[
            jax.ShapeDtypeStruct((2, ring, TP, seqs, rows, keys), BF),
            jax.ShapeDtypeStruct((ring, TP, seqs, rows, keys), BF),
        ],
        input_output_aliases={11: 0, 12: 1} if extra else {},
        compiler_params=pltpu.CompilerParams(vmem_limit_bytes=VMEM_LIMIT),
        cost_estimate=pl.CostEstimate(flops=12 * tokens * width * keys * 2, bytes_accessed=12 << 20, transcendentals=0),
        name="project",
    )(spot, *pieces, weight, bias, *extra)


def keys_spec(h, shards, rows):
    return pl.BlockSpec((1, shards, 1, rows, 128), lambda s, pair, *_: (pair[h], 0, s, 0, h))


def attend_forward(q_all, kv, pair, begin, last, end_row_own):
    _, shards, seqs, rows, _ = kv.shape
    nq = TP * rows
    row_spec = pl.BlockSpec((TP, 1, rows, 384), lambda s, pair, begin, last: (last[seqs * HG], s, 0, 0))
    end_spec = pl.BlockSpec((1, HG, 1, nq), lambda s, *_: (s, 0, 0, 0))
    return pl.pallas_call(
        functools.partial(forward_kernel, rows, shards),
        grid_spec=pltpu.PrefetchScalarGridSpec(
            num_scalar_prefetch=3,
            grid=(seqs,),
            in_specs=[row_spec] + [keys_spec(h, shards, rows) for h in range(HG)] + [end_spec],
            out_specs=pl.BlockSpec((TP, 1, rows, 256), lambda s, *_: (0, s, 0, 0)),
            scratch_shapes=[pltpu.VMEM((HG, 1, nq), F32), pltpu.VMEM((HG, 1, nq), F32), pltpu.VMEM((HG, 128, nq), F32)],
        ),
        out_shape=jax.ShapeDtypeStruct((TP, seqs, rows, 256), BF),
        compiler_params=pltpu.CompilerParams(vmem_limit_bytes=VMEM_LIMIT),
        cost_estimate=pl.CostEstimate(flops=4 * 9 * nq * shards * rows * 128, bytes_accessed=12 << 20, transcendentals=0),
        name="attend_forward",
    )(pair, begin, last, q_all, kv, kv, kv, end_row_own)


def attend_query(q_all, kv, pair, begin, last, end_row_own, load):
    _, shards, seqs, rows, _ = kv.shape
    nq = TP * rows
    row_spec = pl.BlockSpec((TP, 1, rows, 384), lambda s, pair, begin, last: (last[seqs * HG], s, 0, 0))
    end_spec = pl.BlockSpec((1, HG, 1, nq), lambda s, *_: (s, 0, 0, 0))
    return pl.pallas_call(
        functools.partial(query_kernel, rows, shards),
        grid_spec=pltpu.PrefetchScalarGridSpec(
            num_scalar_prefetch=3,
            grid=(seqs,),
            in_specs=[row_spec]
            + [keys_spec(h, shards, rows) for h in range(HG)]
            + [end_spec, pl.BlockSpec((TP, 1, rows, 256), lambda s, *_: (0, s, 0, 0))],
            out_specs=pl.BlockSpec((TP, 1, rows, HG * HD), lambda s, *_: (0, s, 0, 0)),
            scratch_shapes=[pltpu.VMEM((HG, 128, nq), F32)],
        ),
        out_shape=jax.ShapeDtypeStruct((TP, seqs, rows, HG * HD), BF),
        compiler_params=pltpu.CompilerParams(vmem_limit_bytes=VMEM_LIMIT),
        cost_estimate=pl.CostEstimate(flops=6 * 9 * nq * shards * rows * 128, bytes_accessed=12 << 20, transcendentals=0),
        name="attend_query",
    )(pair, begin, last, q_all, kv, kv, kv, end_row_own, load)


def attend_key(q_all, load, kv, pair, begin, reach, place, end_row, old):
    _, shards, seqs, rows, _ = kv.shape

    def own_keys(h):
        return pl.BlockSpec((1, TP, 1, rows, 128), lambda s, pair, begin, reach, place: (pair[h], place[1], s, 0, h))

    total = pl.BlockSpec((TP, 1, rows, 384), lambda s, *_: (0, s, 0, 0))
    return pl.pallas_call(
        functools.partial(key_kernel, rows),
        grid_spec=pltpu.PrefetchScalarGridSpec(
            num_scalar_prefetch=4,
            grid=(seqs,),
            in_specs=[
                pl.BlockSpec((TP, 1, rows, 384), lambda s, pair, begin, reach, place: (place[2], s, 0, 0)),
                pl.BlockSpec((TP, 1, rows, 256), lambda s, *_: (0, s, 0, 0)),
            ]
            + [own_keys(h) for h in range(HG)]
            + [pl.BlockSpec((1, HG, 1, TP * rows), lambda s, *_: (s, 0, 0, 0)), total],
            out_specs=total,
        ),
        out_shape=jax.ShapeDtypeStruct((TP, seqs, rows, 384), F32),
        input_output_aliases={10: 0},
        compiler_params=pltpu.CompilerParams(vmem_limit_bytes=VMEM_LIMIT),
        cost_estimate=pl.CostEstimate(flops=8 * 9 * (TP * rows) ** 2 * 128, bytes_accessed=8 << 20, transcendentals=0),
        name="attend_key",
    )(pair, begin, reach, place, q_all, load, kv, kv, kv, end_row, old)


def norm_parts(summed):
    centred = summed - jnp.mean(summed, axis=1, keepdims=True)
    inv_std = lax.rsqrt(jnp.mean(centred * centred, axis=1, keepdims=True) + NORM_EPS)
    return centred * inv_std, inv_std


def dense_kernel(fold, att_ref, x_ref, cot_ref, order_ref, dense_ref, out_ref, load_ref, dsum_ref, keep_ref, send_ref, w, note, grad, grad_note, act, slope, turn, in_sem, out_sem):
    tokens, width = x_ref.shape
    blocks = 2 * fold + 1

    def fetch(b):
        wide = pl.ds(b * width, width) if b < blocks else pl.ds(blocks * width, 128)
        return pltpu.make_async_copy(dense_ref.at[:, wide], w.at[b] if b < blocks else note, in_sem.at[b])

    def ship(b, side):
        wide = pl.ds(b * width, width) if b < blocks else pl.ds(blocks * width, 128)
        rows = pl.ds(side * (width // 2), width // 2)
        source = grad.at[b, rows] if b < blocks else grad_note.at[rows]
        return pltpu.make_async_copy(source, (send_ref if side else keep_ref).at[:, wide], out_sem.at[2 * b + side])

    def start_ship(b):
        ship(b, 0).start()
        ship(b, 1).start()

    for b in [0, blocks] + list(range(1, blocks)):
        fetch(b).start()
    att = jnp.concatenate([att_ref[t, :, : HG * HD] for t in range(TP)], axis=1)
    row = lax.broadcasted_iota(jnp.int32, (width, width), 0)
    turn[...] = (row == order_ref[0:1]).astype(F32).astype(BF)

    def turned(v):
        return dot_nn(v, turn[...]).astype(BF)

    fetch(0).wait()
    fetch(blocks).wait()
    vec = note[...].astype(F32).T
    gain_one, gain_two, shift_one, shift_two = (vec[i : i + 1] for i in range(2, 6))
    normed_one, inv_one = norm_parts(x_ref[...].astype(F32) + dot_nn(att, w[0]) + vec[0:1])
    mid = normed_one * gain_one + shift_one
    mid_low = mid.astype(BF)
    feed = mid + vec[1:2]
    for k in range(fold):
        fetch(1 + k).wait()
        inner = dot_nn(mid_low, w[1 + k]) + vec[6 + k : 7 + k]
        spread = 0.5 + 0.5 * lax.erf(inner * (0.5**0.5))
        act[k] = (inner * spread).astype(BF)
        slope[k] = spread + inner * (jnp.exp(-0.5 * inner * inner) * 0.3989422804014327)
    for k in range(fold):
        fetch(1 + fold + k).wait()
        feed = feed + dot_nn(act[k], w[1 + fold + k])
    normed_two, inv_two = norm_parts(feed)
    out_ref[...] = (normed_two * gain_two + shift_two).astype(BF)
    grad_out = cot_ref[...].astype(F32)

    def back(incoming, normed, inv_std, gain):
        scaled = incoming * gain
        along = jnp.mean(scaled * normed, axis=1, keepdims=True)
        return inv_std * (scaled - jnp.mean(scaled, axis=1, keepdims=True) - normed * along)

    def total(v):
        return jnp.sum(v, axis=0, keepdims=True)

    dsecond = back(grad_out, normed_two, inv_two, gain_two)
    dfeed = dsecond.astype(BF)
    sums = [None, total(dfeed.astype(F32)), None, total(grad_out * normed_two), None, total(grad_out)]
    dmid = dsecond
    mid_turned = turned(mid_low)
    for k in range(fold):
        dinner = (dot_nt(dfeed, w[1 + fold + k]) * slope[k]).astype(BF)
        sums.append(total(dinner.astype(F32)))
        grad[k] = dot_tn(mid_turned, dinner).astype(BF)
        start_ship(k)
        grad[fold + k] = dot_tn(turned(act[k]), dfeed).astype(BF)
        start_ship(fold + k)
        dmid = dmid + dot_nt(dinner, w[1 + k])
    dsum = back(dmid, normed_one, inv_one, gain_one)
    dsum_ref[...] = dsum
    dproj = dsum.astype(BF)
    sums[0], sums[2], sums[4] = total(dproj.astype(F32)), total(dmid * normed_one), total(dmid)
    datt = dot_nt(dproj, w[0]).astype(BF)
    product = datt.astype(F32) * att.astype(F32)
    high = product.astype(BF)
    rest = (product - high.astype(F32)).astype(BF)
    feature = lax.broadcasted_iota(jnp.int32, (width, 128), 0)
    lane = lanes_like((width, 128))
    third = lanes_like((tokens, HD)) % 3
    for t in range(TP):
        of_head = ((feature // HD == t * HG + lane // 3) & (lane < 3 * HG)).astype(F32).astype(BF)
        delta = (dot_nn(high, of_head) + dot_nn(rest, of_head))[:, :HD]
        one, two, three = (v.astype(F32) for v in split_three(delta))
        notes = jnp.where(third == 0, one, jnp.where(third == 1, two, three))
        load_ref[t, :, : HG * HD] = datt[:, t * HG * HD : (t + 1) * HG * HD]
        load_ref[t, :, HG * HD :] = (notes + att_ref[t, :, HG * HD :].astype(F32)).astype(BF)
    grad[2 * fold] = dot_tn(turned(att), dproj).astype(BF)
    start_ship(2 * fold)
    table = jnp.concatenate(sums + [jnp.zeros((128 - len(sums), width), F32)], axis=0)
    grad_note[...] = dot_nn(table.astype(BF), turn[...]).T.astype(BF)
    start_ship(blocks)
    for b in range(blocks + 1):
        ship(b, 0).wait()
        ship(b, 1).wait()


def dense_layers(att, x, cotangent, order, dense, fold):
    tokens, width = x.shape
    blocks = 2 * fold + 1
    local = pl.BlockSpec(memory_space=pltpu.VMEM)
    anywhere = pl.BlockSpec(memory_space=pl.ANY)
    return pl.pallas_call(
        functools.partial(dense_kernel, fold),
        in_specs=[local, local, local, local, anywhere],
        out_specs=[local, local, local, anywhere, anywhere],
        out_shape=[
            jax.ShapeDtypeStruct((tokens, width), BF),
            jax.ShapeDtypeStruct((TP, tokens, 256), BF),
            jax.ShapeDtypeStruct((tokens, width), F32),
            jax.ShapeDtypeStruct((width // 2, blocks * width + 128), BF),
            jax.ShapeDtypeStruct((width // 2, blocks * width + 128), BF),
        ],
        scratch_shapes=[
            pltpu.VMEM((blocks, width, width), BF),
            pltpu.VMEM((width, 128), BF),
            pltpu.VMEM((blocks, width, width), BF),
            pltpu.VMEM((width, 128), BF),
            pltpu.VMEM((fold, tokens, width), BF),
            pltpu.VMEM((fold, tokens, width), F32),
            pltpu.VMEM((width, width), BF),
            pltpu.SemaphoreType.DMA((blocks + 1,)),
            pltpu.SemaphoreType.DMA((2 * blocks + 2,)),
        ],
        compiler_params=pltpu.CompilerParams(vmem_limit_bytes=VMEM_LIMIT),
        cost_estimate=pl.CostEstimate(flops=54 * tokens * width * width, bytes_accessed=24 << 20, transcendentals=0),
        name="dense_layers",
    )(att, x, cotangent, order, dense)


def tail_kernel(rows, part, spot_ref, dq_ref, dkv_ref, w_ref, *refs):
    pieces, (keep_ref, send_ref, dw_ref) = refs[:8], refs[8:]
    me_y, me_c = spot_ref[1], spot_ref[2]
    lane = lanes_like((1, HG * 128))
    is_own = jnp.zeros((1, HG * 128), jnp.int32)
    for h in range(HG):
        is_own = jnp.where(lane // 128 == h, spot_ref[3 + h], is_own)
    tokens, width = pieces[0].shape
    own_side, oth_side, near_x, far_x = [], [], [], []
    sum_q = sum_kv = 0.0
    for which, out_ref in enumerate((keep_ref, send_ref)):
        core = me_c if which == 0 else 1 - me_c
        middle = [pieces[4 * which + i][...] for i in (1, 2)]
        for y_rel in range(2):
            shard = jnp.bitwise_xor(me_y, y_rel) * 2 + core
            dq = dq_ref[shard].reshape(tokens, HG * HD)
            dkv = dkv_ref[shard].reshape(tokens, HG * 128)
            own = jnp.concatenate([jnp.where(is_own == 1, dkv, 0.0).astype(BF), dq], axis=1)
            oth = jnp.where(is_own == 1, 0.0, dkv).astype(BF)
            sum_q = sum_q + jnp.sum(dq.astype(F32), axis=0, keepdims=True)
            sum_kv = sum_kv + jnp.sum(dkv.astype(BF).astype(F32), axis=0, keepdims=True)
            to_own = dot_nt(own, w_ref[:, : HG * (128 + HD)]).astype(BF)
            to_oth = dot_nt(oth, w_ref[:, : HG * 128]).astype(BF)
            for x_rel, value in enumerate((to_own, to_oth)):
                out_ref[jnp.where(core == 0, x_rel, y_rel), jnp.where(core == 0, y_rel, x_rel)] = value
            own_side.append(own)
            oth_side.append(oth)
            first, last = pieces[4 * which][...], pieces[4 * which + 3][...]
            one = jnp.where(core == 0, middle[0], middle[1])
            two = jnp.where(core == 0, middle[1], middle[0])
            near_x.append(first if y_rel == 0 else two)
            far_x.append(one if y_rel == 0 else last)
    near = dot_tn(jnp.concatenate(near_x, axis=0), jnp.concatenate(own_side, axis=0))
    far = dot_tn(jnp.concatenate(far_x, axis=0), jnp.concatenate(oth_side, axis=0))
    dw_ref[:, : HG * 128] = (near[:, : HG * 128] + far).astype(BF)
    dw_ref[:, HG * 128 : HG * (128 + HD)] = near[:, HG * 128 :].astype(BF)
    values = [sum_q[:, h * HD : (h + 1) * HD] for h in range(HG)]
    values += [sum_kv[:, h * 128 + HD : (h + 1) * 128] for h in range(HG)]
    values = jnp.concatenate(values + [jnp.zeros((128 - 2 * HG, HD), F32)], axis=0).astype(BF)
    inside = lax.broadcasted_iota(jnp.int32, (width, 128), 0) % part
    place = (inside == lanes_like((width, 128))).astype(F32).astype(BF)
    dw_ref[:, HG * (128 + HD) :] = dot_nn(place, values).astype(BF)


def tail(spot, dq, dkv, weight, pieces, part):
    _, seqs, rows, _ = dq.shape
    tokens, width = pieces[0].shape
    local = pl.BlockSpec(memory_space=pltpu.VMEM)
    return pl.pallas_call(
        functools.partial(tail_kernel, rows, part),
        in_specs=[pl.BlockSpec(memory_space=pltpu.SMEM)] + [local] * 11,
        out_specs=[local, local, local],
        out_shape=[
            jax.ShapeDtypeStruct((2, 2, tokens, width), BF),
            jax.ShapeDtypeStruct((2, 2, tokens, width), BF),
            jax.ShapeDtypeStruct((width, 640), BF),
        ],
        compiler_params=pltpu.CompilerParams(vmem_limit_bytes=VMEM_LIMIT),
        cost_estimate=pl.CostEstimate(flops=16 * tokens * width * 480, bytes_accessed=16 << 20, transcendentals=0),
        name="tail",
    )(spot, dq, dkv, weight, *pieces)


def finish_kernel(fold, *refs):
    blocks, (in_ref, down_ref, out_ref, note_ref) = refs[:-4], refs[-4:]
    part, width = out_ref.shape
    hidden = fold * width
    piece = width // fold

    def total(at, size):
        value = blocks[0][:, at : at + size].astype(F32)
        for block in blocks[1:]:
            value = value + block[:, at : at + size].astype(F32)
        return value

    row = lax.broadcasted_iota(jnp.int32, (piece, width), 0)
    for k in range(fold):
        target = row // part * (fold * part) + k * part + row % part
        move = (lanes_like((piece, width)) == target).astype(F32).astype(BF)
        value = total(k * width, width)
        high = value.astype(BF)
        rest = (value - high.astype(F32)).astype(BF)
        for o in range(fold):
            cols = slice(o * piece, (o + 1) * piece)
            placed = dot_nn(high[:, cols], move) + dot_nn(rest[:, cols], move)
            to = slice(o * width, (o + 1) * width)
            in_ref[:, to] = placed if k == 0 else in_ref[:, to] + placed
        down_ref[k] = total(hidden + k * width, width)
    out_ref[...] = total(2 * hidden, width)
    note_ref[...] = total(2 * hidden + width, 128)


def finish(blocks, fold, width):
    part = blocks[0].shape[0]
    local = pl.BlockSpec(memory_space=pltpu.VMEM)
    return pl.pallas_call(
        functools.partial(finish_kernel, fold),
        in_specs=[local] * len(blocks),
        out_specs=[local] * 4,
        out_shape=[
            jax.ShapeDtypeStruct((part, fold * width), F32),
            jax.ShapeDtypeStruct((fold, part, width), F32),
            jax.ShapeDtypeStruct((part, width), F32),
            jax.ShapeDtypeStruct((part, 128), F32),
        ],
        compiler_params=pltpu.CompilerParams(vmem_limit_bytes=VMEM_LIMIT),
        cost_estimate=pl.CostEstimate(flops=1 << 27, bytes_accessed=2 << 20, transcendentals=0),
        name="finish",
    )(*blocks)


def assemble_kernel(got_ref, grad_ref, note_ref):
    width = grad_ref.shape[1] // 3
    for t in range(TP):
        total = got_ref[0, t].astype(F32)
        for i in range(1, got_ref.shape[0]):
            total = total + got_ref[i, t].astype(F32)
        at = t * HG * HD
        grad_ref[:, at : at + HG * HD] = total[:, HG * 128 : HG * (128 + HD)]
        for h in range(HG):
            for j in range(2):
                to = (1 + j) * width + at + h * HD
                grad_ref[:, to : to + HD] = total[:, h * 128 + j * HD : h * 128 + (j + 1) * HD]
        note_ref[t] = total[:, HG * (128 + HD) :]


def assemble(got):
    _, _, part, _ = got.shape
    local = pl.BlockSpec(memory_space=pltpu.VMEM)
    return pl.pallas_call(
        assemble_kernel,
        in_specs=[local],
        out_specs=[local, local],
        out_shape=[
            jax.ShapeDtypeStruct((part, 3 * H * HD), F32),
            jax.ShapeDtypeStruct((TP, part, HD), F32),
        ],
        compiler_params=pltpu.CompilerParams(vmem_limit_bytes=VMEM_LIMIT),
        name="assemble",
    )(got)


def swap_on(axis):
    return lambda v: lax.ppermute(v, axis, [(0, 1), (1, 0)])


def crossing(first):
    pairs = []
    for u in range(2):
        for y in range(2):
            for c in range(2):
                along_u = (c == 0) == first
                to = (1 - u, y, c) if along_u else (u, 1 - y, c)
                pairs.append(((u * 2 + y) * 2 + c, (to[0] * 2 + to[1]) * 2 + to[2]))
    return lambda v: lax.ppermute(v, ("u", "y", "c"), pairs)


def after(v, *earlier):
    return lax.optimization_barrier((v,) + earlier)[0]


def add(a, b):
    return (a.astype(F32) + b.astype(F32)).astype(BF)


def pick(v, index, axis):
    return lax.dynamic_index_in_dim(v, index, axis, keepdims=False)


def put(buffer, v, index):
    return lax.dynamic_update_index_in_dim(buffer, v, index, 0)


def per_device(layer_input, wqkv, wo, wi, wd, biases, hidden_bias, gains, shifts, cotangent, block_ids, offsets, pairing):
    seqs, rows, width = layer_input.shape
    devices = lax.axis_size(ALL)
    ring = lax.axis_size("r")
    shards = ring * TP
    half = shards * rows
    tokens = seqs * rows
    me_u, me_r, me_y, me_c = (lax.axis_index(a) for a in ALL)
    me_t = me_y * 2 + me_c
    part = wqkv.shape[0]
    hidden = wi.shape[1]
    fold = hidden // width
    swap_u, swap_c = swap_on("u"), swap_on("c")
    cross_one, cross_two = crossing(True), crossing(False)
    forward = [(i, (i + 1) % ring) for i in range(ring)]

    notes = [biases[2:].T, gains.T, shifts.T, hidden_bias.reshape(fold, part).T]
    notes = jnp.concatenate(notes + [jnp.zeros((part, 128 - 6 - fold), BF)], axis=1)
    wi_turned = wi.reshape(part, devices, fold, part).transpose(0, 2, 1, 3).reshape(part, hidden)
    wd_cols = [wd[k * part : (k + 1) * part] for k in range(fold)]
    dense_own = jnp.concatenate([wo, wi_turned] + wd_cols + [notes], axis=1)

    by_head = wqkv.reshape(part, 3, TP, HG, HD)
    blocks_kv = by_head[:, 1:].transpose(2, 0, 3, 1, 4).reshape(TP, part, HG * 128)
    blocks_q = by_head[:, 0].transpose(1, 0, 2, 3).reshape(TP, part, HG * HD)
    ends = jnp.pad(biases[:2].T, ((0, 0), (0, HD - 2)))
    blocks = jnp.concatenate([blocks_kv, blocks_q, jnp.broadcast_to(ends, (TP, part, HD))], axis=2)
    blocks = lax.all_to_all(blocks, ("y", "c"), split_axis=0, concat_axis=0, tiled=True)
    column = put(jnp.zeros((ring,) + blocks.shape, BF), blocks, me_r)
    for k in range(1, ring):
        got = lax.ppermute(blocks, "r", [(i, (i + k) % ring) for i in range(ring)])
        column = put(column, got, (me_r - k) % ring)
    early = (cross_one(layer_input.reshape(tokens, width)), cross_two(layer_input.reshape(tokens, width)))
    column = after(column, *early)
    dense = lax.all_gather(after(dense_own, column), ALL, axis=0, tiled=True)
    both = jnp.zeros((2,) + column.shape, BF)
    w_here = put(put(both, column, me_u), swap_u(column), 1 - me_u).reshape(width, 640)
    b_heads = w_here[:, 576:578].astype(F32)
    b_heads = lax.dynamic_slice_in_dim(b_heads, me_t * HG * HD, HG * HD, 0).T
    b_kv = jnp.concatenate([jnp.zeros((HG, HD), F32), b_heads[1].reshape(HG, HD)], axis=1).reshape(-1)
    b_here = jnp.concatenate([b_kv, b_heads[0], jnp.zeros((HD,), F32)])
    b_here = jnp.broadcast_to(b_here, (8, 640))

    x_own = layer_input.reshape(tokens, width)
    piece = x_own
    stages = []
    for k in range(ring):
        if k == 1:
            piece, column = lax.optimization_barrier((piece, column))
        if k:
            piece = lax.ppermute(piece, "r", forward)
        if k >= 2:
            piece, stages[k - 2] = lax.optimization_barrier((piece, stages[k - 2]))
        one, two = early if k == 0 else (cross_one(piece), cross_two(piece))
        if k == 1:
            one, w_here = lax.optimization_barrier((one, w_here))
        three = cross_two(one)
        if k >= 2:
            three, stages[k - 1] = lax.optimization_barrier((three, stages[k - 1]))
        mine = [piece, one, two, three]
        theirs = [swap_c(m) for m in mine]
        if k == 0:
            x_near = (mine, theirs)
        spot = jnp.stack([me_u, me_y, me_c, (me_r - k) % ring]).astype(jnp.int32)
        stages.append(project(mine + theirs, w_here, b_here, spot, stages[-1] if stages else None, ring, seqs, rows))
    buffers = stages[-1]
    kv = buffers[0].reshape(2, shards, seqs, rows, HG * 128)
    q_all = buffers[1].reshape(shards, seqs, rows, HG * 128)

    pair = lax.dynamic_slice_in_dim(pick(pairing, me_u, 1), me_t * HG, HG, 0)
    ids = block_ids.reshape(seqs, 2, half)
    ids_own = pick(ids, me_u, 1)
    ends = jnp.sum((ids[:, :, None, :] <= ids_own[:, None, :, None]).astype(jnp.int32), axis=-1)
    end_all = jnp.where((pair == 0)[None, :, None], ends[:, 0:1], ends[:, 1:2])
    end_loc = lax.dynamic_slice_in_dim(end_all, me_r * TP * rows, TP * rows, 2)
    begin = jnp.maximum(offsets[:, None] - pair[None, :] * half, 0).reshape(-1)
    last = jnp.concatenate([end_loc[:, :, -1].reshape(-1), me_r[None].astype(jnp.int32)])
    start = me_r * TP * rows
    end_ring = end_all.reshape(seqs, HG, ring, TP * rows)
    end_row_own = end_loc[:, :, None]

    att = attend_forward(q_all, kv, pair, begin, last, end_row_own)
    att = lax.all_to_all(att, ("y", "c"), split_axis=0, concat_axis=0, tiled=True).reshape(TP, tokens, 256)

    index = jnp.arange(width, dtype=jnp.int32)
    inner_at, index = index % part, index // part
    r_rel, index = index % ring, index // ring
    s_rel, f_rel, c_rel = index % 2, index // 2 % 2, index // 4
    core = me_c ^ c_rel
    to_u = me_u ^ jnp.where(core == 0, f_rel, s_rel)
    to_y = me_y ^ jnp.where(core == 0, s_rel, f_rel)
    order = (((to_u * ring + (me_r + r_rel) % ring) * 2 + to_y) * 2 + core) * part + inner_at
    order = jnp.broadcast_to(order.astype(jnp.int32), (8, width))
    hidden_out, load, dsum, stay, leave = dense_layers(att, x_own, cotangent.reshape(tokens, width), order, dense, fold)
    hidden_out = hidden_out.reshape(seqs, rows, width)
    came = swap_c(leave)
    cut = width // 4
    high, low = add(stay[cut:], came[cut:]), add(stay[:cut], came[:cut])
    high_first = high
    cut = width // 8
    load = load.reshape(TP, seqs, rows, 256)
    load = lax.all_to_all(load, ("y", "c"), split_axis=0, concat_axis=0, tiled=True)
    came = cross_one(after(high_first, load))
    place = jnp.stack([start, me_r])
    dkv = jnp.zeros((TP, seqs, rows, HG * 128), F32)
    moving = load
    done = []
    for k in range(ring):
        if k >= 2:
            moving, done[k - 2] = lax.optimization_barrier((moving, done[k - 2]))
        if k:
            moving = lax.ppermute(moving, "r", forward)
        source = (me_r - k) % ring
        ends_k = pick(end_ring, source, 2)
        where = jnp.concatenate([place, source[None]]).astype(jnp.int32)
        before = done[-1] if done else dkv
        if k == 2:
            dq = attend_query(q_all, kv, pair, begin, last, end_row_own, after(load, high_first, moving))
        if k == ring - 1:
            before = after(before, dq)
        if k == ring - 2:
            came = after(came, done[1], moving)
            high2, low2 = add(low[cut:], came[cut:]), add(low[:cut], came[:cut])
            stay = add(low2, cross_two(high2))
            before = after(before, high2)
        done.append(attend_key(q_all, moving, kv, pair, begin, ends_k[:, :, -1].reshape(-1), where, ends_k[:, :, None], before))

    moved = []
    for j in range(1, ring):
        along = [(i, (i + j) % ring) for i in range(ring)]
        moved.append(lax.ppermute(stay[j * part : (j + 1) * part], "r", along))
    spot = jnp.concatenate([jnp.stack([me_u, me_y, me_c]), (pair == me_u).astype(jnp.int32)])
    keep, send, dw = tail(spot.astype(jnp.int32), dq, done[-1], w_here, x_near[0] + x_near[1], part)
    keep = add(keep, swap_c(send))
    dw = after(dw, keep, moved[0])
    got = lax.all_to_all(dw.reshape(devices, part, 640), ALL, split_axis=0, concat_axis=0, tiled=True)
    came = cross_one(keep[1])
    onward = add(keep[0, 1], came[1])
    summed = stay[:part].astype(F32) + moved[0].astype(F32)
    for m in moved[1:]:
        summed = summed + after(m, onward).astype(F32)
    final = cross_two(onward)
    grad_w_in, grad_w_down, grad_w_out, flat = finish([after(summed, onward)], fold, width)
    grad_w_down = grad_w_down.reshape(fold * part, width)
    flat = flat[:, : 6 + fold].T
    grad_bo, grad_gains, grad_shifts, grad_bin = flat[0:2], flat[2:4], flat[4:6], flat[6:].reshape(-1)

    grad_input = dsum + keep[0, 0].astype(F32) + came[0].astype(F32) + final.astype(F32)
    grad_input = grad_input.astype(BF).reshape(seqs, rows, width)
    grad_w_qkv, note = assemble(after(got, final).reshape(2 * ring, TP, part, 640))
    at = lax.axis_index(ALL) * part
    grad_bq = lax.dynamic_slice_in_dim(note[:, :HG].reshape(width), at, part, 0)
    grad_bv = lax.dynamic_slice_in_dim(note[:, HG : 2 * HG].reshape(width), at, part, 0)
    grad_biases = jnp.concatenate([jnp.stack([grad_bq, grad_bv]), grad_bo])
    return (hidden_out, grad_input, grad_w_qkv, grad_w_out, grad_w_in, grad_w_down, grad_biases, grad_bin, grad_gains, grad_shifts)


def solution(mesh):
    wide = mesh.shape["blk"]
    grid = Mesh(mesh.devices.reshape(2, wide // TP, 2, TP // 2), ALL)
    rows2, cols1 = P(ALL, None), P(None, ALL)
    toks = P(None, ALL, None)
    return jax.shard_map(
        per_device,
        mesh=grid,
        in_specs=(toks, rows2, rows2, rows2, rows2, cols1, P(ALL), cols1, cols1, toks, P(), P(), P()),
        out_specs=(toks, toks, rows2, rows2, rows2, rows2, cols1, P(ALL), cols1, cols1),
        check_vma=False,
    )
```
